256 devices in a mesh: pair: 32 (over x, z), tile: 8 (over y, core).
Axes of the slice: x: 4, y: 4, z: 8, core: 2. Of those that a mesh axis runs over, the one named last changes fastest.
Arguments:
- valence_waves: bfloat16 [32, 96, 9216], P('pair', 'tile'), may hold values from -6 to 6
- cond_waves: bfloat16 [64, 96, 9216], P('pair', 'tile'), may hold values from -6 to 6
- valence_energy: float32 [128], replicated, may hold values from -16 to -1
- conduction_energy: float32 [256], replicated, may hold values from 0.5 to 12
- valence_pick: int32 [32], replicated, may hold values from 0 to 127, as said below
- cond_pick: int32 [64], replicated, may hold values from 0 to 255, as said below
- cond_slot: int32 [64], replicated, may hold values from 0 to 63, each once
- g_index: int32 [12000], replicated, may hold values from 0 to 52021, as said below
Outputs:
- chi0: float32 [12000, 12000], P('pair', 'tile')
The draws below stay inside these ranges and needn't reach their ends.
Inputs may be any that keep to these rules, and one draw needn't show every extreme that they name: `valence_pick`: distinct levels. `cond_pick`: distinct levels. `cond_slot`: each slot once. `g_index`: distinct positions in the flattened spectrum of 2 x (37) x (37) x (19) entries.
All inputs are finite; a program needn't handle non-finite values.
Results may differ from the reference program's by a relative error of at most 0.019.
Values may be sent and summed in bfloat16 or wider, within the bound.
No kernel may reach another device: no remote copies, remote signals or barrier semaphores. Data moves between devices by JAX's collectives and lax.ppermute only.
A program may use at most 192 MiB of HBM per device.

```python
import math
import jax
import jax.numpy as jnp
from jax import lax

NV = 32
NC = 64
GRID = 96
KM = 18
NG = 12000
VTAB = 128
CTAB = 256


def distinct_values(key, total, count):
    middle = jax.random.permutation(key, total - 2)[:count - 2] + 1
    ends = jnp.array([0, total - 1], dtype=jnp.int32)
    values = jnp.concatenate([ends, middle.astype(jnp.int32)])
    return jax.random.permutation(jax.random.fold_in(key, 5), values).astype(jnp.int32)


def draw_valence_pick(key, part):
    key = jax.random.fold_in(key, 3)
    return distinct_values(key, VTAB, NV)


def draw_cond_pick(key, part):
    key = jax.random.fold_in(key, 7)
    return distinct_values(key, CTAB, NC)


def draw_g_index(key, part):
    key = jax.random.fold_in(key, 11)
    return distinct_values(key, 2 * (2 * KM + 1) ** 2 * (KM + 1), NG)


def steps_of(rng, extent, pieces, smallest, top_value):
    level = 1.0
    for dim, shards_of in pieces:
        heights = jax.random.uniform(jax.random.fold_in(jax.random.fold_in(rng, 6), dim), (shards_of,), jnp.float32, smallest / len(pieces), top_value / len(pieces))
        level = level * jnp.repeat(jnp.exp(heights), extent[dim] // shards_of).reshape((-1,) + (1,) * (len(extent) - 1 - dim))
    return level


def normal_values(key, dims, spread, most, pieces=(), kind=jnp.bfloat16):
    values = spread * jax.random.normal(key, dims, jnp.float32)
    if pieces:
        values = values * steps_of(key, dims, pieces, -0.22, 0.18)
    return jnp.clip(values, -most, most).astype(kind)


def setup_inputs(seed: int = 0) -> dict:
    splits = jax.random.split(jax.random.key(seed), 9)
    return {
        "valence_waves": normal_values(splits[0], (NV, GRID, GRID * GRID), 1.0, 6.0, ((0, 32), (1, 8))),
        "cond_waves": normal_values(splits[1], (NC, GRID, GRID * GRID), 1.0, 6.0, ((0, 32), (1, 8))),
        "valence_energy": jnp.clip(jax.random.uniform(splits[2], (VTAB,), jnp.float32, -16.0, -1.0), -16.0, -1.0),
        "conduction_energy": jnp.clip(jax.random.uniform(splits[3], (CTAB,), jnp.float32, 0.5, 12.0), 0.5, 12.0),
        "valence_pick": draw_valence_pick(jax.random.fold_in(splits[8], 71), 0),
        "cond_pick": draw_cond_pick(jax.random.fold_in(splits[8], 71), 0),
        "cond_slot": jax.random.permutation(splits[6], NC).astype(jnp.int32),
        "g_index": draw_g_index(jax.random.fold_in(splits[8], 71), 0),
    }


def phase_angles(freqs, positions):
    turns = jnp.mod(freqs, GRID)[None, :] * positions[:, None] % GRID
    return turns.astype(jnp.float32) * (2.0 * math.pi / GRID)

def depth_table(positions):
    angle = phase_angles(jnp.arange(KM + 1, dtype=jnp.int32), positions)
    scale = 1.0 / math.sqrt(GRID)
    table = jnp.stack([jnp.cos(angle), -jnp.sin(angle)], axis=1) * scale
    return table.reshape(positions.shape[0], 2 * (KM + 1)).astype(jnp.bfloat16)

def plane_table(positions):
    angle = phase_angles(jnp.arange(2 * KM + 1, dtype=jnp.int32) - KM, positions)
    scale = 1.0 / math.sqrt(GRID)
    cosine = jnp.cos(angle)
    sine = jnp.sin(angle)
    real_part = jnp.stack([cosine, sine])
    imag_part = jnp.stack([-sine, cosine])
    return (jnp.stack([real_part, imag_part], axis=2) * scale).astype(jnp.bfloat16)

def reference(valence_waves, cond_waves, valence_energy, conduction_energy, valence_pick, cond_pick, cond_slot, g_index):
    positions = jnp.arange(GRID, dtype=jnp.int32)
    depth = depth_table(positions).astype(jnp.float32)
    plane = plane_table(positions).astype(jnp.float32)
    kept = 2 * KM + 1
    spectrum_size = 2 * kept * kept * (KM + 1)

    def one_valence(wave):
        density = (wave[None].astype(jnp.float32) * cond_waves.astype(jnp.float32)).astype(jnp.bfloat16)
        density = density.reshape(NC, GRID, GRID, GRID).astype(jnp.float32)
        z_spec = jnp.einsum('sxyz,zm->sxym', density, depth).astype(jnp.bfloat16)
        z_spec = z_spec.reshape(NC, GRID, GRID, 2, KM + 1).astype(jnp.float32)
        y_spec = jnp.einsum('sxycz,cyek->ekszx', z_spec, plane).astype(jnp.bfloat16).astype(jnp.float32)
        spectrum = jnp.einsum('ekszx,exfj->sfjkz', y_spec, plane).reshape(NC, spectrum_size)
        return jnp.take(spectrum, g_index, axis=1).astype(jnp.bfloat16)
    pair_density = lax.map(one_valence, valence_waves).reshape(NV * NC, NG)
    valence_level = valence_energy[valence_pick]
    band_level = conduction_energy[cond_pick]
    slot_level = jnp.zeros((NC,), jnp.float32).at[cond_slot].set(band_level)
    factor = 4.0 / math.sqrt(NV * NC)
    weight = (factor / (valence_level[:, None] - slot_level[None, :])).reshape(NV * NC)
    weighted = (weight[:, None] * pair_density.astype(jnp.float32)).astype(jnp.bfloat16)
    return jnp.dot(weighted.T, pair_density, preferred_element_type=jnp.float32)
```

```python
import functools
import math

import jax
import jax.numpy as jnp
import ml_dtypes
import numpy as np
from jax import lax
from jax.experimental import pallas as pl
from jax.experimental.pallas import tpu as pltpu
from jax.sharding import Mesh, PartitionSpec as P

NV = 32
NC = 64
GRID = 96
KM = 18
NG = 12000
KEPT = 2 * KM + 1
HALF = KM + 1
NX, NZ, NY, NCORE = 4, 8, 4, 2
NT = NY * NCORE
SLAB = GRID // NT
VB = 8
SB = 8
ROWS = SLAB * VB * SB
ZGRP = 384
ZOUT = HALF * 8
YSTEP = 768
NSTEP = GRID * GRID // YSTEP
BTILE = 128
NBT = 5
KWIN = 5
YL = 1408
AEI = 2 * KEPT
RB = 384
GP = 32 * RB
GCH = 768
CODES = 256
NGRP = 3
BF = jnp.bfloat16
F32 = jnp.float32


def tables():
    pos = np.arange(GRID)
    scale = 1.0 / math.sqrt(GRID)

    def angles(freqs):
        turns = (np.mod(freqs, GRID)[None, :] * pos[:, None]) % GRID
        return turns.astype(np.float64) * (2.0 * math.pi / GRID)

    ad = angles(np.arange(HALF))
    depth = np.stack([np.cos(ad), -np.sin(ad)], axis=1) * scale
    ap = angles(np.arange(KEPT) - KM)
    c, s = np.cos(ap), np.sin(ap)
    plane = np.stack([np.stack([c, s]), np.stack([-s, c])], axis=2) * scale
    return depth, plane


def depth_block():
    depth, _ = tables()
    out = np.zeros((HALF, 2, 4, 4, GRID), np.float64)
    for y in range(4):
        out[:, :, y, y, :] = depth.transpose(2, 1, 0)
    return out.reshape(ZOUT, ZGRP).astype(ml_dtypes.bfloat16)


def window(n):
    return min((BTILE * n) // KEPT, HALF - KWIN)


def plane_block():
    _, plane = tables()
    perk = plane.reshape(2, GRID // 4, 4, 2, KEPT).transpose(3, 4, 1, 0, 2).reshape(2, KEPT, 2 * GRID)
    out = np.zeros((YL, KWIN, 2 * GRID), np.float64)
    for d in range(2):
        for b in range(KEPT * HALF):
            k, j = divmod(b, KEPT)
            n, r = divmod(b, BTILE)
            row = n * 2 * BTILE + d * (BTILE if n < NBT else 64) + r
            out[row, k - window(n)] = perk[d, j]
    return out.reshape(YL, KWIN * 2 * GRID).astype(ml_dtypes.bfloat16)


def kron_block(q):
    _, plane = tables()
    out = np.zeros((2, AEI, q, GRID, q), np.float64)
    for s in range(q):
        out[:, :, s, :, s] = plane.reshape(2, GRID, AEI).transpose(0, 2, 1)
    return out.reshape(2, AEI * q, GRID * q).astype(ml_dtypes.bfloat16)


def spectra_kernel(*refs):
    v_refs, c_refs = refs[:VB], refs[VB : VB + NX + 1]
    t_ref, w_ref, o_ref, vf, cf, dens, zs = refs[VB + NX + 1 :]
    step = pl.program_id(0)
    for v in range(VB):
        vf[v] = v_refs[v][0].astype(F32)
    for m in range(3):
        cf[:, pl.ds(2 * m, 2), :] = c_refs[m][...].astype(F32)
    for h in range(2):
        cf[pl.ds(h * (SLAB // 2), SLAB // 2), pl.ds(6, 2), :] = c_refs[3 + h][...].astype(F32)
    parts = []
    for sub in range(YSTEP // ZGRP):
        lanes = pl.ds(sub * ZGRP, ZGRP)
        for x in range(SLAB):
            cx = cf[x, :, lanes]
            for v in range(0, VB, 2):
                pair = jnp.concatenate([vf[v, pl.ds(x, 1), lanes] * cx, vf[v + 1, pl.ds(x, 1), lanes] * cx], axis=0)
                dens[sub, pl.ds(x * VB * SB + v * SB, 2 * SB), :] = pair.astype(BF)
        z = lax.dot_general(t_ref[...], dens[sub], (((1,), (1,)), ((), ())), preferred_element_type=F32)
        parts.append(z.reshape(HALF, 8, ROWS))
    zs[:, pl.ds(pl.multiple_of(step * 16, 16), 16), :] = jnp.concatenate(parts, axis=1).astype(BF)

    @pl.when(step == NSTEP - 1)
    def _():
        for n in range(NBT + 1):
            r0 = n * 2 * BTILE
            rows = 2 * BTILE if n < NBT else BTILE
            k0 = window(n)
            zk = zs[k0 : k0 + KWIN].reshape(KWIN * 2 * GRID, ROWS)
            y = jnp.dot(w_ref[r0 : r0 + rows, :], zk, preferred_element_type=F32)
            yt = y.T.reshape(SLAB, VB, SB, rows)
            for v in range(VB):
                o_ref[v, :, r0 : r0 + rows] = yt[:, v].reshape(SLAB * SB, rows).astype(BF)


def spectra(vs, cs, t, w):
    return pl.pallas_call(
        spectra_kernel,
        grid=(NSTEP,),
        in_specs=[pl.BlockSpec((1, SLAB, YSTEP), lambda i: (0, 0, i))] * VB
        + [pl.BlockSpec((SLAB, 2, YSTEP), lambda i: (0, 0, i))] * (NX - 1)
        + [pl.BlockSpec((SLAB // 2, 2, YSTEP), lambda i: (0, 0, i))] * 2
        + [
            pl.BlockSpec((ZOUT, ZGRP), lambda i: (0, 0)),
            pl.BlockSpec((YL, KWIN * 2 * GRID), lambda i: (0, 0)),
        ],
        out_specs=pl.BlockSpec((VB, SLAB * SB, YL), lambda i: (0, 0, 0)),
        out_shape=jax.ShapeDtypeStruct((VB, SLAB * SB, YL), BF),
        scratch_shapes=[
            pltpu.VMEM((VB, SLAB, YSTEP), F32),
            pltpu.VMEM((SLAB, SB, YSTEP), F32),
            pltpu.VMEM((YSTEP // ZGRP, ROWS, ZGRP), BF),
            pltpu.VMEM((HALF, 2 * GRID, ROWS), BF),
        ],
        compiler_params=pltpu.CompilerParams(vmem_limit_bytes=56 * 2**20),
        name="spectra",
    )(*vs, *cs, t, w)


def pick_kernel(y_ref, m_ref, a_ref, b_ref, oc_ref, or_ref, s_ref):
    @pl.when(pl.program_id(0) == 0)
    def _():
        rows = AEI * SB

        def place(n, s):
            s_ref[n // 2 * rows : (n // 2 + 1) * rows, n % 2 * BTILE : (n % 2 + 1) * BTILE] = s.astype(BF)

        for n in range(NBT):
            l0 = n * 2 * BTILE
            s = jnp.dot(m_ref[0], y_ref[:, l0 : l0 + BTILE], preferred_element_type=F32)
            s += jnp.dot(m_ref[1], y_ref[:, l0 + BTILE : l0 + 2 * BTILE], preferred_element_type=F32)
            place(n, s)
        last = y_ref[:, NBT * 2 * BTILE : YL]
        s0 = jnp.dot(m_ref[0], last, preferred_element_type=F32)
        s1 = jnp.dot(m_ref[1], last, preferred_element_type=F32)
        place(NBT, s0 + pltpu.roll(s1, 64, 1))

    codes = lax.broadcasted_iota(jnp.int32, (CODES, CODES), 0)
    outs = []
    for g in range(GCH // CODES):
        lanes = pl.ds(g * CODES, CODES)
        chosen = (codes == b_ref[:, lanes]).astype(F32).astype(BF)
        r = jnp.dot(s_ref[...], chosen, preferred_element_type=F32)
        code = jnp.broadcast_to(a_ref[:, lanes], (SB, CODES))
        acc = jnp.zeros((SB, CODES), F32)
        for a in range(NGRP * AEI):
            acc = jnp.where(code == a, r[a * SB : (a + 1) * SB], acc)
        outs.append(acc.astype(BF))
    out = jnp.concatenate(outs, axis=1)
    oc_ref[0] = out
    for h in range(GCH // RB):
        or_ref[h] = out[:, h * RB : (h + 1) * RB]


def pick(y, m, a, b):
    per = 4 * RB // GCH
    return pl.pallas_call(
        pick_kernel,
        grid=(GP // GCH,),
        in_specs=[
            pl.BlockSpec((GRID * SB, YL), lambda i: (0, 0)),
            pl.BlockSpec((2, AEI * SB, GRID * SB), lambda i: (0, 0, 0)),
            pl.BlockSpec((1, GCH), lambda i: (0, i)),
            pl.BlockSpec((1, GCH), lambda i: (0, i)),
        ],
        out_specs=[
            pl.BlockSpec((1, SB, GCH), lambda i: (i // per, 0, i % per)),
            pl.BlockSpec((GCH // RB, SB, RB), lambda i: (i, 0, 0)),
        ],
        out_shape=[
            jax.ShapeDtypeStruct((NT, SB, 4 * RB), BF),
            jax.ShapeDtypeStruct((32, SB, RB), BF),
        ],
        scratch_shapes=[pltpu.VMEM((NGRP * AEI * SB, CODES), BF)],
        compiler_params=pltpu.CompilerParams(vmem_limit_bytes=48 * 2**20),
        name="pick",
    )(y, m, a, b)


KP = NT * SB
LH = 2 * RB
XORDER = (0, 1, 3, 2)
ZORDER = (0, 1, 2, 3, 7, 6, 5, 4)


def a_pieces():
    whole = [[(x, z) for x in XORDER] for z in ZORDER[:-1]]
    return whole + [[(x, 4) for x in XORDER[:2]], [(x, 4) for x in XORDER[2:]]]


def b_pieces():
    whole = [[(x, z) for z in ZORDER] for x in XORDER[:-1]]
    return whole + [[(2, z) for z in ZORDER[:4]], [(2, z) for z in ZORDER[4:]]]


def product_kernel(xz_ref, r_ref, w_ref, *refs):
    na, nb = len(a_pieces()), len(b_pieces())
    a_refs, b_refs, (o_ref, wr) = refs[:na], refs[na : na + nb], refs[na + nb :]
    for p in range(32):
        rows = jnp.concatenate([r_ref[t, p].astype(F32) for t in range(NT)], axis=0)
        wr[p] = (rows * w_ref[KP * p : KP * (p + 1), :]).astype(BF)

    def part(pieces, ref):
        lhs = []
        for dx, dz in pieces:
            place = lax.rem(xz_ref[0] + (NX - dx), NX) * NZ + lax.rem(xz_ref[1] + (NZ - dz), NZ)
            lhs.append(wr[place])
        return lax.dot_general(
            jnp.concatenate(lhs, axis=0), ref[...], (((0,), (0,)), ((), ())), preferred_element_type=F32
        )

    for h, (pieces, operands) in enumerate(((a_pieces(), a_refs), (b_pieces(), b_refs))):
        acc = part(pieces[0], operands[0])
        for piece, ref in zip(pieces[1:], operands[1:]):
            acc += part(piece, ref)
        for q in range(2):
            o_ref[:, 375 * (2 * h + q) : 375 * (2 * h + q + 1)] = acc[:375, RB * q : RB * q + 375]


def product(place, rows, weight, a_cols, b_cols):
    vmem = pl.BlockSpec(memory_space=pltpu.VMEM)
    return pl.pallas_call(
        product_kernel,
        in_specs=[pl.BlockSpec(memory_space=pltpu.SMEM)] + [vmem] * (2 + len(a_cols) + len(b_cols)),
        out_specs=vmem,
        out_shape=jax.ShapeDtypeStruct((375, 1500), F32),
        scratch_shapes=[pltpu.VMEM((32, KP, RB), BF)],
        compiler_params=pltpu.CompilerParams(vmem_limit_bytes=48 * 2**20),
        name="product",
    )(place, rows, weight, *a_cols, *b_cols)


def ring(value, axis, size):
    out_up, out_down = [value], [value]
    for _ in range(size // 2 - 1):
        out_up.append(shift(out_up[-1], axis, size, 1))
        out_down.append(shift(out_down[-1], axis, size, -1))
    half = value.shape[0] // 2
    far = [shift(out_up[-1][:half], axis, size, 1), shift(out_down[-1][half:], axis, size, -1)]
    return out_up + out_down[1:], far


def pick_levels(picks, table):
    codes = jnp.arange(table.shape[0], dtype=jnp.int32)
    return jnp.sum(jnp.where(picks[:, None] == codes[None, :], table[None, :], 0.0), axis=1)


def spread(levels, places):
    codes = jnp.arange(levels.shape[0], dtype=jnp.int32)[None, :]
    return jnp.sum(jnp.where(codes == places.astype(np.int32), levels[None, :], 0.0), axis=1, keepdims=True)


def shift(value, axis, size, step):
    return lax.ppermute(value, axis, [(i, (i + step) % size) for i in range(size)])


def per_device(
    valence_waves,
    cond_waves,
    valence_energy,
    conduction_energy,
    valence_pick,
    cond_pick,
    cond_slot,
    g_index,
):
    cond_waves = cond_waves.transpose(1, 0, 2)
    cs, far = ring(cond_waves, "x", NX)
    cs += far
    vs = [valence_waves] + [None] * (VB - 1)
    for m in range(1, VB // 2 + 1):
        vs[m] = shift(vs[m - 1], "z", NZ, 1)
        if m < VB // 2:
            vs[VB - m] = shift(vs[(VB - m + 1) % VB], "z", NZ, -1)

    valence_level = pick_levels(valence_pick, valence_energy)
    band_level = pick_levels(cond_pick, conduction_energy)
    slot_codes = jnp.arange(NC, dtype=jnp.int32)
    slot_level = jnp.sum(
        jnp.where(cond_slot[:, None] == slot_codes[None, :], band_level[:, None], 0.0), axis=0
    )
    factor = 4.0 / math.sqrt(NV * NC)
    xs, zs, ts, ms, bs = np.ix_(*(np.arange(n) for n in (NX, NZ, NT, NX, 2)))
    v_of = np.broadcast_to(VB * xs + (zs - ts) % NZ, (NX, NZ, NT, NX, 2)).reshape(NV * NC, 1)
    s_of = np.broadcast_to(2 * NZ * ((xs - np.array(XORDER)[ms]) % NX) + 2 * zs + bs, (NX, NZ, NT, NX, 2)).reshape(NV * NC, 1)
    weight = factor / (spread(valence_level, v_of) - spread(slot_level, s_of))

    index = jnp.pad(g_index.reshape(32, 375), ((0, 0), (0, RB - 375))).reshape(1, GP)
    a_code = index // (KEPT * HALF)
    rest = index % (KEPT * HALF)
    b_code = (rest % HALF) * KEPT + rest // HALF
    a_code = a_code + AEI * (b_code // CODES)
    b_code = b_code % CODES

    spec = spectra(
        vs,
        cs,
        jnp.asarray(depth_block()),
        jnp.asarray(plane_block()),
    )
    slabs = lax.all_to_all(spec, ("y", "core"), split_axis=0, concat_axis=0, tiled=True)
    for_cols, for_rows = pick(slabs.reshape(GRID * SB, YL), jnp.asarray(kron_block(SB)), a_code, b_code)
    cols = lax.all_to_all(for_cols, ("y", "core"), split_axis=0, concat_axis=0, tiled=True).reshape(KP, 2 * LH)
    a_near, a_far = ring(cols[:, :LH], "x", NX)
    a_cols, far = ring(jnp.concatenate(a_near + a_far, axis=0), "z", NZ)
    a_cols += far
    b_near, b_far = ring(cols[:, LH:], "z", NZ)
    b_cols, far = ring(jnp.concatenate(b_near + b_far, axis=0), "x", NX)
    b_cols += far
    for_rows, _ = lax.optimization_barrier((for_rows, cols))
    rows = lax.all_to_all(for_rows, ("x", "z"), split_axis=0, concat_axis=0, tiled=True)
    rows = lax.all_gather(rows, ("y", "core"), axis=0, tiled=False)
    place = jnp.stack([lax.axis_index("x"), lax.axis_index("z")]).astype(jnp.int32)
    return product(place, rows, weight, a_cols, b_cols)


def solution(mesh):
    fine = Mesh(mesh.devices.reshape(NX, NZ, NY, NCORE), ("x", "z", "y", "core"))
    waves = P(("x", "z"), ("y", "core"), None)
    return jax.shard_map(
        per_device,
        mesh=fine,
        in_specs=(waves, waves, P(), P(), P(), P(), P(), P()),
        out_specs=P(("x", "z"), ("y", "core")),
        check_vma=False,
    )
```

```python
import functools
import math

import jax
import jax.numpy as jnp
import ml_dtypes
import numpy as np
from jax import lax
from jax.experimental import pallas as pl
from jax.experimental.pallas import tpu as pltpu
from jax.sharding import Mesh, PartitionSpec as P

NV = 32
NC = 64
GRID = 96
KM = 18
NG = 12000
KEPT = 2 * KM + 1
HALF = KM + 1
NX, NZ, NY, NCORE = 4, 8, 4, 2
NT = NY * NCORE
SLAB = GRID // NT
VB = 8
SB = 8
VC = 4
QC = 4
SLOTS = ((0, 1, 7, 2), (6, 3, 5, 4))
ROWS = SLAB * VC * SB
ZGRP = 384
ZOUT = HALF * 8
YSTEP = 768
NSTEP = GRID * GRID // YSTEP
BTILE = 128
NBT = 5
KWIN = 5
YL = 1408
AEI = 2 * KEPT
RB = 384
GP = 32 * RB
GCH = 768
CODES = 256
NGRP = 3
BF = jnp.bfloat16
F32 = jnp.float32


def tables():
    pos = np.arange(GRID)
    scale = 1.0 / math.sqrt(GRID)

    def angles(freqs):
        turns = (np.mod(freqs, GRID)[None, :] * pos[:, None]) % GRID
        return turns.astype(np.float64) * (2.0 * math.pi / GRID)

    ad = angles(np.arange(HALF))
    depth = np.stack([np.cos(ad), -np.sin(ad)], axis=1) * scale
    ap = angles(np.arange(KEPT) - KM)
    c, s = np.cos(ap), np.sin(ap)
    plane = np.stack([np.stack([c, s]), np.stack([-s, c])], axis=2) * scale
    return depth, plane


def depth_block():
    depth, _ = tables()
    out = np.zeros((HALF, 2, 4, 4, GRID), np.float64)
    for y in range(4):
        out[:, :, y, y, :] = depth.transpose(2, 1, 0)
    return out.reshape(ZOUT, ZGRP).T.astype(ml_dtypes.bfloat16)


def window(n):
    return min((BTILE * n) // KEPT, HALF - KWIN)


def plane_block():
    _, plane = tables()
    perk = plane.reshape(2, GRID // 4, 4, 2, KEPT).transpose(3, 4, 1, 0, 2).reshape(2, KEPT, 2 * GRID)
    out = np.zeros((YL, KWIN, 2 * GRID), np.float64)
    for d in range(2):
        for b in range(KEPT * HALF):
            k, j = divmod(b, KEPT)
            n, r = divmod(b, BTILE)
            row = n * 2 * BTILE + d * (BTILE if n < NBT else 64) + r
            out[row, k - window(n)] = perk[d, j]
    return out.reshape(YL, KWIN * 2 * GRID).astype(ml_dtypes.bfloat16)


def kron_block():
    _, plane = tables()
    out = np.zeros((2, 2, AEI, SB, NT, QC, SLAB), np.float64)
    for c in range(2):
        for q in range(QC):
            out[c, :, :, c * QC + q, :, q, :] = plane.reshape(2, NT, SLAB, AEI).transpose(0, 3, 1, 2)
    return out.reshape(2, 2, AEI * SB, GRID * QC).astype(ml_dtypes.bfloat16)


def spectra_kernel(*refs):
    v_refs, c_refs = refs[:VC], refs[VC : VC + NX + 1]
    t_ref, w_ref, o_ref, wide, dens, zs = refs[VC + NX + 1 :]
    step = pl.program_id(0)

    def stack(pieces):
        for i, piece in enumerate(pieces):
            wide[i * SLAB : (i + 1) * SLAB, :] = piece.astype(F32)
        return wide[...].astype(BF)

    bands = [c_refs[m][b] for m in range(3) for b in range(2)] + [c_refs[3][0], c_refs[4][0]]
    cond = [stack(bands[QC * h : QC * (h + 1)]) for h in range(2)]
    for v in range(VC):
        val = stack([v_refs[v][0]] * QC)
        for h in range(2):
            r0 = (v * 2 + h) * SLAB * QC
            dens[r0 : r0 + SLAB * QC, :] = val * cond[h]
    parts = []
    for sub in range(YSTEP // ZGRP):
        z = jnp.dot(dens[:, sub * ZGRP : (sub + 1) * ZGRP], t_ref[...], preferred_element_type=F32)
        parts.append(z.T.reshape(HALF, 8, ROWS))
    zs[:, pl.ds(pl.multiple_of(step * 16, 16), 16), :] = jnp.concatenate(parts, axis=1).astype(BF)

    @pl.when(step == NSTEP - 1)
    def _():
        for n in range(NBT + 1):
            r0 = n * 2 * BTILE
            rows = 2 * BTILE if n < NBT else BTILE
            k0 = window(n)
            zk = zs[k0 : k0 + KWIN].reshape(KWIN * 2 * GRID, ROWS)
            y = jnp.dot(w_ref[r0 : r0 + rows, :], zk, preferred_element_type=F32)
            yt = y.T.astype(BF).reshape(NT, SLAB * QC, rows)
            if n < NBT - 1:
                l0 = n // 2 * 512 + n % 2 * BTILE
                o_ref[:, :, l0 : l0 + BTILE] = yt[:, :, :BTILE]
                o_ref[:, :, l0 + 256 : l0 + 256 + BTILE] = yt[:, :, BTILE:]
            else:
                o_ref[:, :, r0 : r0 + rows] = yt


def spectra(vs, cs, t, w):
    one = pl.BlockSpec((1, SLAB, YSTEP), lambda i: (0, 0, i))
    two = pl.BlockSpec((2, SLAB, YSTEP), lambda i: (0, 0, i))
    return pl.pallas_call(
        spectra_kernel,
        grid=(NSTEP,),
        in_specs=[one] * VC
        + [two, two, two, one, one]
        + [
            pl.BlockSpec((ZGRP, ZOUT), lambda i: (0, 0)),
            pl.BlockSpec((YL, KWIN * 2 * GRID), lambda i: (0, 0)),
        ],
        out_specs=pl.BlockSpec((NT, SLAB * QC, YL), lambda i: (0, 0, 0)),
        out_shape=jax.ShapeDtypeStruct((NT, SLAB * QC, YL), BF),
        scratch_shapes=[
            pltpu.VMEM((QC * SLAB, YSTEP), F32),
            pltpu.VMEM((ROWS, YSTEP), BF),
            pltpu.VMEM((HALF, 2 * GRID, ROWS), BF),
        ],
        compiler_params=pltpu.CompilerParams(vmem_limit_bytes=48 * 2**20),
        name="spectra",
    )(*vs, *cs, t, w)


def lines_kernel(y0_ref, y1_ref, m_ref, s_ref):
    rows = AEI * SB

    def line(d, lanes):
        parts = [
            jnp.dot(m_ref[c, d], ref[:, lanes], preferred_element_type=F32) for c, ref in ((0, y0_ref), (1, y1_ref))
        ]
        return parts[0] + parts[1]

    for g in range(2):
        s = line(0, pl.ds(512 * g, 256)) + line(1, pl.ds(512 * g + 256, 256))
        s_ref[g * rows : (g + 1) * rows, :] = s.astype(BF)
    s = line(0, pl.ds(1024, BTILE)) + line(1, pl.ds(1024 + BTILE, BTILE))
    s_ref[2 * rows :, :BTILE] = s.astype(BF)
    last = pl.ds(1024 + 2 * BTILE, BTILE)
    s = line(0, last) + pltpu.roll(line(1, last), 64, 1)
    s_ref[2 * rows :, BTILE:] = s.astype(BF)


def lines(y0, y1, m):
    return pl.pallas_call(
        lines_kernel,
        out_shape=jax.ShapeDtypeStruct((NGRP * AEI * SB, CODES), BF),
        compiler_params=pltpu.CompilerParams(vmem_limit_bytes=48 * 2**20),
        name="lines",
    )(y0, y1, m)


def pick_kernel(s_ref, a_ref, b_ref, oc_ref, or_ref):
    codes = lax.broadcasted_iota(jnp.int32, (CODES, CODES), 0)
    outs = []
    for g in range(GCH // CODES):
        lanes = pl.ds(g * CODES, CODES)
        chosen = (codes == b_ref[:, lanes]).astype(F32).astype(BF)
        r = jnp.dot(s_ref[...], chosen, preferred_element_type=F32)
        code = jnp.broadcast_to(a_ref[:, lanes], (SB, CODES))
        acc = jnp.zeros((SB, CODES), F32)
        for a in range(NGRP * AEI):
            acc = jnp.where(code == a, r[a * SB : (a + 1) * SB], acc)
        outs.append(acc.astype(BF))
    out = jnp.concatenate(outs, axis=1)
    oc_ref[0] = out
    for h in range(GCH // RB):
        or_ref[h] = out[:, h * RB : (h + 1) * RB]


def pick(s, a, b):
    per = 4 * RB // GCH
    return pl.pallas_call(
        pick_kernel,
        grid=(GP // GCH,),
        in_specs=[
            pl.BlockSpec((NGRP * AEI * SB, CODES), lambda i: (0, 0)),
            pl.BlockSpec((1, GCH), lambda i: (0, i)),
            pl.BlockSpec((1, GCH), lambda i: (0, i)),
        ],
        out_specs=[
            pl.BlockSpec((1, SB, GCH), lambda i: (i // per, 0, i % per)),
            pl.BlockSpec((GCH // RB, SB, RB), lambda i: (i, 0, 0)),
        ],
        out_shape=[
            jax.ShapeDtypeStruct((NT, SB, 4 * RB), BF),
            jax.ShapeDtypeStruct((32, SB, RB), BF),
        ],
        compiler_params=pltpu.CompilerParams(vmem_limit_bytes=48 * 2**20),
        name="pick",
    )(s, a, b)


KP = NT * SB
LH = 2 * RB
XORDER = (0, 1, 3, 2)
ZORDER = (0, 1, 2, 3, 7, 6, 5, 4)


def a_pieces():
    whole = [[(x, z) for x in XORDER] for z in ZORDER[:-1]]
    return whole + [[(x, 4) for x in XORDER[:2]], [(x, 4) for x in XORDER[2:]]]


def b_pieces():
    whole = [[(x, z) for z in ZORDER] for x in XORDER[:-1]]
    return whole + [[(2, z) for z in ZORDER[:4]], [(2, z) for z in ZORDER[4:]]]


def product_kernel(xz_ref, r_ref, w_ref, *refs):
    na, nb = len(a_pieces()), len(b_pieces())
    a_refs, b_refs, (o_ref, wr) = refs[:na], refs[na : na + nb], refs[na + nb :]
    for p in range(32):
        rows = jnp.concatenate([r_ref[t, p].astype(F32) for t in range(NT)], axis=0)
        wr[p] = (rows * w_ref[KP * p : KP * (p + 1), :]).astype(BF)

    def part(pieces, ref):
        lhs = []
        for dx, dz in pieces:
            place = lax.rem(xz_ref[0] + (NX - dx), NX) * NZ + lax.rem(xz_ref[1] + (NZ - dz), NZ)
            lhs.append(wr[place])
        return lax.dot_general(
            jnp.concatenate(lhs, axis=0), ref[...], (((0,), (0,)), ((), ())), preferred_element_type=F32
        )

    for h, (pieces, operands) in enumerate(((a_pieces(), a_refs), (b_pieces(), b_refs))):
        acc = part(pieces[0], operands[0])
        for piece, ref in zip(pieces[1:], operands[1:]):
            acc += part(piece, ref)
        for q in range(2):
            o_ref[:, 375 * (2 * h + q) : 375 * (2 * h + q + 1)] = acc[:375, RB * q : RB * q + 375]


def product(place, rows, weight, a_cols, b_cols):
    vmem = pl.BlockSpec(memory_space=pltpu.VMEM)
    return pl.pallas_call(
        product_kernel,
        in_specs=[pl.BlockSpec(memory_space=pltpu.SMEM)] + [vmem] * (2 + len(a_cols) + len(b_cols)),
        out_specs=vmem,
        out_shape=jax.ShapeDtypeStruct((375, 1500), F32),
        scratch_shapes=[pltpu.VMEM((32, KP, RB), BF)],
        compiler_params=pltpu.CompilerParams(vmem_limit_bytes=48 * 2**20),
        name="product",
    )(place, rows, weight, *a_cols, *b_cols)


def ring(value, axis, size):
    out_up, out_down = [value], [value]
    for _ in range(size // 2 - 1):
        out_up.append(shift(out_up[-1], axis, size, 1))
        out_down.append(shift(out_down[-1], axis, size, -1))
    half = value.shape[0] // 2
    far = [shift(out_up[-1][:half], axis, size, 1), shift(out_down[-1][half:], axis, size, -1)]
    return out_up + out_down[1:], far


def pick_levels(picks, table):
    codes = jnp.arange(table.shape[0], dtype=jnp.int32)
    return jnp.sum(jnp.where(picks[:, None] == codes[None, :], table[None, :], 0.0), axis=1)


def spread(levels, places):
    codes = jnp.arange(levels.shape[0], dtype=jnp.int32)[None, :]
    return jnp.sum(jnp.where(codes == places.astype(np.int32), levels[None, :], 0.0), axis=1, keepdims=True)


def shift(value, axis, size, step):
    return lax.ppermute(value, axis, [(i, (i + step) % size) for i in range(size)])


def per_device(
    valence_waves,
    cond_waves,
    valence_energy,
    conduction_energy,
    valence_pick,
    cond_pick,
    cond_slot,
    g_index,
):
    cs, far = ring(cond_waves, "x", NX)
    cs += far
    depth, plane, kron = jnp.asarray(depth_block()), jnp.asarray(plane_block()), jnp.asarray(kron_block())
    tile = ("y", "core")
    vs = [valence_waves] + [None] * (VB - 1)
    specs = []
    for m in range(1, VB // 2 + 1):
        if m == VB // 2:
            specs.append(spectra([vs[k] for k in SLOTS[0]], cs, depth, plane))
        vs[m] = shift(vs[m - 1], "z", NZ, 1)
        if m < VB // 2:
            vs[VB - m] = shift(vs[(VB - m + 1) % VB], "z", NZ, -1)
    specs.append(spectra([vs[k] for k in SLOTS[1]], cs, depth, plane))
    slabs = [lax.all_to_all(spec, tile, split_axis=0, concat_axis=0, tiled=True) for spec in specs]

    valence_level = pick_levels(valence_pick, valence_energy)
    band_level = pick_levels(cond_pick, conduction_energy)
    slot_codes = jnp.arange(NC, dtype=jnp.int32)
    slot_level = jnp.sum(
        jnp.where(cond_slot[:, None] == slot_codes[None, :], band_level[:, None], 0.0), axis=0
    )
    factor = 4.0 / math.sqrt(NV * NC)
    xs, zs, ts, c, ms, bs = np.ix_(*(np.arange(n) for n in (NX, NZ, NT, 2, 2, 2)))
    v_of = VB * xs + (zs - np.array(SLOTS)[c, ts // 2]) % NZ
    s_of = 2 * NZ * ((xs - np.array(XORDER)[2 * (ts % 2) + ms]) % NX) + 2 * zs + bs
    v_of, s_of = (np.broadcast_to(m, (NX, NZ, NT, 2, 2, 2)).reshape(NV * NC, 1) for m in (v_of, s_of))
    weight = factor / (spread(valence_level, v_of) - spread(slot_level, s_of))

    index = jnp.pad(g_index.reshape(32, 375), ((0, 0), (0, RB - 375))).reshape(1, GP)
    a_code = index // (KEPT * HALF)
    rest = index % (KEPT * HALF)
    b_code = (rest % HALF) * KEPT + rest // HALF
    a_code = a_code + AEI * (b_code // CODES)
    b_code = b_code % CODES

    combined = lines(slabs[0].reshape(GRID * QC, YL), slabs[1].reshape(GRID * QC, YL), kron)
    cols, for_rows = pick(combined, a_code, b_code)
    cols = lax.all_to_all(cols, tile, split_axis=0, concat_axis=0, tiled=True).reshape(KP, 2 * LH)
    near, far = ring(cols[:, :LH], "x", NX)
    bundle = jnp.concatenate(near + far, axis=0)
    a_up, a_down = shift(bundle, "z", NZ, 1), shift(bundle, "z", NZ, -1)

    half = KP // 2
    b_up, b_down = [cols[:, LH:]], [cols[:, LH:]]
    for _ in range(3):
        b_up.append(shift(b_up[-1], "z", NZ, 1))
        b_down.append(shift(b_down[-1], "z", NZ, -1))
    b_last, b_late, a_up, a_down, for_rows = lax.optimization_barrier((b_up[3], b_down[3], a_up, a_down, for_rows))
    b_far = [shift(b_last[:half], "z", NZ, 1), shift(b_late[half:], "z", NZ, -1)]
    b_bundle = jnp.concatenate(b_up[:3] + [b_last] + b_down[1:3] + [b_late] + b_far, axis=0)

    ups, downs = [a_up], [a_down]
    for _ in range(2):
        ups.append(shift(ups[-1], "z", NZ, 1))
        downs.append(shift(downs[-1], "z", NZ, -1))
    half = bundle.shape[0] // 2
    a_cols = [bundle] + ups + downs + [shift(ups[-1][:half], "z", NZ, 1), shift(downs[-1][half:], "z", NZ, -1)]
    b_cols, far = ring(b_bundle, "x", NX)
    b_cols += far
    rows = lax.all_to_all(for_rows, ("x", "z"), split_axis=0, concat_axis=0, tiled=True)
    rows = lax.all_gather(rows, ("y", "core"), axis=0, tiled=False)
    place = jnp.stack([lax.axis_index("x"), lax.axis_index("z")]).astype(jnp.int32)
    return product(place, rows, weight, a_cols, b_cols)


def solution(mesh):
    fine = Mesh(mesh.devices.reshape(NX, NZ, NY, NCORE), ("x", "z", "y", "core"))
    waves = P(("x", "z"), ("y", "core"), None)
    return jax.shard_map(
        per_device,
        mesh=fine,
        in_specs=(waves, waves, P(), P(), P(), P(), P(), P()),
        out_specs=P(("x", "z"), ("y", "core")),
        check_vma=False,
    )
```

```python
import functools
import math

import jax
import jax.numpy as jnp
import ml_dtypes
import numpy as np
from jax import lax
from jax.experimental import pallas as pl
from jax.experimental.pallas import tpu as pltpu
from jax.sharding import Mesh, PartitionSpec as P

NV = 32
NC = 64
GRID = 96
KM = 18
NG = 12000
KEPT = 2 * KM + 1
HALF = KM + 1
NX, NZ, NY, NCORE = 4, 8, 4, 2
NT = NY * NCORE
SLAB = GRID // NT
VB = 8
SB = 8
VC = 4
QC = 4
SLOTS = ((0, 1, 7, 2), (6, 3, 5, 4))
ROWS = SLAB * VC * SB
ZOUT = HALF * 16
YSTEP = 768
NSTEP = GRID * GRID // YSTEP
BTILE = 128
NBT = 5
KWIN = 5
YL = 1408
AEI = 2 * KEPT
RB = 384
GP = 32 * RB
GCH = 768
CODES = 256
NGRP = 3
BF = jnp.bfloat16
F32 = jnp.float32


def tables():
    pos = np.arange(GRID)
    scale = 1.0 / math.sqrt(GRID)

    def angles(freqs):
        turns = (np.mod(freqs, GRID)[None, :] * pos[:, None]) % GRID
        return turns.astype(np.float64) * (2.0 * math.pi / GRID)

    ad = angles(np.arange(HALF))
    depth = np.stack([np.cos(ad), -np.sin(ad)], axis=1) * scale
    ap = angles(np.arange(KEPT) - KM)
    c, s = np.cos(ap), np.sin(ap)
    plane = np.stack([np.stack([c, s]), np.stack([-s, c])], axis=2) * scale
    return depth, plane


def depth_block():
    depth, _ = tables()
    out = np.zeros((2, 4, GRID, HALF, 2, 2, 4), np.float64)
    for h in range(2):
        for y in range(4):
            out[h, y, :, :, h, :, y] = depth.transpose(0, 2, 1)
    return out.reshape(YSTEP, ZOUT).astype(ml_dtypes.bfloat16)


def window(n):
    return min((BTILE * n) // KEPT, HALF - KWIN)


def plane_block():
    _, plane = tables()
    perk = plane.reshape(2, GRID // 4, 4, 2, KEPT).transpose(3, 4, 1, 0, 2).reshape(2, KEPT, 2 * GRID)
    out = np.zeros((YL, KWIN, 2 * GRID), np.float64)
    for d in range(2):
        for b in range(KEPT * HALF):
            k, j = divmod(b, KEPT)
            n, r = divmod(b, BTILE)
            row = n * 2 * BTILE + d * (BTILE if n < NBT else 64) + r
            out[row, k - window(n)] = perk[d, j]
    return out.reshape(YL, KWIN * 2 * GRID).astype(ml_dtypes.bfloat16)


def kron_block():
    _, plane = tables()
    out = np.zeros((2, 2, AEI, SB, NT, QC, SLAB), np.float64)
    for c in range(2):
        for q in range(QC):
            out[c, :, :, c * QC + q, :, q, :] = plane.reshape(2, NT, SLAB, AEI).transpose(0, 3, 1, 2)
    return out.reshape(2, 2, AEI * SB, GRID * QC).astype(ml_dtypes.bfloat16)


def copy_in(refs, spaces, sems):
    copies = [pltpu.make_async_copy(ref, space, sems.at[i]) for i, (ref, space) in enumerate(zip(refs, spaces))]
    for copy in copies:
        copy.start()
    return copies


def spectra_kernel(*refs):
    n = VC + NX + 3
    o_ref, wide, dens, zs, sems = refs[n], *refs[2 * n + 1 :]
    spaces = refs[n + 1 : 2 * n + 1]
    copies = copy_in(refs[:n], spaces, sems)
    v_refs, c_refs, (t_ref, w_ref) = spaces[:VC], spaces[VC : n - 2], spaces[n - 2 :]
    for copy in copies[:-1]:
        copy.wait()

    def body(step, _):
        lanes = pl.ds(pl.multiple_of(step * YSTEP, YSTEP), YSTEP)

        def stack(slot, pieces):
            for i, (ref, b) in enumerate(pieces):
                wide[slot, i * SLAB : (i + 1) * SLAB, :] = ref[b, :, lanes].astype(F32)
            return wide[slot].astype(BF)

        bands = [(c_refs[m], b) for m in range(3) for b in range(2)] + [(c_refs[3], 0), (c_refs[4], 0)]
        cond = [stack(h, bands[QC * h : QC * (h + 1)]) for h in range(2)]
        for v in range(VC):
            val = stack(2 + v, [(v_refs[v], 0)] * QC)
            for h in range(2):
                r0 = (v * 2 + h) * SLAB * QC
                dens[r0 : r0 + SLAB * QC, :] = val * cond[h]
        z = jnp.dot(dens[...], t_ref[...], preferred_element_type=F32).astype(BF)
        zs[:, pl.ds(pl.multiple_of(step * 16, 16), 16), :] = z.T.reshape(HALF, 16, ROWS)
        return 0

    lax.fori_loop(0, NSTEP, body, 0)
    copies[-1].wait()
    for n in range(NBT + 1):
        r0 = n * 2 * BTILE
        rows = 2 * BTILE if n < NBT else BTILE
        k0 = window(n)
        zk = zs[k0 : k0 + KWIN].reshape(KWIN * 2 * GRID, ROWS)
        y = jnp.dot(w_ref[r0 : r0 + rows, :], zk, preferred_element_type=F32)
        yt = y.astype(BF).T.reshape(NT, SLAB * QC, rows)
        if n < NBT - 1:
            l0 = n // 2 * 512 + n % 2 * BTILE
            o_ref[:, :, l0 : l0 + BTILE] = yt[:, :, :BTILE]
            o_ref[:, :, l0 + 256 : l0 + 256 + BTILE] = yt[:, :, BTILE:]
        else:
            o_ref[:, :, r0 : r0 + rows] = yt


def spectra(vs, cs, t, w):
    operands = [*vs, *cs, t, w]
    return pl.pallas_call(
        spectra_kernel,
        in_specs=[pl.BlockSpec(memory_space=pl.ANY)] * len(operands),
        out_specs=pl.BlockSpec(memory_space=pltpu.VMEM),
        out_shape=jax.ShapeDtypeStruct((NT, SLAB * QC, YL), BF),
        scratch_shapes=[pltpu.VMEM(x.shape, BF) for x in operands]
        + [
            pltpu.VMEM((2 + VC, QC * SLAB, YSTEP), F32),
            pltpu.VMEM((ROWS, YSTEP), BF),
            pltpu.VMEM((HALF, 2 * GRID, ROWS), BF),
            pltpu.SemaphoreType.DMA((len(operands),)),
        ],
        compiler_params=pltpu.CompilerParams(vmem_limit_bytes=40 * 2**20),
        name="spectra",
    )(*operands)


def lines_kernel(y0_ref, y1_ref, m_ref, s_ref):
    rows = AEI * SB

    def line(d, lanes):
        parts = [
            jnp.dot(m_ref[c, d], ref[:, lanes], preferred_element_type=F32) for c, ref in ((0, y0_ref), (1, y1_ref))
        ]
        return parts[0] + parts[1]

    for g in range(2):
        s = line(0, pl.ds(512 * g, 256)) + line(1, pl.ds(512 * g + 256, 256))
        s_ref[g * rows : (g + 1) * rows, :] = s.astype(BF)
    s = line(0, pl.ds(1024, BTILE)) + line(1, pl.ds(1024 + BTILE, BTILE))
    s_ref[2 * rows :, :BTILE] = s.astype(BF)
    last = pl.ds(1024 + 2 * BTILE, BTILE)
    s = line(0, last) + pltpu.roll(line(1, last), 64, 1)
    s_ref[2 * rows :, BTILE:] = s.astype(BF)


def lines(y0, y1, m):
    return pl.pallas_call(
        lines_kernel,
        out_shape=jax.ShapeDtypeStruct((NGRP * AEI * SB, CODES), BF),
        compiler_params=pltpu.CompilerParams(vmem_limit_bytes=40 * 2**20),
        name="lines",
    )(y0, y1, m)


def pick_kernel(s_ref, a_ref, b_ref, oc_ref, or_ref):
    codes = lax.broadcasted_iota(jnp.int32, (CODES, CODES), 0)
    outs = []
    for g in range(GCH // CODES):
        lanes = pl.ds(g * CODES, CODES)
        chosen = (codes == b_ref[:, lanes]).astype(F32).astype(BF)
        r = jnp.dot(s_ref[...], chosen, preferred_element_type=F32)
        code = jnp.broadcast_to(a_ref[:, lanes], (SB, CODES))
        acc = jnp.zeros((SB, CODES), F32)
        for a in range(NGRP * AEI):
            acc = jnp.where(code == a, r[a * SB : (a + 1) * SB], acc)
        outs.append(acc.astype(BF))
    out = jnp.concatenate(outs, axis=1)
    oc_ref[0] = out
    for h in range(GCH // RB):
        or_ref[h] = out[:, h * RB : (h + 1) * RB]


def pick(s, a, b):
    per = 4 * RB // GCH
    return pl.pallas_call(
        pick_kernel,
        grid=(GP // GCH,),
        in_specs=[
            pl.BlockSpec((NGRP * AEI * SB, CODES), lambda i: (0, 0)),
            pl.BlockSpec((1, GCH), lambda i: (0, i)),
            pl.BlockSpec((1, GCH), lambda i: (0, i)),
        ],
        out_specs=[
            pl.BlockSpec((1, SB, GCH), lambda i: (i // per, 0, i % per)),
            pl.BlockSpec((GCH // RB, SB, RB), lambda i: (i, 0, 0)),
        ],
        out_shape=[
            jax.ShapeDtypeStruct((NT, SB, 4 * RB), BF),
            jax.ShapeDtypeStruct((32, SB, RB), BF),
        ],
        compiler_params=pltpu.CompilerParams(vmem_limit_bytes=40 * 2**20),
        name="pick",
    )(s, a, b)


KP = NT * SB
LA = 512
XORDER = (0, 1, 3, 2)
ZORDER = (0, 1, 2, 3, 7, 6, 5, 4)


def a_pieces():
    whole = [[(x, z) for x in XORDER] for z in ZORDER[:-1]]
    return whole + [[(x, 4) for x in XORDER[:2]], [(x, 4) for x in XORDER[2:]]]


def b_pieces():
    whole = [[(x, z) for z in range(NZ)] for x in XORDER[:-1]]
    return whole + [[(2, z) for z in range(NZ // 2)], [(2, z) for z in range(NZ // 2, NZ)]]


def product_kernel(xz_ref, w_ref, *refs):
    na, nb = len(a_pieces()), len(b_pieces())
    n = 1 + na + nb
    o_ref, spaces, (wr, acc_ref, sems) = refs[n], refs[n + 1 : 2 * n + 1], refs[2 * n + 1 :]
    copies = copy_in(refs[:n], spaces, sems)
    r_ref, a_refs, b_refs = spaces[0], spaces[1 : 1 + na], spaces[1 + na :]
    copies[0].wait()
    for p in range(32):
        rows = jnp.concatenate([r_ref[t, p].astype(F32) for t in range(NT)], axis=0)
        wr[p] = (rows * w_ref[KP * p : KP * (p + 1), :]).astype(BF)
    for copy in copies[1:]:
        copy.wait()

    def part(pieces, ref, z_of):
        lhs = [wr[lax.rem(xz_ref[0] + (NX - dx), NX) * NZ + z_of(dz)] for dx, dz in pieces]
        return lax.dot_general(
            jnp.concatenate(lhs, axis=0), ref[...], (((0,), (0,)), ((), ())), preferred_element_type=F32
        )

    def total(pieces, operands, z_of):
        acc = part(pieces[0], operands[0], z_of)
        for piece, ref in zip(pieces[1:], operands[1:]):
            acc += part(piece, ref, z_of)
        return acc

    acc_ref[:, :LA] = total(a_pieces(), a_refs, lambda dz: lax.rem(xz_ref[1] + (NZ - dz), NZ))
    acc_ref[:, LA:] = total(b_pieces(), b_refs, lambda z: z)
    for q in range(4):
        o_ref[:, 375 * q : 375 * (q + 1)] = acc_ref[:375, RB * q : RB * q + 375]


def product(place, rows, weight, a_cols, b_cols):
    operands = [rows, *a_cols, *b_cols]
    vmem = pl.BlockSpec(memory_space=pltpu.VMEM)
    return pl.pallas_call(
        product_kernel,
        in_specs=[pl.BlockSpec(memory_space=pltpu.SMEM), vmem] + [pl.BlockSpec(memory_space=pl.ANY)] * len(operands),
        out_specs=vmem,
        out_shape=jax.ShapeDtypeStruct((375, 1500), F32),
        scratch_shapes=[pltpu.VMEM(x.shape, BF) for x in operands]
        + [
            pltpu.VMEM((32, KP, RB), BF),
            pltpu.VMEM((RB, 4 * RB), F32),
            pltpu.SemaphoreType.DMA((len(operands),)),
        ],
        compiler_params=pltpu.CompilerParams(vmem_limit_bytes=48 * 2**20),
        name="product",
    )(place, weight, *operands)


def ring(value, axis, size):
    out_up, out_down = [value], [value]
    for _ in range(size // 2 - 1):
        out_up.append(shift(out_up[-1], axis, size, 1))
        out_down.append(shift(out_down[-1], axis, size, -1))
    half = value.shape[0] // 2
    far = [shift(out_up[-1][:half], axis, size, 1), shift(out_down[-1][half:], axis, size, -1)]
    return out_up + out_down[1:], far


def pick_levels(picks, table):
    codes = jnp.arange(table.shape[0], dtype=jnp.int32)
    return jnp.sum(jnp.where(picks[:, None] == codes[None, :], table[None, :], 0.0), axis=1)


def spread(levels, places):
    codes = jnp.arange(levels.shape[0], dtype=jnp.int32)[None, :]
    return jnp.sum(jnp.where(codes == places.astype(np.int32), levels[None, :], 0.0), axis=1, keepdims=True)


def shift(value, axis, size, step):
    return lax.ppermute(value, axis, [(i, (i + step) % size) for i in range(size)])


def per_device(
    valence_waves,
    cond_waves,
    valence_energy,
    conduction_energy,
    valence_pick,
    cond_pick,
    cond_slot,
    g_index,
):
    cs, far = ring(cond_waves, "x", NX)
    cs += far
    depth, plane, kron = jnp.asarray(depth_block()), jnp.asarray(plane_block()), jnp.asarray(kron_block())
    tile = ("y", "core")
    vs = [valence_waves] + [None] * (VB - 1)
    specs = []
    for m in range(1, VB // 2 + 1):
        if m == VB // 2:
            specs.append(spectra([vs[k] for k in SLOTS[0]], cs, depth, plane))
        vs[m] = shift(vs[m - 1], "z", NZ, 1)
        if m < VB // 2:
            vs[VB - m] = shift(vs[(VB - m + 1) % VB], "z", NZ, -1)
    specs.append(spectra([vs[k] for k in SLOTS[1]], cs, depth, plane))
    slabs = [lax.all_to_all(spec, tile, split_axis=0, concat_axis=0, tiled=True) for spec in specs]

    valence_level = pick_levels(valence_pick, valence_energy)
    band_level = pick_levels(cond_pick, conduction_energy)
    slot_codes = jnp.arange(NC, dtype=jnp.int32)
    slot_level = jnp.sum(
        jnp.where(cond_slot[:, None] == slot_codes[None, :], band_level[:, None], 0.0), axis=0
    )
    factor = 4.0 / math.sqrt(NV * NC)
    xs, zs, ts, c, ms, bs = np.ix_(*(np.arange(n) for n in (NX, NZ, NT, 2, 2, 2)))
    v_of = VB * xs + (zs - np.array(SLOTS)[c, ts // 2]) % NZ
    s_of = 2 * NZ * ((xs - np.array(XORDER)[2 * (ts % 2) + ms]) % NX) + 2 * zs + bs
    v_of, s_of = (np.broadcast_to(m, (NX, NZ, NT, 2, 2, 2)).reshape(NV * NC, 1) for m in (v_of, s_of))
    weight = factor / (spread(valence_level, v_of) - spread(slot_level, s_of))

    index = jnp.pad(g_index.reshape(32, 375), ((0, 0), (0, RB - 375))).reshape(1, GP)
    a_code = index // (KEPT * HALF)
    rest = index % (KEPT * HALF)
    b_code = (rest % HALF) * KEPT + rest // HALF
    a_code = a_code + AEI * (b_code // CODES)
    b_code = b_code % CODES

    combined = lines(slabs[0].reshape(GRID * QC, YL), slabs[1].reshape(GRID * QC, YL), kron)
    cols, for_rows = pick(combined, a_code, b_code)
    cols = lax.all_to_all(cols, tile, split_axis=0, concat_axis=0, tiled=True).reshape(KP, 4 * RB)
    b_bundle = lax.all_gather(cols[:, LA:], "z", axis=0, tiled=True)
    near, far = ring(cols[:, :LA], "x", NX)
    for_rows, near[1] = lax.optimization_barrier((for_rows, near[1]))
    a_cols, a_far = ring(jnp.concatenate(near + far, axis=0), "z", NZ)
    b_cols, b_far = ring(b_bundle, "x", NX)
    rows = lax.all_to_all(for_rows, ("x", "z"), split_axis=0, concat_axis=0, tiled=True)
    rows = lax.all_gather(rows, ("y", "core"), axis=0, tiled=False)
    place = jnp.stack([lax.axis_index("x"), lax.axis_index("z")]).astype(jnp.int32)
    return product(place, rows, weight, a_cols + a_far, b_cols + b_far)


def solution(mesh):
    fine = Mesh(mesh.devices.reshape(NX, NZ, NY, NCORE), ("x", "z", "y", "core"))
    waves = P(("x", "z"), ("y", "core"), None)
    return jax.shard_map(
        per_device,
        mesh=fine,
        in_specs=(waves, waves, P(), P(), P(), P(), P(), P()),
        out_specs=P(("x", "z"), ("y", "core")),
        check_vma=False,
    )
```

```python
import functools
import math

import jax
import jax.numpy as jnp
import ml_dtypes
import numpy as np
from jax import lax
from jax.experimental import pallas as pl
from jax.experimental.pallas import tpu as pltpu
from jax.sharding import Mesh, PartitionSpec as P

NV = 32
NC = 64
GRID = 96
KM = 18
NG = 12000
KEPT = 2 * KM + 1
HALF = KM + 1
NX, NZ, NY, NCORE = 4, 8, 4, 2
NT = NY * NCORE
SLAB = GRID // NT
VB = 8
SB = 8
VC = 4
QC = 4
SLOTS = ((0, 1, 7, 2), (6, 3, 5, 4))
ROWS = SLAB * VC * SB
ZOUT = HALF * 16
YSTEP = 768
NSTEP = GRID * GRID // YSTEP
BTILE = 128
NBT = 5
KWIN = 5
YL = 1408
AEI = 2 * KEPT
RB = 384
GP = 32 * RB
GCH = 768
CODES = 256
NGRP = 3
BF = jnp.bfloat16
F32 = jnp.float32


def tables():
    pos = np.arange(GRID)
    scale = 1.0 / math.sqrt(GRID)

    def angles(freqs):
        turns = (np.mod(freqs, GRID)[None, :] * pos[:, None]) % GRID
        return turns.astype(np.float64) * (2.0 * math.pi / GRID)

    ad = angles(np.arange(HALF))
    depth = np.stack([np.cos(ad), -np.sin(ad)], axis=1) * scale
    ap = angles(np.arange(KEPT) - KM)
    c, s = np.cos(ap), np.sin(ap)
    plane = np.stack([np.stack([c, s]), np.stack([-s, c])], axis=2) * scale
    return depth, plane


def depth_block():
    depth, _ = tables()
    out = np.zeros((2, 4, GRID, HALF, 2, 2, 4), np.float64)
    for h in range(2):
        for y in range(4):
            out[h, y, :, :, h, :, y] = depth.transpose(0, 2, 1)
    return out.reshape(YSTEP, ZOUT).astype(ml_dtypes.bfloat16)


def window(n):
    return min((BTILE * n) // KEPT, HALF - KWIN)


def plane_block():
    _, plane = tables()
    perk = plane.reshape(2, GRID // 4, 4, 2, KEPT).transpose(3, 4, 1, 0, 2).reshape(2, KEPT, 2 * GRID)
    out = np.zeros((YL, KWIN, 2 * GRID), np.float64)
    for d in range(2):
        for b in range(KEPT * HALF):
            k, j = divmod(b, KEPT)
            n, r = divmod(b, BTILE)
            row = n * 2 * BTILE + d * (BTILE if n < NBT else 64) + r
            out[row, k - window(n)] = perk[d, j]
    return out.reshape(YL, KWIN * 2 * GRID).astype(ml_dtypes.bfloat16)


def kron_block():
    _, plane = tables()
    out = np.zeros((2, AEI, QC, NT, QC, SLAB), np.float64)
    for q in range(QC):
        out[:, :, q, :, q, :] = plane.reshape(2, NT, SLAB, AEI).transpose(0, 3, 1, 2)
    return out.reshape(2, AEI * QC, GRID * QC).astype(ml_dtypes.bfloat16)


def copy_in(refs, spaces, sems):
    copies = [pltpu.make_async_copy(ref, space, sems.at[i]) for i, (ref, space) in enumerate(zip(refs, spaces))]
    for copy in copies:
        copy.start()
    return copies


def spectra_kernel(*refs):
    n = VC + NX + 3
    o_ref, wide, dens, zs, sems = refs[n], *refs[2 * n + 1 :]
    spaces = refs[n + 1 : 2 * n + 1]
    copies = copy_in(refs[:n], spaces, sems)
    v_refs, c_refs, (t_ref, w_ref) = spaces[:VC], spaces[VC : n - 2], spaces[n - 2 :]
    for copy in copies[:-1]:
        copy.wait()

    def body(step, _):
        lanes = pl.ds(pl.multiple_of(step * YSTEP, YSTEP), YSTEP)

        def stack(slot, pieces):
            for i, (ref, b) in enumerate(pieces):
                wide[slot, i * SLAB : (i + 1) * SLAB, :] = ref[b, :, lanes].astype(F32)
            return wide[slot].astype(BF)

        bands = [(c_refs[m], b) for m in range(3) for b in range(2)] + [(c_refs[3], 0), (c_refs[4], 0)]
        cond = [stack(h, bands[QC * h : QC * (h + 1)]) for h in range(2)]
        for v in range(VC):
            val = stack(2 + v, [(v_refs[v], 0)] * QC)
            for h in range(2):
                r0 = (v * 2 + h) * SLAB * QC
                dens[r0 : r0 + SLAB * QC, :] = val * cond[h]
        z = jnp.dot(dens[...], t_ref[...], preferred_element_type=F32).astype(BF)
        zs[:, pl.ds(pl.multiple_of(step * 16, 16), 16), :] = z.T.reshape(HALF, 16, ROWS)
        return 0

    lax.fori_loop(0, NSTEP, body, 0)
    copies[-1].wait()
    for n in range(NBT + 1):
        r0 = n * 2 * BTILE
        rows = 2 * BTILE if n < NBT else BTILE
        k0 = window(n)
        zk = zs[k0 : k0 + KWIN].reshape(KWIN * 2 * GRID, ROWS)
        y = jnp.dot(w_ref[r0 : r0 + rows, :], zk, preferred_element_type=F32)
        yt = y.astype(BF).T.reshape(NT, SLAB * QC, rows)
        if n < NBT - 1:
            l0 = n // 2 * 512 + n % 2 * BTILE
            o_ref[:, :, l0 : l0 + BTILE] = yt[:, :, :BTILE]
            o_ref[:, :, l0 + 256 : l0 + 256 + BTILE] = yt[:, :, BTILE:]
        else:
            o_ref[:, :, r0 : r0 + rows] = yt


def spectra(vs, cs, t, w):
    operands = [*vs, *cs, t, w]
    return pl.pallas_call(
        spectra_kernel,
        in_specs=[pl.BlockSpec(memory_space=pl.ANY)] * len(operands),
        out_specs=pl.BlockSpec(memory_space=pltpu.VMEM),
        out_shape=jax.ShapeDtypeStruct((NT, SLAB * QC, YL), BF),
        scratch_shapes=[pltpu.VMEM(x.shape, BF) for x in operands]
        + [
            pltpu.VMEM((2 + VC, QC * SLAB, YSTEP), F32),
            pltpu.VMEM((ROWS, YSTEP), BF),
            pltpu.VMEM((HALF, 2 * GRID, ROWS), BF),
            pltpu.SemaphoreType.DMA((len(operands),)),
        ],
        compiler_params=pltpu.CompilerParams(vmem_limit_bytes=58 * 2**20),
        name="spectra",
    )(*operands)


def lines_kernel(y_ref, m_ref, s_ref):
    rows = AEI * QC

    def line(d, lanes):
        return jnp.dot(m_ref[d], y_ref[:, lanes], preferred_element_type=F32)

    for g in range(2):
        s = line(0, pl.ds(512 * g, 256)) + line(1, pl.ds(512 * g + 256, 256))
        s_ref[g * rows : (g + 1) * rows, :] = s.astype(BF)
    s = line(0, pl.ds(1024, BTILE)) + line(1, pl.ds(1024 + BTILE, BTILE))
    s_ref[2 * rows :, :BTILE] = s.astype(BF)
    last = pl.ds(1024 + 2 * BTILE, BTILE)
    s = line(0, last) + pltpu.roll(line(1, last), 64, 1)
    s_ref[2 * rows :, BTILE:] = s.astype(BF)


def lines(y, m):
    return pl.pallas_call(
        lines_kernel,
        out_shape=jax.ShapeDtypeStruct((NGRP * AEI * QC, CODES), BF),
        compiler_params=pltpu.CompilerParams(vmem_limit_bytes=40 * 2**20),
        name="lines",
    )(y, m)


def picked(s_ref, a_ref, b_ref, chunk):
    codes = lax.broadcasted_iota(jnp.int32, (CODES, CODES), 0)
    row = lax.broadcasted_iota(jnp.int32, (SB, CODES), 0)
    outs = []
    for g in range(GCH // CODES):
        lanes = pl.ds(g * CODES, CODES)
        chosen = (codes == b_ref[:, lanes]).astype(F32).astype(BF)
        r = jnp.dot(s_ref[...], chosen, preferred_element_type=F32)
        code = a_ref[:, lanes] - row // QC
        acc = jnp.zeros((SB, CODES), F32)
        for a in range(0, NGRP * AEI, 2):
            acc = jnp.where(code == a, r[a * QC : (a + 2) * QC], acc)
        both = acc + pltpu.roll(acc, QC, 0)
        outs.append(jnp.where(row // QC == chunk, both, 0.0))
    return jnp.concatenate(outs, axis=1)


def first_kernel(s_ref, a_ref, b_ref, o_ref):
    o_ref[...] = picked(s_ref, a_ref, b_ref, 0)


def second_kernel(s_ref, a_ref, b_ref, first_ref, oc_ref, or_ref):
    out = (first_ref[...] + picked(s_ref, a_ref, b_ref, 1)).astype(BF)
    oc_ref[0] = out
    for h in range(GCH // RB):
        or_ref[h] = out[:, h * RB : (h + 1) * RB]


def pick_specs():
    return [
        pl.BlockSpec((NGRP * AEI * QC, CODES), lambda i: (0, 0)),
        pl.BlockSpec((1, GCH), lambda i: (0, i)),
        pl.BlockSpec((1, GCH), lambda i: (0, i)),
    ]


def pick_first(s, a, b):
    return pl.pallas_call(
        first_kernel,
        grid=(GP // GCH,),
        in_specs=pick_specs(),
        out_specs=pl.BlockSpec((SB, GCH), lambda i: (0, i)),
        out_shape=jax.ShapeDtypeStruct((SB, GP), F32),
        compiler_params=pltpu.CompilerParams(vmem_limit_bytes=40 * 2**20),
        name="pick_first",
    )(s, a, b)


def pick_second(s, a, b, first):
    per = 4 * RB // GCH
    return pl.pallas_call(
        second_kernel,
        grid=(GP // GCH,),
        in_specs=pick_specs() + [pl.BlockSpec((SB, GCH), lambda i: (0, i))],
        out_specs=[
            pl.BlockSpec((1, SB, GCH), lambda i: (i // per, 0, i % per)),
            pl.BlockSpec((GCH // RB, SB, RB), lambda i: (i, 0, 0)),
        ],
        out_shape=[
            jax.ShapeDtypeStruct((NT, SB, 4 * RB), BF),
            jax.ShapeDtypeStruct((32, SB, RB), BF),
        ],
        compiler_params=pltpu.CompilerParams(vmem_limit_bytes=40 * 2**20),
        name="pick_second",
    )(s, a, b, first)


KP = NT * SB
LA = 512
XORDER = (0, 1, 3, 2)
ZORDER = (0, 1, 2, 3, 7, 6, 5, 4)


def a_pieces():
    whole = [[(x, z) for x in XORDER] for z in ZORDER[:-1]]
    return whole + [[(x, 4) for x in XORDER[:2]], [(x, 4) for x in XORDER[2:]]]


def b_pieces():
    whole = [[(x, z) for z in range(NZ)] for x in XORDER[:-1]]
    return whole + [[(2, z) for z in range(NZ // 2)], [(2, z) for z in range(NZ // 2, NZ)]]


def product_kernel(xz_ref, w_ref, *refs):
    na, nb = len(a_pieces()), len(b_pieces())
    n = 1 + na + nb
    o_ref, spaces, (wr, acc_ref, sems) = refs[n], refs[n + 1 : 2 * n + 1], refs[2 * n + 1 :]
    copies = copy_in(refs[:n], spaces, sems)
    r_ref, a_refs, b_refs = spaces[0], spaces[1 : 1 + na], spaces[1 + na :]
    copies[0].wait()
    for p in range(32):
        rows = jnp.concatenate([r_ref[t, p].astype(F32) for t in range(NT)], axis=0)
        wr[p] = (rows * w_ref[KP * p : KP * (p + 1), :]).astype(BF)
    for copy in copies[1:]:
        copy.wait()

    def part(pieces, ref, z_of):
        lhs = [wr[lax.rem(xz_ref[0] + (NX - dx), NX) * NZ + z_of(dz)] for dx, dz in pieces]
        return lax.dot_general(
            jnp.concatenate(lhs, axis=0), ref[...], (((0,), (0,)), ((), ())), preferred_element_type=F32
        )

    def total(pieces, operands, z_of):
        acc = part(pieces[0], operands[0], z_of)
        for piece, ref in zip(pieces[1:], operands[1:]):
            acc += part(piece, ref, z_of)
        return acc

    acc_ref[:, :LA] = total(a_pieces(), a_refs, lambda dz: lax.rem(xz_ref[1] + (NZ - dz), NZ))
    acc_ref[:, LA:] = total(b_pieces(), b_refs, lambda z: z)
    for q in range(4):
        o_ref[:, 375 * q : 375 * (q + 1)] = acc_ref[:375, RB * q : RB * q + 375]


def product(place, rows, weight, a_cols, b_cols):
    operands = [rows, *a_cols, *b_cols]
    vmem = pl.BlockSpec(memory_space=pltpu.VMEM)
    return pl.pallas_call(
        product_kernel,
        in_specs=[pl.BlockSpec(memory_space=pltpu.SMEM), vmem] + [pl.BlockSpec(memory_space=pl.ANY)] * len(operands),
        out_specs=vmem,
        out_shape=jax.ShapeDtypeStruct((375, 1500), F32),
        scratch_shapes=[pltpu.VMEM(x.shape, BF) for x in operands]
        + [
            pltpu.VMEM((32, KP, RB), BF),
            pltpu.VMEM((RB, 4 * RB), F32),
            pltpu.SemaphoreType.DMA((len(operands),)),
        ],
        compiler_params=pltpu.CompilerParams(vmem_limit_bytes=58 * 2**20),
        name="product",
    )(place, weight, *operands)


def ring(value, axis, size):
    out_up, out_down = [value], [value]
    for _ in range(size // 2 - 1):
        out_up.append(shift(out_up[-1], axis, size, 1))
        out_down.append(shift(out_down[-1], axis, size, -1))
    half = value.shape[0] // 2
    far = [shift(out_up[-1][:half], axis, size, 1), shift(out_down[-1][half:], axis, size, -1)]
    return out_up + out_down[1:], far


def pick_levels(picks, table):
    codes = jnp.arange(table.shape[0], dtype=jnp.int32)
    return jnp.sum(jnp.where(picks[:, None] == codes[None, :], table[None, :], 0.0), axis=1)


def spread(levels, places):
    codes = jnp.arange(levels.shape[0], dtype=jnp.int32)[None, :]
    return jnp.sum(jnp.where(codes == places.astype(np.int32), levels[None, :], 0.0), axis=1, keepdims=True)


def shift(value, axis, size, step):
    return lax.ppermute(value, axis, [(i, (i + step) % size) for i in range(size)])


def per_device(
    valence_waves,
    cond_waves,
    valence_energy,
    conduction_energy,
    valence_pick,
    cond_pick,
    cond_slot,
    g_index,
):
    cs, far = ring(cond_waves, "x", NX)
    cs += far
    depth, plane, kron = jnp.asarray(depth_block()), jnp.asarray(plane_block()), jnp.asarray(kron_block())
    tile = ("y", "core")
    vs = [valence_waves] + [None] * (VB - 1)
    specs = []
    for m in range(1, VB // 2 + 1):
        if m == VB // 2:
            specs.append(spectra([vs[k] for k in SLOTS[0]], cs, depth, plane))
        vs[m] = shift(vs[m - 1], "z", NZ, 1)
        if m < VB // 2:
            vs[VB - m] = shift(vs[(VB - m + 1) % VB], "z", NZ, -1)
    specs.append(spectra([vs[k] for k in SLOTS[1]], cs, depth, plane))
    slabs = [lax.all_to_all(specs[0], tile, split_axis=0, concat_axis=0, tiled=True)]
    slabs[0], specs[1] = lax.optimization_barrier((slabs[0], specs[1]))
    slabs.append(lax.all_to_all(specs[1], tile, split_axis=0, concat_axis=0, tiled=True))

    valence_level = pick_levels(valence_pick, valence_energy)
    band_level = pick_levels(cond_pick, conduction_energy)
    slot_codes = jnp.arange(NC, dtype=jnp.int32)
    slot_level = jnp.sum(
        jnp.where(cond_slot[:, None] == slot_codes[None, :], band_level[:, None], 0.0), axis=0
    )
    factor = 4.0 / math.sqrt(NV * NC)
    xs, zs, ts, c, ms, bs = np.ix_(*(np.arange(n) for n in (NX, NZ, NT, 2, 2, 2)))
    v_of = VB * xs + (zs - np.array(SLOTS)[c, ts // 2]) % NZ
    s_of = 2 * NZ * ((xs - np.array(XORDER)[2 * (ts % 2) + ms]) % NX) + 2 * zs + bs
    v_of, s_of = (np.broadcast_to(m, (NX, NZ, NT, 2, 2, 2)).reshape(NV * NC, 1) for m in (v_of, s_of))
    weight = factor / (spread(valence_level, v_of) - spread(slot_level, s_of))

    index = jnp.pad(g_index.reshape(32, 375), ((0, 0), (0, RB - 375))).reshape(1, GP)
    a_code = index // (KEPT * HALF)
    rest = index % (KEPT * HALF)
    b_code = (rest % HALF) * KEPT + rest // HALF
    a_code = a_code + AEI * (b_code // CODES)
    b_code = b_code % CODES

    first = pick_first(lines(slabs[0].reshape(GRID * QC, YL), kron), a_code, b_code)
    cols, for_rows = pick_second(lines(slabs[1].reshape(GRID * QC, YL), kron), a_code, b_code, first)
    cols = lax.all_to_all(cols, tile, split_axis=0, concat_axis=0, tiled=True).reshape(KP, 4 * RB)
    b_bundle = lax.all_gather(cols[:, LA:], "z", axis=0, tiled=True)
    near, far = ring(cols[:, :LA], "x", NX)
    for_rows, near[1], near[2] = lax.optimization_barrier((for_rows, near[1], near[2]))
    a_cols, a_far = ring(jnp.concatenate(near + far, axis=0), "z", NZ)
    b_cols, b_far = ring(b_bundle, "x", NX)
    rows = lax.all_to_all(for_rows, ("x", "z"), split_axis=0, concat_axis=0, tiled=True)
    rows = lax.all_gather(rows, ("y", "core"), axis=0, tiled=False)
    place = jnp.stack([lax.axis_index("x"), lax.axis_index("z")]).astype(jnp.int32)
    return product(place, rows, weight, a_cols + a_far, b_cols + b_far)


def solution(mesh):
    fine = Mesh(mesh.devices.reshape(NX, NZ, NY, NCORE), ("x", "z", "y", "core"))
    waves = P(("x", "z"), ("y", "core"), None)
    return jax.shard_map(
        per_device,
        mesh=fine,
        in_specs=(waves, waves, P(), P(), P(), P(), P(), P()),
        out_specs=P(("x", "z"), ("y", "core")),
        check_vma=False,
    )
```

```python
import functools
import math

import jax
import jax.numpy as jnp
import ml_dtypes
import numpy as np
from jax import lax
from jax.experimental import pallas as pl
from jax.experimental.pallas import tpu as pltpu
from jax.sharding import Mesh, PartitionSpec as P

NV = 32
NC = 64
GRID = 96
KM = 18
NG = 12000
KEPT = 2 * KM + 1
HALF = KM + 1
NX, NZ, NY, NCORE = 4, 8, 4, 2
NT = NY * NCORE
SLAB = GRID // NT
VB = 8
SB = 8
VC = 4
QC = 4
SLOTS = ((0, 1, 7, 2), (6, 3, 5, 4))
ROWS = SLAB * VC * SB
ZOUT = HALF * 16
YSTEP = 768
NSTEP = GRID * GRID // YSTEP
BTILE = 128
NBT = 5
KWIN = 5
YL = 1408
AEI = 2 * KEPT
RB = 384
GP = 32 * RB
GCH = 768
CODES = 256
NGRP = 3
BF = jnp.bfloat16
F32 = jnp.float32


def tables():
    pos = np.arange(GRID)
    scale = 1.0 / math.sqrt(GRID)

    def angles(freqs):
        turns = (np.mod(freqs, GRID)[None, :] * pos[:, None]) % GRID
        return turns.astype(np.float64) * (2.0 * math.pi / GRID)

    ad = angles(np.arange(HALF))
    depth = np.stack([np.cos(ad), -np.sin(ad)], axis=1) * scale
    ap = angles(np.arange(KEPT) - KM)
    c, s = np.cos(ap), np.sin(ap)
    plane = np.stack([np.stack([c, s]), np.stack([-s, c])], axis=2) * scale
    return depth, plane


def depth_block():
    depth, _ = tables()
    out = np.zeros((2, 4, GRID, HALF, 2, 2, 4), np.float64)
    for h in range(2):
        for y in range(4):
            out[h, y, :, :, h, :, y] = depth.transpose(0, 2, 1)
    return out.reshape(YSTEP, ZOUT).astype(ml_dtypes.bfloat16)


def window(n):
    return min((BTILE * n) // KEPT, HALF - KWIN)


def plane_block():
    _, plane = tables()
    perk = plane.reshape(2, GRID // 4, 4, 2, KEPT).transpose(3, 4, 1, 0, 2).reshape(2, KEPT, 2 * GRID)
    out = np.zeros((YL, KWIN, 2 * GRID), np.float64)
    for d in range(2):
        for b in range(KEPT * HALF):
            k, j = divmod(b, KEPT)
            n, r = divmod(b, BTILE)
            row = n * 2 * BTILE + d * (BTILE if n < NBT else 64) + r
            out[row, k - window(n)] = perk[d, j]
    return out.reshape(YL, KWIN * 2 * GRID).astype(ml_dtypes.bfloat16)


def kron_block():
    _, plane = tables()
    out = np.zeros((2, AEI, QC, NT, QC * SLAB), np.float64)
    slabs = plane.reshape(2, NT, SLAB, AEI).transpose(0, 3, 1, 2)
    for q in range(QC):
        out[:, :, q, :, 8 * q : 8 * q + 8] = slabs[..., :8]
        out[:, :, q, :, 8 * QC + 4 * q : 8 * QC + 4 * q + 4] = slabs[..., 8:]
    return out.reshape(2, AEI * QC, GRID * QC).astype(ml_dtypes.bfloat16)


def copy_in(refs, spaces, sems):
    copies = [pltpu.make_async_copy(ref, space, sems.at[i]) for i, (ref, space) in enumerate(zip(refs, spaces))]
    for copy in copies:
        copy.start()
    return copies


def spectra_kernel(*refs):
    n = VC + NX + 3
    o_ref, dens, zs, sems = refs[n], *refs[2 * n + 1 :]
    spaces = refs[n + 1 : 2 * n + 1]
    copies = copy_in(refs[:n], spaces, sems)
    v_refs, c_refs, (t_ref, w_ref) = spaces[:VC], spaces[VC : n - 2], spaces[n - 2 :]
    for copy in copies[:-1]:
        copy.wait()

    def body(step, _):
        lanes = pl.ds(pl.multiple_of(step * YSTEP, YSTEP), YSTEP)

        def parts(ref, b):
            wave = ref[b, :, lanes].astype(F32)
            return wave[:8], wave[8:]

        def tile(pieces):
            heads = [head for head, _ in pieces]
            tails = [jnp.concatenate([pieces[i][1], pieces[i + 1][1]], axis=0) for i in range(0, QC, 2)]
            return jnp.concatenate(heads + tails, axis=0).astype(BF)

        bands = [(c_refs[m], b) for m in range(3) for b in range(2)] + [(c_refs[3], 0), (c_refs[4], 0)]
        cond = [tile([parts(ref, b) for ref, b in bands[QC * h : QC * (h + 1)]]) for h in range(2)]
        for v in range(VC):
            val = tile([parts(v_refs[v], 0)] * QC)
            for h in range(2):
                r0 = (v * 2 + h) * SLAB * QC
                dens[r0 : r0 + SLAB * QC, :] = val * cond[h]
        z = jnp.dot(dens[...], t_ref[...], preferred_element_type=F32).astype(BF)
        zs[:, pl.ds(pl.multiple_of(step * 16, 16), 16), :] = z.T.reshape(HALF, 16, ROWS)
        return 0

    lax.fori_loop(0, NSTEP, body, 0)
    copies[-1].wait()
    for n in range(NBT + 1):
        r0 = n * 2 * BTILE
        rows = 2 * BTILE if n < NBT else BTILE
        k0 = window(n)
        zk = zs[k0 : k0 + KWIN].reshape(KWIN * 2 * GRID, ROWS)
        y = jnp.dot(w_ref[r0 : r0 + rows, :], zk, preferred_element_type=F32)
        yt = y.astype(BF).T.reshape(NT, SLAB * QC, rows)
        if n < NBT - 1:
            l0 = n // 2 * 512 + n % 2 * BTILE
            o_ref[:, :, l0 : l0 + BTILE] = yt[:, :, :BTILE]
            o_ref[:, :, l0 + 256 : l0 + 256 + BTILE] = yt[:, :, BTILE:]
        else:
            o_ref[:, :, r0 : r0 + rows] = yt


def spectra(vs, cs, t, w):
    operands = [*vs, *cs, t, w]
    return pl.pallas_call(
        spectra_kernel,
        in_specs=[pl.BlockSpec(memory_space=pl.ANY)] * len(operands),
        out_specs=pl.BlockSpec(memory_space=pltpu.VMEM),
        out_shape=jax.ShapeDtypeStruct((NT, SLAB * QC, YL), BF),
        scratch_shapes=[pltpu.VMEM(x.shape, BF) for x in operands]
        + [
            pltpu.VMEM((ROWS, YSTEP), BF),
            pltpu.VMEM((HALF, 2 * GRID, ROWS), BF),
            pltpu.SemaphoreType.DMA((len(operands),)),
        ],
        compiler_params=pltpu.CompilerParams(vmem_limit_bytes=58 * 2**20),
        name="spectra",
    )(*operands)


def lines_kernel(y_ref, m_ref, s_ref):
    rows = AEI * QC

    def line(d, lanes):
        return jnp.dot(m_ref[d], y_ref[:, lanes], preferred_element_type=F32)

    for g in range(2):
        s = line(0, pl.ds(512 * g, 256)) + line(1, pl.ds(512 * g + 256, 256))
        s_ref[g * rows : (g + 1) * rows, :] = s.astype(BF)
    s = line(0, pl.ds(1024, BTILE)) + line(1, pl.ds(1024 + BTILE, BTILE))
    s_ref[2 * rows :, :BTILE] = s.astype(BF)
    last = pl.ds(1024 + 2 * BTILE, BTILE)
    s = line(0, last) + pltpu.roll(line(1, last), 64, 1)
    s_ref[2 * rows :, BTILE:] = s.astype(BF)


def lines(y, m):
    return pl.pallas_call(
        lines_kernel,
        out_shape=jax.ShapeDtypeStruct((NGRP * AEI * QC, CODES), BF),
        compiler_params=pltpu.CompilerParams(vmem_limit_bytes=40 * 2**20),
        name="lines",
    )(y, m)


def picked(s_ref, a_ref, b_ref, chunk):
    codes = lax.broadcasted_iota(jnp.int32, (CODES, CODES), 0)
    row = lax.broadcasted_iota(jnp.int32, (SB, CODES), 0)
    outs = []
    for g in range(GCH // CODES):
        lanes = pl.ds(g * CODES, CODES)
        chosen = (codes == b_ref[:, lanes]).astype(F32).astype(BF)
        r = jnp.dot(s_ref[...], chosen, preferred_element_type=F32)
        code = a_ref[:, lanes] - row // QC
        acc = jnp.zeros((SB, CODES), F32)
        for a in range(0, NGRP * AEI, 2):
            acc = jnp.where(code == a, r[a * QC : (a + 2) * QC], acc)
        both = acc + pltpu.roll(acc, QC, 0)
        outs.append(jnp.where(row // QC == chunk, both, 0.0))
    return jnp.concatenate(outs, axis=1)


def first_kernel(s_ref, a_ref, b_ref, o_ref):
    o_ref[...] = picked(s_ref, a_ref, b_ref, 0)


def second_kernel(s_ref, a_ref, b_ref, first_ref, oc_ref, or_ref):
    out = (first_ref[...] + picked(s_ref, a_ref, b_ref, 1)).astype(BF)
    oc_ref[0] = out
    for h in range(GCH // RB):
        or_ref[h] = out[:, h * RB : (h + 1) * RB]


def pick_specs():
    return [
        pl.BlockSpec((NGRP * AEI * QC, CODES), lambda i: (0, 0)),
        pl.BlockSpec((1, GCH), lambda i: (0, i)),
        pl.BlockSpec((1, GCH), lambda i: (0, i)),
    ]


def pick_first(s, a, b):
    return pl.pallas_call(
        first_kernel,
        grid=(GP // GCH,),
        in_specs=pick_specs(),
        out_specs=pl.BlockSpec((SB, GCH), lambda i: (0, i)),
        out_shape=jax.ShapeDtypeStruct((SB, GP), F32),
        compiler_params=pltpu.CompilerParams(vmem_limit_bytes=40 * 2**20),
        name="pick_first",
    )(s, a, b)


def pick_second(s, a, b, first):
    per = 4 * RB // GCH
    return pl.pallas_call(
        second_kernel,
        grid=(GP // GCH,),
        in_specs=pick_specs() + [pl.BlockSpec((SB, GCH), lambda i: (0, i))],
        out_specs=[
            pl.BlockSpec((1, SB, GCH), lambda i: (i // per, 0, i % per)),
            pl.BlockSpec((GCH // RB, SB, RB), lambda i: (i, 0, 0)),
        ],
        out_shape=[
            jax.ShapeDtypeStruct((NT, SB, 4 * RB), BF),
            jax.ShapeDtypeStruct((32, SB, RB), BF),
        ],
        compiler_params=pltpu.CompilerParams(vmem_limit_bytes=40 * 2**20),
        name="pick_second",
    )(s, a, b, first)


KP = NT * SB
LA = 512
XORDER = (0, 1, 3, 2)
ZORDER = (0, 1, 2, 3, 7, 6, 5, 4)


def a_pieces():
    whole = [[(x, z) for x in XORDER] for z in ZORDER[:-1]]
    return whole + [[(x, 4) for x in XORDER[:2]], [(x, 4) for x in XORDER[2:]]]


def b_pieces():
    whole = [[(x, z) for z in range(NZ)] for x in XORDER[:-1]]
    return whole + [[(2, z) for z in range(NZ // 2)], [(2, z) for z in range(NZ // 2, NZ)]]


def product_kernel(xz_ref, w_ref, *refs):
    na, nb = len(a_pieces()), len(b_pieces())
    n = 1 + na + nb
    o_ref, spaces, (wr, acc_ref, sems) = refs[n], refs[n + 1 : 2 * n + 1], refs[2 * n + 1 :]
    copies = copy_in(refs[:n], spaces, sems)
    r_ref, a_refs, b_refs = spaces[0], spaces[1 : 1 + na], spaces[1 + na :]
    copies[0].wait()
    for p in range(32):
        rows = jnp.concatenate([r_ref[t, p].astype(F32) for t in range(NT)], axis=0)
        wr[p] = (rows * w_ref[KP * p : KP * (p + 1), :]).astype(BF)
    for copy in copies[1:]:
        copy.wait()

    def part(pieces, ref, z_of):
        lhs = [wr[lax.rem(xz_ref[0] + (NX - dx), NX) * NZ + z_of(dz)] for dx, dz in pieces]
        return lax.dot_general(
            jnp.concatenate(lhs, axis=0), ref[...], (((0,), (0,)), ((), ())), preferred_element_type=F32
        )

    def total(pieces, operands, z_of):
        acc = part(pieces[0], operands[0], z_of)
        for piece, ref in zip(pieces[1:], operands[1:]):
            acc += part(piece, ref, z_of)
        return acc

    acc_ref[:, :LA] = total(a_pieces(), a_refs, lambda dz: lax.rem(xz_ref[1] + (NZ - dz), NZ))
    acc_ref[:, LA:] = total(b_pieces(), b_refs, lambda z: z)
    for q in range(4):
        o_ref[:, 375 * q : 375 * (q + 1)] = acc_ref[:375, RB * q : RB * q + 375]


def product(place, rows, weight, a_cols, b_cols):
    operands = [rows, *a_cols, *b_cols]
    vmem = pl.BlockSpec(memory_space=pltpu.VMEM)
    return pl.pallas_call(
        product_kernel,
        in_specs=[pl.BlockSpec(memory_space=pltpu.SMEM), vmem] + [pl.BlockSpec(memory_space=pl.ANY)] * len(operands),
        out_specs=vmem,
        out_shape=jax.ShapeDtypeStruct((375, 1500), F32),
        scratch_shapes=[pltpu.VMEM(x.shape, BF) for x in operands]
        + [
            pltpu.VMEM((32, KP, RB), BF),
            pltpu.VMEM((RB, 4 * RB), F32),
            pltpu.SemaphoreType.DMA((len(operands),)),
        ],
        compiler_params=pltpu.CompilerParams(vmem_limit_bytes=58 * 2**20),
        name="product",
    )(place, weight, *operands)


def ring(value, axis, size):
    return ring_on(value, shift(value, axis, size, 1), shift(value, axis, size, -1), axis, size)


def ring_on(value, up, down, axis, size):
    ups, downs = [up], [down]
    for _ in range(size // 2 - 2):
        ups.append(shift(ups[-1], axis, size, 1))
        downs.append(shift(downs[-1], axis, size, -1))
    half = value.shape[0] // 2
    far = [shift(ups[-1][:half], axis, size, 1), shift(downs[-1][half:], axis, size, -1)]
    return [value] + ups + downs, far


def pick_levels(picks, table):
    codes = jnp.arange(table.shape[0], dtype=jnp.int32)
    return jnp.sum(jnp.where(picks[:, None] == codes[None, :], table[None, :], 0.0), axis=1)


def spread(levels, places):
    codes = jnp.arange(levels.shape[0], dtype=jnp.int32)[None, :]
    return jnp.sum(jnp.where(codes == places.astype(np.int32), levels[None, :], 0.0), axis=1, keepdims=True)


def shift(value, axis, size, step):
    return lax.ppermute(value, axis, [(i, (i + step) % size) for i in range(size)])


def per_device(
    valence_waves,
    cond_waves,
    valence_energy,
    conduction_energy,
    valence_pick,
    cond_pick,
    cond_slot,
    g_index,
):
    cs, far = ring(cond_waves, "x", NX)
    cs += far
    depth, plane, kron = jnp.asarray(depth_block()), jnp.asarray(plane_block()), jnp.asarray(kron_block())
    tile = ("y", "core")
    vs = [valence_waves] + [None] * (VB - 1)
    for m in range(1, VB // 2):
        vs[m] = shift(vs[m - 1], "z", NZ, 1)
        vs[VB - m] = shift(vs[(VB - m + 1) % VB], "z", NZ, -1)
    vs[VB // 2] = shift(vs[2], "z", NZ, 2)
    specs = [spectra([vs[k] for k in slots], cs, depth, plane) for slots in SLOTS]
    slabs = [lax.all_to_all(specs[0], tile, split_axis=0, concat_axis=0, tiled=True)]
    slabs[0], specs[1] = lax.optimization_barrier((slabs[0], specs[1]))
    slabs.append(lax.all_to_all(specs[1], tile, split_axis=0, concat_axis=0, tiled=True))

    valence_level = pick_levels(valence_pick, valence_energy)
    band_level = pick_levels(cond_pick, conduction_energy)
    slot_codes = jnp.arange(NC, dtype=jnp.int32)
    slot_level = jnp.sum(
        jnp.where(cond_slot[:, None] == slot_codes[None, :], band_level[:, None], 0.0), axis=0
    )
    factor = 4.0 / math.sqrt(NV * NC)
    xs, zs, ts, c, ms, bs = np.ix_(*(np.arange(n) for n in (NX, NZ, NT, 2, 2, 2)))
    v_of = VB * xs + (zs - np.array(SLOTS)[c, ts // 2]) % NZ
    s_of = 2 * NZ * ((xs - np.array(XORDER)[2 * (ts % 2) + ms]) % NX) + 2 * zs + bs
    v_of, s_of = (np.broadcast_to(m, (NX, NZ, NT, 2, 2, 2)).reshape(NV * NC, 1) for m in (v_of, s_of))
    weight = factor / (spread(valence_level, v_of) - spread(slot_level, s_of))

    index = jnp.pad(g_index.reshape(32, 375), ((0, 0), (0, RB - 375))).reshape(1, GP)
    a_code = index // (KEPT * HALF)
    rest = index % (KEPT * HALF)
    b_code = (rest % HALF) * KEPT + rest // HALF
    a_code = a_code + AEI * (b_code // CODES)
    b_code = b_code % CODES

    first = pick_first(lines(slabs[0].reshape(GRID * QC, YL), kron), a_code, b_code)
    cols, for_rows = pick_second(lines(slabs[1].reshape(GRID * QC, YL), kron), a_code, b_code, first)
    cols = lax.all_to_all(cols, tile, split_axis=0, concat_axis=0, tiled=True).reshape(KP, 4 * RB)
    b_bundle = lax.all_gather(cols[:, LA:], "z", axis=0, tiled=True)
    near, far = ring(cols[:, :LA], "x", NX)
    a_bundle = jnp.concatenate(near + far, axis=0)
    a_up, a_down = shift(a_bundle, "z", NZ, 1), shift(a_bundle, "z", NZ, -1)
    for_rows, a_up, a_down = lax.optimization_barrier((for_rows, a_up, a_down))
    a_cols, a_far = ring_on(a_bundle, a_up, a_down, "z", NZ)
    b_cols, b_far = ring(b_bundle, "x", NX)
    rows = lax.all_to_all(for_rows, ("x", "z"), split_axis=0, concat_axis=0, tiled=True)
    rows = lax.all_gather(rows, ("y", "core"), axis=0, tiled=False)
    place = jnp.stack([lax.axis_index("x"), lax.axis_index("z")]).astype(jnp.int32)
    return product(place, rows, weight, a_cols + a_far, b_cols + b_far)


def solution(mesh):
    fine = Mesh(mesh.devices.reshape(NX, NZ, NY, NCORE), ("x", "z", "y", "core"))
    waves = P(("x", "z"), ("y", "core"), None)
    return jax.shard_map(
        per_device,
        mesh=fine,
        in_specs=(waves, waves, P(), P(), P(), P(), P(), P()),
        out_specs=P(("x", "z"), ("y", "core")),
        check_vma=False,
    )
```

```python
import functools
import math

import jax
import jax.numpy as jnp
import ml_dtypes
import numpy as np
from jax import lax
from jax.experimental import pallas as pl
from jax.experimental.pallas import tpu as pltpu
from jax.sharding import Mesh, PartitionSpec as P

NV = 32
NC = 64
GRID = 96
KM = 18
NG = 12000
KEPT = 2 * KM + 1
HALF = KM + 1
NX, NZ, NY, NCORE = 4, 8, 4, 2
NT = NY * NCORE
SLAB = GRID // NT
VB = 8
SB = 8
VC = 4
QC = 4
SLOTS = ((0, 1, 7, 2), (6, 3, 5, 4))
ROWS = SLAB * VC * SB
ZGRP = 384
ZOUT = HALF * 8
YSTEP = 768
NSTEP = GRID * GRID // YSTEP
NCUT = 4
BTILE = 128
NBT = 5
KWIN = 5
YL = 1408
AEI = 2 * KEPT
RB = 384
GP = 32 * RB
GCH = 768
CODES = 256
NGRP = 3
BF = jnp.bfloat16
F32 = jnp.float32


def tables():
    pos = np.arange(GRID)
    scale = 1.0 / math.sqrt(GRID)

    def angles(freqs):
        turns = (np.mod(freqs, GRID)[None, :] * pos[:, None]) % GRID
        return turns.astype(np.float64) * (2.0 * math.pi / GRID)

    ad = angles(np.arange(HALF))
    depth = np.stack([np.cos(ad), -np.sin(ad)], axis=1) * scale
    ap = angles(np.arange(KEPT) - KM)
    c, s = np.cos(ap), np.sin(ap)
    plane = np.stack([np.stack([c, s]), np.stack([-s, c])], axis=2) * scale
    return depth, plane


def depth_block():
    depth, _ = tables()
    out = np.zeros((4, GRID, HALF, 2, 4), np.float64)
    for y in range(4):
        out[y, :, :, :, y] = depth.transpose(0, 2, 1)
    return out.reshape(ZGRP, ZOUT).astype(ml_dtypes.bfloat16)


def window(n):
    first = BTILE * n // KEPT
    return first, min((BTILE * n + BTILE - 1) // KEPT, HALF - 1) + 1 - first


def plane_block():
    _, plane = tables()
    perk = plane.reshape(2, GRID // 4, 4, 2, KEPT).transpose(3, 4, 1, 0, 2).reshape(2, KEPT, 2 * GRID)
    out = np.zeros((YL, KWIN, 2 * GRID), np.float64)
    for d in range(2):
        for b in range(KEPT * HALF):
            k, j = divmod(b, KEPT)
            n, r = divmod(b, BTILE)
            row = n * 2 * BTILE + d * (BTILE if n < NBT else 64) + r
            out[row, k - window(n)[0]] = perk[d, j]
    return out.reshape(YL, KWIN * 2 * GRID).astype(ml_dtypes.bfloat16)


def kron_block():
    _, plane = tables()
    out = np.zeros((2, AEI, QC, NT, QC * SLAB), np.float64)
    slabs = plane.reshape(2, NT, SLAB, AEI).transpose(0, 3, 1, 2)
    for q in range(QC):
        out[:, :, q, :, 8 * q : 8 * q + 8] = slabs[..., :8]
        out[:, :, q, :, 8 * QC + 4 * q : 8 * QC + 4 * q + 4] = slabs[..., 8:]
    return out.reshape(2, AEI * QC, GRID * QC).astype(ml_dtypes.bfloat16)


def copy_in(refs, spaces, sems):
    copies = [pltpu.make_async_copy(ref, space, sems.at[i]) for i, (ref, space) in enumerate(zip(refs, spaces))]
    for copy in copies:
        copy.start()
    return copies


def spectra_kernel(*refs):
    n = VC + NX + 3
    o_ref, dens, zs, sems = refs[n], *refs[2 * n + 1 :]
    spaces = refs[n + 1 : 2 * n + 1]
    v_refs, c_refs, (t_ref, w_ref) = spaces[:VC], spaces[VC : n - 2], spaces[n - 2 :]
    tables = copy_in(refs[n - 2 : n], spaces[n - 2 :], sems.at[NCUT])
    cuts = []
    for cut in range(NCUT):
        lanes = pl.ds(cut * (GRID * GRID // NCUT), GRID * GRID // NCUT)
        cuts.append(copy_in([r.at[:, :, lanes] for r in refs[: n - 2]], [r.at[:, :, lanes] for r in spaces[: n - 2]], sems.at[cut]))
    tables[0].wait()

    def body(step, _):
        lanes = pl.ds(pl.multiple_of(step * YSTEP, YSTEP), YSTEP)

        def parts(ref, b):
            wave = ref[b, :, lanes].astype(F32)
            return wave[:8], wave[8:]

        def tile(pieces):
            heads = [head for head, _ in pieces]
            tails = [jnp.concatenate([pieces[i][1], pieces[i + 1][1]], axis=0) for i in range(0, QC, 2)]
            return jnp.concatenate(heads + tails, axis=0).astype(BF)

        bands = [(c_refs[m], b) for m in range(3) for b in range(2)] + [(c_refs[3], 0), (c_refs[4], 0)]
        cond = [tile([parts(ref, b) for ref, b in bands[QC * h : QC * (h + 1)]]) for h in range(2)]
        for v in range(VC):
            val = tile([parts(v_refs[v], 0)] * QC)
            for h in range(2):
                r0 = (v * 2 + h) * SLAB * QC
                dens[r0 : r0 + SLAB * QC, :] = val * cond[h]
        groups = []
        for sub in range(YSTEP // ZGRP):
            z = jnp.dot(dens[:, sub * ZGRP : (sub + 1) * ZGRP], t_ref[...], preferred_element_type=F32)
            groups.append(z.T.reshape(HALF, 8, ROWS))
        zs[:, pl.ds(pl.multiple_of(step * 16, 16), 16), :] = jnp.concatenate(groups, axis=1).astype(BF)
        return 0

    for cut in range(NCUT):
        for copy in cuts[cut]:
            copy.wait()
        lax.fori_loop(cut * (NSTEP // NCUT), (cut + 1) * (NSTEP // NCUT), body, 0)
    tables[1].wait()
    for n in range(NBT + 1):
        r0 = n * 2 * BTILE
        rows = 2 * BTILE if n < NBT else BTILE
        k0, width = window(n)
        zk = zs[k0 : k0 + width].reshape(width * 2 * GRID, ROWS)
        y = jnp.dot(w_ref[r0 : r0 + rows, : width * 2 * GRID], zk, preferred_element_type=F32)
        yt = y.T.astype(BF).reshape(NT, SLAB * QC, rows)
        if n < NBT - 1:
            l0 = n // 2 * 512 + n % 2 * BTILE
            o_ref[:, :, l0 : l0 + BTILE] = yt[:, :, :BTILE]
            o_ref[:, :, l0 + 256 : l0 + 256 + BTILE] = yt[:, :, BTILE:]
        else:
            o_ref[:, :, r0 : r0 + rows] = yt


def spectra(vs, cs, t, w):
    operands = [*vs, *cs, t, w]
    return pl.pallas_call(
        spectra_kernel,
        in_specs=[pl.BlockSpec(memory_space=pl.ANY)] * len(operands),
        out_specs=pl.BlockSpec(memory_space=pltpu.VMEM),
        out_shape=jax.ShapeDtypeStruct((NT, SLAB * QC, YL), BF),
        scratch_shapes=[pltpu.VMEM(x.shape, BF) for x in operands]
        + [
            pltpu.VMEM((ROWS, YSTEP), BF),
            pltpu.VMEM((HALF, 2 * GRID, ROWS), BF),
            pltpu.SemaphoreType.DMA((NCUT + 1, len(operands) - 2)),
        ],
        compiler_params=pltpu.CompilerParams(vmem_limit_bytes=58 * 2**20),
        name="spectra",
    )(*operands)


def lines_kernel(y_ref, m_ref, s_ref):
    rows = AEI * QC

    def line(d, lanes):
        return jnp.dot(m_ref[d], y_ref[:, lanes], preferred_element_type=F32)

    for g in range(2):
        s = line(0, pl.ds(512 * g, 256)) + line(1, pl.ds(512 * g + 256, 256))
        s_ref[g * rows : (g + 1) * rows, :] = s.astype(BF)
    s = line(0, pl.ds(1024, BTILE)) + line(1, pl.ds(1024 + BTILE, BTILE))
    s_ref[2 * rows :, :BTILE] = s.astype(BF)
    last = pl.ds(1024 + 2 * BTILE, BTILE)
    s = line(0, last) + pltpu.roll(line(1, last), 64, 1)
    s_ref[2 * rows :, BTILE:] = s.astype(BF)


def lines(y, m):
    return pl.pallas_call(
        lines_kernel,
        out_shape=jax.ShapeDtypeStruct((NGRP * AEI * QC, CODES), BF),
        compiler_params=pltpu.CompilerParams(vmem_limit_bytes=40 * 2**20),
        name="lines",
    )(y, m)


def picked(s_ref, a_ref, b_ref, chunk):
    codes = lax.broadcasted_iota(jnp.int32, (CODES, CODES), 0)
    row = lax.broadcasted_iota(jnp.int32, (SB, CODES), 0)
    outs = []
    for g in range(GCH // CODES):
        lanes = pl.ds(g * CODES, CODES)
        chosen = (codes == b_ref[:, lanes]).astype(F32).astype(BF)
        r = jnp.dot(s_ref[...], chosen, preferred_element_type=F32)
        code = a_ref[:, lanes] - row // QC
        acc = jnp.zeros((SB, CODES), F32)
        for a in range(0, NGRP * AEI, 2):
            acc = jnp.where(code == a, r[a * QC : (a + 2) * QC], acc)
        both = acc + pltpu.roll(acc, QC, 0)
        outs.append(jnp.where(row // QC == chunk, both, 0.0))
    return jnp.concatenate(outs, axis=1)


def first_kernel(s_ref, a_ref, b_ref, o_ref):
    o_ref[...] = picked(s_ref, a_ref, b_ref, 0)


def second_kernel(s_ref, a_ref, b_ref, first_ref, oc_ref, or_ref):
    out = (first_ref[...] + picked(s_ref, a_ref, b_ref, 1)).astype(BF)
    oc_ref[0] = out
    for h in range(GCH // RB):
        or_ref[h] = out[:, h * RB : (h + 1) * RB]


def pick_specs():
    return [
        pl.BlockSpec((NGRP * AEI * QC, CODES), lambda i: (0, 0)),
        pl.BlockSpec((1, GCH), lambda i: (0, i)),
        pl.BlockSpec((1, GCH), lambda i: (0, i)),
    ]


def pick_first(s, a, b):
    return pl.pallas_call(
        first_kernel,
        grid=(GP // GCH,),
        in_specs=pick_specs(),
        out_specs=pl.BlockSpec((SB, GCH), lambda i: (0, i)),
        out_shape=jax.ShapeDtypeStruct((SB, GP), F32),
        compiler_params=pltpu.CompilerParams(vmem_limit_bytes=40 * 2**20),
        name="pick_first",
    )(s, a, b)


def pick_second(s, a, b, first):
    per = 4 * RB // GCH
    return pl.pallas_call(
        second_kernel,
        grid=(GP // GCH,),
        in_specs=pick_specs() + [pl.BlockSpec((SB, GCH), lambda i: (0, i))],
        out_specs=[
            pl.BlockSpec((1, SB, GCH), lambda i: (i // per, 0, i % per)),
            pl.BlockSpec((GCH // RB, SB, RB), lambda i: (i, 0, 0)),
        ],
        out_shape=[
            jax.ShapeDtypeStruct((NT, SB, 4 * RB), BF),
            jax.ShapeDtypeStruct((32, SB, RB), BF),
        ],
        compiler_params=pltpu.CompilerParams(vmem_limit_bytes=40 * 2**20),
        name="pick_second",
    )(s, a, b, first)


KP = NT * SB
LA = 512
XORDER = (0, 1, 3, 2)
ZORDER = (0, 1, 2, 3, 7, 6, 5, 4)


def a_pieces():
    whole = [[(x, z) for x in XORDER] for z in ZORDER[:-1]]
    return whole + [[(x, 4) for x in XORDER[:2]], [(x, 4) for x in XORDER[2:]]]


def b_pieces():
    whole = [[(x, z) for z in range(NZ)] for x in XORDER[:-1]]
    return whole + [[(2, z) for z in range(NZ // 2)], [(2, z) for z in range(NZ // 2, NZ)]]


def product_kernel(xz_ref, w_ref, *refs):
    na, nb = len(a_pieces()), len(b_pieces())
    n = 1 + na + nb
    o_ref, spaces, (wr, acc_ref, sems) = refs[n], refs[n + 1 : 2 * n + 1], refs[2 * n + 1 :]
    copies = copy_in(refs[:n], spaces, sems)
    r_ref, a_refs, b_refs = spaces[0], spaces[1 : 1 + na], spaces[1 + na :]
    copies[0].wait()
    for p in range(32):
        rows = jnp.concatenate([r_ref[t, p].astype(F32) for t in range(NT)], axis=0)
        wr[p] = (rows * w_ref[KP * p : KP * (p + 1), :]).astype(BF)

    def part(pieces, ref, z_of):
        lhs = [wr[lax.rem(xz_ref[0] + (NX - dx), NX) * NZ + z_of(dz)] for dx, dz in pieces]
        return lax.dot_general(
            jnp.concatenate(lhs, axis=0), ref[...], (((0,), (0,)), ((), ())), preferred_element_type=F32
        )

    def total(pieces, operands, waits, z_of):
        acc = None
        for piece, ref, copy in zip(pieces, operands, waits):
            copy.wait()
            more = part(piece, ref, z_of)
            acc = more if acc is None else acc + more
        return acc

    acc_ref[:, :LA] = total(a_pieces(), a_refs, copies[1 : 1 + na], lambda dz: lax.rem(xz_ref[1] + (NZ - dz), NZ))
    acc_ref[:, LA:] = total(b_pieces(), b_refs, copies[1 + na :], lambda z: z)
    for q in range(4):
        o_ref[:, 375 * q : 375 * (q + 1)] = acc_ref[:375, RB * q : RB * q + 375]


def product(place, rows, weight, a_cols, b_cols):
    operands = [rows, *a_cols, *b_cols]
    vmem = pl.BlockSpec(memory_space=pltpu.VMEM)
    return pl.pallas_call(
        product_kernel,
        in_specs=[pl.BlockSpec(memory_space=pltpu.SMEM), vmem] + [pl.BlockSpec(memory_space=pl.ANY)] * len(operands),
        out_specs=vmem,
        out_shape=jax.ShapeDtypeStruct((375, 1500), F32),
        scratch_shapes=[pltpu.VMEM(x.shape, BF) for x in operands]
        + [
            pltpu.VMEM((32, KP, RB), BF),
            pltpu.VMEM((RB, 4 * RB), F32),
            pltpu.SemaphoreType.DMA((len(operands),)),
        ],
        compiler_params=pltpu.CompilerParams(vmem_limit_bytes=58 * 2**20),
        name="product",
    )(place, weight, *operands)


def ring(value, axis, size):
    return ring_on(value, shift(value, axis, size, 1), shift(value, axis, size, -1), axis, size)


def ring_on(value, up, down, axis, size):
    ups, downs = [up], [down]
    for _ in range(size // 2 - 2):
        ups.append(shift(ups[-1], axis, size, 1))
        downs.append(shift(downs[-1], axis, size, -1))
    half = value.shape[0] // 2
    far = [shift(ups[-1][:half], axis, size, 1), shift(downs[-1][half:], axis, size, -1)]
    return [value] + ups + downs, far


def pick_levels(picks, table):
    codes = jnp.arange(table.shape[0], dtype=jnp.int32)
    return jnp.sum(jnp.where(picks[:, None] == codes[None, :], table[None, :], 0.0), axis=1)


def spread(levels, places):
    codes = jnp.arange(levels.shape[0], dtype=jnp.int32)[None, :]
    return jnp.sum(jnp.where(codes == places.astype(np.int32), levels[None, :], 0.0), axis=1, keepdims=True)


def shift(value, axis, size, step):
    return lax.ppermute(value, axis, [(i, (i + step) % size) for i in range(size)])


def per_device(
    valence_waves,
    cond_waves,
    valence_energy,
    conduction_energy,
    valence_pick,
    cond_pick,
    cond_slot,
    g_index,
):
    cs, far = ring(cond_waves, "x", NX)
    cs += far
    depth, plane, kron = jnp.asarray(depth_block()), jnp.asarray(plane_block()), jnp.asarray(kron_block())
    tile = ("y", "core")
    vs = [valence_waves] + [None] * (VB - 1)
    for m in range(1, VB // 2):
        vs[m] = shift(vs[m - 1], "z", NZ, 1)
        vs[VB - m] = shift(vs[(VB - m + 1) % VB], "z", NZ, -1)
    vs[VB // 2] = shift(vs[2], "z", NZ, 2)
    specs = [spectra([vs[k] for k in slots], cs, depth, plane) for slots in SLOTS]
    slabs = [lax.all_to_all(specs[0], tile, split_axis=0, concat_axis=0, tiled=True)]
    slabs[0], specs[1] = lax.optimization_barrier((slabs[0], specs[1]))
    slabs.append(lax.all_to_all(specs[1], tile, split_axis=0, concat_axis=0, tiled=True))

    valence_level = pick_levels(valence_pick, valence_energy)
    band_level = pick_levels(cond_pick, conduction_energy)
    slot_codes = jnp.arange(NC, dtype=jnp.int32)
    slot_level = jnp.sum(
        jnp.where(cond_slot[:, None] == slot_codes[None, :], band_level[:, None], 0.0), axis=0
    )
    factor = 4.0 / math.sqrt(NV * NC)
    xs, zs, ts, c, ms, bs = np.ix_(*(np.arange(n) for n in (NX, NZ, NT, 2, 2, 2)))
    v_of = VB * xs + (zs - np.array(SLOTS)[c, ts // 2]) % NZ
    s_of = 2 * NZ * ((xs - np.array(XORDER)[2 * (ts % 2) + ms]) % NX) + 2 * zs + bs
    v_of, s_of = (np.broadcast_to(m, (NX, NZ, NT, 2, 2, 2)).reshape(NV * NC, 1) for m in (v_of, s_of))
    weight = factor / (spread(valence_level, v_of) - spread(slot_level, s_of))

    index = jnp.pad(g_index.reshape(32, 375), ((0, 0), (0, RB - 375))).reshape(1, GP)
    a_code = index // (KEPT * HALF)
    rest = index % (KEPT * HALF)
    b_code = (rest % HALF) * KEPT + rest // HALF
    a_code = a_code + AEI * (b_code // CODES)
    b_code = b_code % CODES

    first = pick_first(lines(slabs[0].reshape(GRID * QC, YL), kron), a_code, b_code)
    cols, for_rows = pick_second(lines(slabs[1].reshape(GRID * QC, YL), kron), a_code, b_code, first)
    cols = lax.all_to_all(cols, tile, split_axis=0, concat_axis=0, tiled=True).reshape(KP, 4 * RB)
    b_bundle = lax.all_gather(cols[:, LA:], "z", axis=0, tiled=True)
    near, far = ring(cols[:, :LA], "x", NX)
    a_bundle = jnp.concatenate(near + far, axis=0)
    a_up, a_down = shift(a_bundle, "z", NZ, 1), shift(a_bundle, "z", NZ, -1)
    for_rows, a_up, a_down = lax.optimization_barrier((for_rows, a_up, a_down))
    a_cols, a_far = ring_on(a_bundle, a_up, a_down, "z", NZ)
    b_cols, b_far = ring(b_bundle, "x", NX)
    rows = lax.all_to_all(for_rows, ("x", "z"), split_axis=0, concat_axis=0, tiled=True)
    rows = lax.all_gather(rows, ("y", "core"), axis=0, tiled=False)
    place = jnp.stack([lax.axis_index("x"), lax.axis_index("z")]).astype(jnp.int32)
    return product(place, rows, weight, a_cols + a_far, b_cols + b_far)


def solution(mesh):
    fine = Mesh(mesh.devices.reshape(NX, NZ, NY, NCORE), ("x", "z", "y", "core"))
    waves = P(("x", "z"), ("y", "core"), None)
    return jax.shard_map(
        per_device,
        mesh=fine,
        in_specs=(waves, waves, P(), P(), P(), P(), P(), P()),
        out_specs=P(("x", "z"), ("y", "core")),
        check_vma=False,
    )
```

```python
import functools
import math

import jax
import jax.numpy as jnp
import ml_dtypes
import numpy as np
from jax import lax
from jax.experimental import pallas as pl
from jax.experimental.pallas import tpu as pltpu
from jax.sharding import Mesh, PartitionSpec as P

NV = 32
NC = 64
GRID = 96
KM = 18
NG = 12000
KEPT = 2 * KM + 1
HALF = KM + 1
NX, NZ, NY, NCORE = 4, 8, 4, 2
NT = NY * NCORE
SLAB = GRID // NT
VB = 8
SB = 8
VC = 4
QC = 4
SLOTS = ((0, 1, 7, 2), (6, 3, 5, 4))
ROWS = SLAB * VC * SB
ZGRP = 384
ZOUT = HALF * 8
YSTEP = 768
NSTEP = GRID * GRID // YSTEP
NCUT = 4
BTILE = 128
NBT = 5
KWIN = 5
YL = 1408
AEI = 2 * KEPT
RB = 384
GP = 32 * RB
GCH = 768
CODES = 256
NGRP = 3
BF = jnp.bfloat16
F32 = jnp.float32


def tables():
    pos = np.arange(GRID)
    scale = 1.0 / math.sqrt(GRID)

    def angles(freqs):
        turns = (np.mod(freqs, GRID)[None, :] * pos[:, None]) % GRID
        return turns.astype(np.float64) * (2.0 * math.pi / GRID)

    ad = angles(np.arange(HALF))
    depth = np.stack([np.cos(ad), -np.sin(ad)], axis=1) * scale
    ap = angles(np.arange(KEPT) - KM)
    c, s = np.cos(ap), np.sin(ap)
    plane = np.stack([np.stack([c, s]), np.stack([-s, c])], axis=2) * scale
    return depth, plane


def depth_block():
    depth, _ = tables()
    out = np.zeros((4, GRID, HALF, 2, 4), np.float64)
    for y in range(4):
        out[y, :, :, :, y] = depth.transpose(0, 2, 1)
    return out.reshape(ZGRP, ZOUT).astype(ml_dtypes.bfloat16)


def window(n):
    first = BTILE * n // KEPT
    return first, min((BTILE * n + BTILE - 1) // KEPT, HALF - 1) + 1 - first


def plane_block():
    _, plane = tables()
    perk = plane.reshape(2, GRID // 4, 4, 2, KEPT).transpose(3, 4, 1, 0, 2).reshape(2, KEPT, 2 * GRID)
    out = np.zeros((YL, KWIN, 2 * GRID), np.float64)
    for d in range(2):
        for b in range(KEPT * HALF):
            k, j = divmod(b, KEPT)
            n, r = divmod(b, BTILE)
            row = n * 2 * BTILE + d * (BTILE if n < NBT else 64) + r
            out[row, k - window(n)[0]] = perk[d, j]
    return out.reshape(YL, KWIN * 2 * GRID).astype(ml_dtypes.bfloat16)


def kron_block():
    _, plane = tables()
    out = np.zeros((2, AEI, QC, NT, QC * SLAB), np.float64)
    slabs = plane.reshape(2, NT, SLAB, AEI).transpose(0, 3, 1, 2)
    for q in range(QC):
        out[:, :, q, :, 8 * q : 8 * q + 8] = slabs[..., :8]
        out[:, :, q, :, 8 * QC + 4 * q : 8 * QC + 4 * q + 4] = slabs[..., 8:]
    return out.reshape(2, AEI * QC, GRID * QC).astype(ml_dtypes.bfloat16)


def copy_in(refs, spaces, sems):
    copies = [pltpu.make_async_copy(ref, space, sems.at[i]) for i, (ref, space) in enumerate(zip(refs, spaces))]
    for copy in copies:
        copy.start()
    return copies


def spectra_kernel(*refs):
    n = VC + NX + 3
    o_ref, dens, zs, sems = refs[n], *refs[2 * n + 1 :]
    spaces = refs[n + 1 : 2 * n + 1]
    v_refs, c_refs, (t_ref, w_ref) = spaces[:VC], spaces[VC : n - 2], spaces[n - 2 :]
    tables = copy_in(refs[n - 2 : n], spaces[n - 2 :], sems.at[NCUT])
    cuts = []
    for cut in range(NCUT):
        lanes = pl.ds(cut * (GRID * GRID // NCUT), GRID * GRID // NCUT)
        cuts.append(copy_in([r.at[:, :, lanes] for r in refs[: n - 2]], [r.at[:, :, lanes] for r in spaces[: n - 2]], sems.at[cut]))
    tables[0].wait()

    def body(step, _):
        lanes = pl.ds(pl.multiple_of(step * YSTEP, YSTEP), YSTEP)

        def parts(ref, b):
            wave = ref[b, :, lanes].astype(F32)
            return wave[:8], wave[8:]

        def tile(pieces):
            heads = [head for head, _ in pieces]
            tails = [jnp.concatenate([pieces[i][1], pieces[i + 1][1]], axis=0) for i in range(0, QC, 2)]
            return jnp.concatenate(heads + tails, axis=0).astype(BF)

        bands = [(c_refs[m], b) for m in range(3) for b in range(2)] + [(c_refs[3], 0), (c_refs[4], 0)]
        cond = [tile([parts(ref, b) for ref, b in bands[QC * h : QC * (h + 1)]]) for h in range(2)]
        for v in range(VC):
            val = tile([parts(v_refs[v], 0)] * QC)
            for h in range(2):
                r0 = (v * 2 + h) * SLAB * QC
                dens[r0 : r0 + SLAB * QC, :] = val * cond[h]
        groups = []
        for sub in range(YSTEP // ZGRP):
            z = jnp.dot(dens[:, sub * ZGRP : (sub + 1) * ZGRP], t_ref[...], preferred_element_type=F32)
            groups.append(z.T.reshape(HALF, 8, ROWS))
        zs[:, pl.ds(pl.multiple_of(step * 16, 16), 16), :] = jnp.concatenate(groups, axis=1).astype(BF)
        return 0

    for cut in range(NCUT):
        for copy in cuts[cut]:
            copy.wait()
        lax.fori_loop(cut * (NSTEP // NCUT), (cut + 1) * (NSTEP // NCUT), body, 0)
    tables[1].wait()
    for n in range(NBT + 1):
        r0 = n * 2 * BTILE
        rows = 2 * BTILE if n < NBT else BTILE
        k0, width = window(n)
        zk = zs[k0 : k0 + width].reshape(width * 2 * GRID, ROWS)
        y = jnp.dot(w_ref[r0 : r0 + rows, : width * 2 * GRID], zk, preferred_element_type=F32)
        yt = y.T.astype(BF).reshape(NT, SLAB * QC, rows)
        if n < NBT - 1:
            l0 = n // 2 * 512 + n % 2 * BTILE
            o_ref[:, :, l0 : l0 + BTILE] = yt[:, :, :BTILE]
            o_ref[:, :, l0 + 256 : l0 + 256 + BTILE] = yt[:, :, BTILE:]
        else:
            o_ref[:, :, r0 : r0 + rows] = yt


def spectra(vs, cs, t, w):
    operands = [*vs, *cs, t, w]
    return pl.pallas_call(
        spectra_kernel,
        in_specs=[pl.BlockSpec(memory_space=pl.ANY)] * len(operands),
        out_specs=pl.BlockSpec(memory_space=pltpu.VMEM),
        out_shape=jax.ShapeDtypeStruct((NT, SLAB * QC, YL), BF),
        scratch_shapes=[pltpu.VMEM(x.shape, BF) for x in operands]
        + [
            pltpu.VMEM((ROWS, YSTEP), BF),
            pltpu.VMEM((HALF, 2 * GRID, ROWS), BF),
            pltpu.SemaphoreType.DMA((NCUT + 1, len(operands) - 2)),
        ],
        compiler_params=pltpu.CompilerParams(vmem_limit_bytes=58 * 2**20),
        name="spectra",
    )(*operands)


def lines_kernel(y_ref, m_ref, s_ref):
    rows = AEI * QC

    def line(d, lanes):
        return jnp.dot(m_ref[d], y_ref[:, lanes], preferred_element_type=F32)

    for g in range(2):
        s = line(0, pl.ds(512 * g, 256)) + line(1, pl.ds(512 * g + 256, 256))
        s_ref[g * rows : (g + 1) * rows, :] = s.astype(BF)
    s = line(0, pl.ds(1024, BTILE)) + line(1, pl.ds(1024 + BTILE, BTILE))
    s_ref[2 * rows :, :BTILE] = s.astype(BF)
    last = pl.ds(1024 + 2 * BTILE, BTILE)
    s = line(0, last) + pltpu.roll(line(1, last), 64, 1)
    s_ref[2 * rows :, BTILE:] = s.astype(BF)


def lines(y, m):
    return pl.pallas_call(
        lines_kernel,
        out_shape=jax.ShapeDtypeStruct((NGRP * AEI * QC, CODES), BF),
        compiler_params=pltpu.CompilerParams(vmem_limit_bytes=40 * 2**20),
        name="lines",
    )(y, m)


def picked(s_ref, a_ref, b_ref, chunk):
    codes = lax.broadcasted_iota(jnp.int32, (CODES, CODES), 0)
    row = lax.broadcasted_iota(jnp.int32, (SB, CODES), 0)
    outs = []
    for g in range(GCH // CODES):
        lanes = pl.ds(g * CODES, CODES)
        chosen = (codes == b_ref[:, lanes]).astype(F32).astype(BF)
        r = jnp.dot(s_ref[...], chosen, preferred_element_type=F32)
        code = a_ref[:, lanes] - row // QC
        acc = jnp.zeros((SB, CODES), F32)
        for a in range(0, NGRP * AEI, 2):
            acc = jnp.where(code == a, r[a * QC : (a + 2) * QC], acc)
        both = acc + pltpu.roll(acc, QC, 0)
        outs.append(jnp.where(row // QC == chunk, both, 0.0))
    return jnp.concatenate(outs, axis=1)


def first_kernel(s_ref, a_ref, b_ref, o_ref):
    o_ref[...] = picked(s_ref, a_ref, b_ref, 0)


def second_kernel(s_ref, a_ref, b_ref, first_ref, oc_ref, or_ref):
    out = (first_ref[...] + picked(s_ref, a_ref, b_ref, 1)).astype(BF)
    oc_ref[0] = out
    for h in range(GCH // RB):
        or_ref[h] = out[:, h * RB : (h + 1) * RB]


def pick_specs():
    return [
        pl.BlockSpec((NGRP * AEI * QC, CODES), lambda i: (0, 0)),
        pl.BlockSpec((1, GCH), lambda i: (0, i)),
        pl.BlockSpec((1, GCH), lambda i: (0, i)),
    ]


def pick_first(s, a, b):
    return pl.pallas_call(
        first_kernel,
        grid=(GP // GCH,),
        in_specs=pick_specs(),
        out_specs=pl.BlockSpec((SB, GCH), lambda i: (0, i)),
        out_shape=jax.ShapeDtypeStruct((SB, GP), F32),
        compiler_params=pltpu.CompilerParams(vmem_limit_bytes=40 * 2**20),
        name="pick_first",
    )(s, a, b)


def pick_second(s, a, b, first):
    per = 4 * RB // GCH
    return pl.pallas_call(
        second_kernel,
        grid=(GP // GCH,),
        in_specs=pick_specs() + [pl.BlockSpec((SB, GCH), lambda i: (0, i))],
        out_specs=[
            pl.BlockSpec((1, SB, GCH), lambda i: (i // per, 0, i % per)),
            pl.BlockSpec((GCH // RB, SB, RB), lambda i: (i, 0, 0)),
        ],
        out_shape=[
            jax.ShapeDtypeStruct((NT, SB, 4 * RB), BF),
            jax.ShapeDtypeStruct((32, SB, RB), BF),
        ],
        compiler_params=pltpu.CompilerParams(vmem_limit_bytes=40 * 2**20),
        name="pick_second",
    )(s, a, b, first)


KP = NT * SB
LA = 640
LB = 4 * RB - LA
LG = 1024
XORDER = (0, 1, 3, 2)
ZORDER = (0, 1, 2, 3, 7, 6, 5, 4)


def a_pieces():
    whole = [[(x, z) for x in XORDER] for z in ZORDER[:-1]]
    return whole + [[(x, 4) for x in XORDER[:2]], [(x, 4) for x in XORDER[2:]]]


def b_pieces():
    whole = [[(x, z) for z in range(NZ)] for x in XORDER[:-1]]
    return whole + [[(2, z) for z in range(NZ // 2)], [(2, z) for z in range(NZ // 2, NZ)]]


def weigh_kernel(xz_ref, r_ref, w_ref, a_ref, b_ref):
    def rows(x, z):
        owner = x * NZ + z
        block = jnp.concatenate([r_ref[t, owner].astype(F32) for t in range(NT)], axis=0)
        return block * w_ref[owner]

    def x_at(dx):
        return lax.rem(xz_ref[0] + (NX - dx), NX)

    def z_at(dz):
        return lax.rem(xz_ref[1] + (NZ - dz), NZ)

    a_blocks = [(x_at(dx), z_at(dz)) for piece in a_pieces() for dx, dz in piece]
    b_blocks = [(x_at(dx), z) for piece in b_pieces() for dx, z in piece]
    for blocks, ref in ((a_blocks, a_ref), (b_blocks, b_ref)):
        for i in range(0, 32, 2):
            both = jnp.concatenate([rows(*blocks[i]), rows(*blocks[i + 1])], axis=0)
            ref[:, i * KP : (i + 2) * KP] = both.T.astype(BF)


def weigh(place, rows, weight):
    vmem = pl.BlockSpec(memory_space=pltpu.VMEM)
    return pl.pallas_call(
        weigh_kernel,
        in_specs=[pl.BlockSpec(memory_space=pltpu.SMEM), vmem, vmem],
        out_specs=[vmem, vmem],
        out_shape=[jax.ShapeDtypeStruct((RB, NV * NC), BF)] * 2,
        compiler_params=pltpu.CompilerParams(vmem_limit_bytes=40 * 2**20),
        name="weigh",
    )(place, rows, weight)


def product_kernel(*refs):
    na, nb = len(a_pieces()), len(b_pieces())
    n = 2 + na + nb
    o_ref, spaces, (acc_ref, sems) = refs[n], refs[n + 1 : 2 * n + 1], refs[2 * n + 1 :]
    copies = copy_in(refs[:n], spaces, sems)

    def total(lhs, operands, waits):
        acc, first = None, 0
        for ref, copy in zip(operands, waits):
            copy.wait()
            more = jnp.dot(lhs[:, first : first + ref.shape[0]], ref[...], preferred_element_type=F32)
            acc = more if acc is None else acc + more
            first += ref.shape[0]
        return acc

    copies[0].wait()
    copies[1].wait()
    acc_ref[:, :LA] = total(spaces[0], spaces[2 : 2 + na], copies[2 : 2 + na])
    acc_ref[:, LA:] = total(spaces[1], spaces[2 + na :], copies[2 + na :])
    for q in range(4):
        o_ref[:, 375 * q : 375 * (q + 1)] = acc_ref[:375, RB * q : RB * q + 375]


def product(a_rows, b_rows, a_cols, b_cols):
    operands = [a_rows, b_rows, *a_cols, *b_cols]
    return pl.pallas_call(
        product_kernel,
        in_specs=[pl.BlockSpec(memory_space=pl.ANY)] * len(operands),
        out_specs=pl.BlockSpec(memory_space=pltpu.VMEM),
        out_shape=jax.ShapeDtypeStruct((375, 1500), F32),
        scratch_shapes=[pltpu.VMEM(x.shape, BF) for x in operands]
        + [pltpu.VMEM((RB, 4 * RB), F32), pltpu.SemaphoreType.DMA((len(operands),))],
        compiler_params=pltpu.CompilerParams(vmem_limit_bytes=58 * 2**20),
        name="product",
    )(*operands)


def ring(value, axis, size):
    return ring_on(value, shift(value, axis, size, 1), shift(value, axis, size, -1), axis, size)


def ring_on(value, up, down, axis, size):
    ups, downs = [up], [down]
    for _ in range(size // 2 - 2):
        ups.append(shift(ups[-1], axis, size, 1))
        downs.append(shift(downs[-1], axis, size, -1))
    half = value.shape[0] // 2
    far = [shift(ups[-1][:half], axis, size, 1), shift(downs[-1][half:], axis, size, -1)]
    return [value] + ups + downs, far


def pick_levels(picks, table):
    codes = jnp.arange(table.shape[0], dtype=jnp.int32)
    return jnp.sum(jnp.where(picks[:, None] == codes[None, :], table[None, :], 0.0), axis=1)


def spread(levels, places):
    codes = jnp.arange(levels.shape[0], dtype=jnp.int32)[None, :]
    return jnp.sum(jnp.where(codes == places.astype(np.int32), levels[None, :], 0.0), axis=1, keepdims=True)


def shift(value, axis, size, step):
    return lax.ppermute(value, axis, [(i, (i + step) % size) for i in range(size)])


def per_device(
    valence_waves,
    cond_waves,
    valence_energy,
    conduction_energy,
    valence_pick,
    cond_pick,
    cond_slot,
    g_index,
):
    cs, far = ring(cond_waves, "x", NX)
    cs += far
    depth, plane, kron = jnp.asarray(depth_block()), jnp.asarray(plane_block()), jnp.asarray(kron_block())
    tile = ("y", "core")
    vs = [valence_waves] + [None] * (VB - 1)
    for m in range(1, VB // 2):
        vs[m] = shift(vs[m - 1], "z", NZ, 1)
        vs[VB - m] = shift(vs[(VB - m + 1) % VB], "z", NZ, -1)
    vs[VB // 2] = shift(vs[2], "z", NZ, 2)
    specs = [spectra([vs[k] for k in slots], cs, depth, plane) for slots in SLOTS]
    slabs = [lax.all_to_all(specs[0], tile, split_axis=0, concat_axis=0, tiled=True)]
    slabs[0], specs[1] = lax.optimization_barrier((slabs[0], specs[1]))
    slabs.append(lax.all_to_all(specs[1], tile, split_axis=0, concat_axis=0, tiled=True))

    valence_level = pick_levels(valence_pick, valence_energy)
    band_level = pick_levels(cond_pick, conduction_energy)
    slot_codes = jnp.arange(NC, dtype=jnp.int32)
    slot_level = jnp.sum(
        jnp.where(cond_slot[:, None] == slot_codes[None, :], band_level[:, None], 0.0), axis=0
    )
    factor = 4.0 / math.sqrt(NV * NC)
    xs, zs, ts, c, ms, bs = np.ix_(*(np.arange(n) for n in (NX, NZ, NT, 2, 2, 2)))
    v_of = VB * xs + (zs - np.array(SLOTS)[c, ts // 2]) % NZ
    s_of = 2 * NZ * ((xs - np.array(XORDER)[2 * (ts % 2) + ms]) % NX) + 2 * zs + bs
    v_of, s_of = (np.broadcast_to(m, (NX, NZ, NT, 2, 2, 2)).reshape(NV * NC, 1) for m in (v_of, s_of))
    weight = factor / (spread(valence_level, v_of) - spread(slot_level, s_of))

    index = jnp.pad(g_index.reshape(32, 375), ((0, 0), (0, RB - 375))).reshape(1, GP)
    a_code = index // (KEPT * HALF)
    rest = index % (KEPT * HALF)
    b_code = (rest % HALF) * KEPT + rest // HALF
    a_code = a_code + AEI * (b_code // CODES)
    b_code = b_code % CODES

    first = pick_first(lines(slabs[0].reshape(GRID * QC, YL), kron), a_code, b_code)
    cols, for_rows = pick_second(lines(slabs[1].reshape(GRID * QC, YL), kron), a_code, b_code, first)
    cols = lax.all_to_all(cols, tile, split_axis=0, concat_axis=0, tiled=True).reshape(KP, 4 * RB)
    b_part = jnp.concatenate([cols[:, LA:], cols[:, LA : LA + LG - LB]], axis=1)
    b_bundle = lax.all_gather(b_part, "z", axis=0, tiled=True)
    up, down = shift(cols[:, :LA], "x", NX, 1), shift(cols[:, :LA], "x", NX, -1)
    for_rows, up, down = lax.optimization_barrier((for_rows, up, down))
    near, far = ring_on(cols[:, :LA], up, down, "x", NX)
    a_bundle = jnp.concatenate(near + far, axis=0)
    a_bundle, b_bundle = lax.optimization_barrier((a_bundle, b_bundle))
    a_cols, a_far = ring(a_bundle, "z", NZ)
    b_cols, b_far = ring(b_bundle[:, :LB], "x", NX)
    rows = lax.all_to_all(for_rows, ("x", "z"), split_axis=0, concat_axis=0, tiled=True)
    rows = lax.all_gather(rows, tile, axis=0, tiled=False)
    place = jnp.stack([lax.axis_index("x"), lax.axis_index("z")]).astype(jnp.int32)
    a_rows, b_rows = weigh(place, rows, weight.reshape(32, KP, 1))
    return product(a_rows, b_rows, a_cols + a_far, b_cols + b_far)


def solution(mesh):
    fine = Mesh(mesh.devices.reshape(NX, NZ, NY, NCORE), ("x", "z", "y", "core"))
    waves = P(("x", "z"), ("y", "core"), None)
    return jax.shard_map(
        per_device,
        mesh=fine,
        in_specs=(waves, waves, P(), P(), P(), P(), P(), P()),
        out_specs=P(("x", "z"), ("y", "core")),
        check_vma=False,
    )
```

```python
import functools
import math

import jax
import jax.numpy as jnp
import ml_dtypes
import numpy as np
from jax import lax
from jax.experimental import pallas as pl
from jax.experimental.pallas import tpu as pltpu
from jax.sharding import Mesh, PartitionSpec as P

NV = 32
NC = 64
GRID = 96
KM = 18
NG = 12000
KEPT = 2 * KM + 1
HALF = KM + 1
NX, NZ, NY, NCORE = 4, 8, 4, 2
NT = NY * NCORE
SLAB = GRID // NT
VB = 8
SB = 8
VC = 4
QC = 4
SLOTS = ((0, 1, 7, 2), (6, 3, 5, 4))
ROWS = SLAB * VC * SB
ZGRP = 384
ZOUT = HALF * 8
YSTEP = 768
NSTEP = GRID * GRID // YSTEP
NCUT = 4
BTILE = 128
NBT = 5
KWIN = 5
YL = 1408
AEI = 2 * KEPT
RB = 384
GP = 32 * RB
GCH = 768
CODES = 256
NGRP = 3
BF = jnp.bfloat16
F32 = jnp.float32


def tables():
    pos = np.arange(GRID)
    scale = 1.0 / math.sqrt(GRID)

    def angles(freqs):
        turns = (np.mod(freqs, GRID)[None, :] * pos[:, None]) % GRID
        return turns.astype(np.float64) * (2.0 * math.pi / GRID)

    ad = angles(np.arange(HALF))
    depth = np.stack([np.cos(ad), -np.sin(ad)], axis=1) * scale
    ap = angles(np.arange(KEPT) - KM)
    c, s = np.cos(ap), np.sin(ap)
    plane = np.stack([np.stack([c, s]), np.stack([-s, c])], axis=2) * scale
    return depth, plane


def depth_block():
    depth, _ = tables()
    out = np.zeros((4, GRID, HALF, 2, 4), np.float64)
    for y in range(4):
        out[y, :, :, :, y] = depth.transpose(0, 2, 1)
    return out.reshape(ZGRP, ZOUT).astype(ml_dtypes.bfloat16)


def window(n):
    first = BTILE * n // KEPT
    return first, min((BTILE * n + BTILE - 1) // KEPT, HALF - 1) + 1 - first


def plane_block():
    _, plane = tables()
    perk = plane.reshape(2, GRID // 4, 4, 2, KEPT).transpose(3, 4, 1, 0, 2).reshape(2, KEPT, 2 * GRID)
    out = np.zeros((YL, KWIN, 2 * GRID), np.float64)
    for d in range(2):
        for b in range(KEPT * HALF):
            k, j = divmod(b, KEPT)
            n, r = divmod(b, BTILE)
            row = n * 2 * BTILE + d * (BTILE if n < NBT else 64) + r
            out[row, k - window(n)[0]] = perk[d, j]
    return out.reshape(YL, KWIN * 2 * GRID).astype(ml_dtypes.bfloat16)


def kron_block():
    _, plane = tables()
    out = np.zeros((2, AEI, QC, NT, QC * SLAB), np.float64)
    slabs = plane.reshape(2, NT, SLAB, AEI).transpose(0, 3, 1, 2)
    for q in range(QC):
        out[:, :, q, :, 8 * q : 8 * q + 8] = slabs[..., :8]
        out[:, :, q, :, 8 * QC + 4 * q : 8 * QC + 4 * q + 4] = slabs[..., 8:]
    return out.reshape(2, AEI * QC, GRID * QC).astype(ml_dtypes.bfloat16)


def copy_in(refs, spaces, sems):
    copies = [pltpu.make_async_copy(ref, space, sems.at[i]) for i, (ref, space) in enumerate(zip(refs, spaces))]
    for copy in copies:
        copy.start()
    return copies


def spectra_kernel(*refs):
    n = VC + NX + 3
    o_ref, dens, zs, sems = refs[n], *refs[2 * n + 1 :]
    spaces = refs[n + 1 : 2 * n + 1]
    v_refs, c_refs, (t_ref, w_ref) = spaces[:VC], spaces[VC : n - 2], spaces[n - 2 :]
    tables = copy_in(refs[n - 2 : n], spaces[n - 2 :], sems.at[NCUT])
    cuts = []
    for cut in range(NCUT):
        lanes = pl.ds(cut * (GRID * GRID // NCUT), GRID * GRID // NCUT)
        cuts.append(copy_in([r.at[:, :, lanes] for r in refs[: n - 2]], [r.at[:, :, lanes] for r in spaces[: n - 2]], sems.at[cut]))
    tables[0].wait()

    def body(step, _):
        lanes = pl.ds(pl.multiple_of(step * YSTEP, YSTEP), YSTEP)

        def parts(ref, b):
            wave = ref[b, :, lanes].astype(F32)
            return wave[:8], wave[8:]

        def tile(pieces):
            heads = [head for head, _ in pieces]
            tails = [jnp.concatenate([pieces[i][1], pieces[i + 1][1]], axis=0) for i in range(0, QC, 2)]
            return jnp.concatenate(heads + tails, axis=0).astype(BF)

        bands = [(c_refs[m], b) for m in range(3) for b in range(2)] + [(c_refs[3], 0), (c_refs[4], 0)]
        cond = [tile([parts(ref, b) for ref, b in bands[QC * h : QC * (h + 1)]]) for h in range(2)]
        for v in range(VC):
            val = tile([parts(v_refs[v], 0)] * QC)
            for h in range(2):
                r0 = (v * 2 + h) * SLAB * QC
                dens[r0 : r0 + SLAB * QC, :] = val * cond[h]
        groups = []
        for sub in range(YSTEP // ZGRP):
            z = jnp.dot(dens[:, sub * ZGRP : (sub + 1) * ZGRP], t_ref[...], preferred_element_type=F32)
            groups.append(z.T.reshape(HALF, 8, ROWS))
        zs[:, pl.ds(pl.multiple_of(step * 16, 16), 16), :] = jnp.concatenate(groups, axis=1).astype(BF)
        return 0

    for cut in range(NCUT):
        for copy in cuts[cut]:
            copy.wait()
        lax.fori_loop(cut * (NSTEP // NCUT), (cut + 1) * (NSTEP // NCUT), body, 0)
    tables[1].wait()
    for n in range(NBT + 1):
        r0 = n * 2 * BTILE
        rows = 2 * BTILE if n < NBT else BTILE
        k0, width = window(n)
        zk = zs[k0 : k0 + width].reshape(width * 2 * GRID, ROWS)
        y = jnp.dot(w_ref[r0 : r0 + rows, : width * 2 * GRID], zk, preferred_element_type=F32)
        yt = y.T.astype(BF).reshape(NT, SLAB * QC, rows)
        if n < NBT - 1:
            l0 = n // 2 * 512 + n % 2 * BTILE
            o_ref[:, :, l0 : l0 + BTILE] = yt[:, :, :BTILE]
            o_ref[:, :, l0 + 256 : l0 + 256 + BTILE] = yt[:, :, BTILE:]
        else:
            o_ref[:, :, r0 : r0 + rows] = yt


def spectra(vs, cs, t, w):
    operands = [*vs, *cs, t, w]
    return pl.pallas_call(
        spectra_kernel,
        in_specs=[pl.BlockSpec(memory_space=pl.ANY)] * len(operands),
        out_specs=pl.BlockSpec(memory_space=pltpu.VMEM),
        out_shape=jax.ShapeDtypeStruct((NT, SLAB * QC, YL), BF),
        scratch_shapes=[pltpu.VMEM(x.shape, BF) for x in operands]
        + [
            pltpu.VMEM((ROWS, YSTEP), BF),
            pltpu.VMEM((HALF, 2 * GRID, ROWS), BF),
            pltpu.SemaphoreType.DMA((NCUT + 1, len(operands) - 2)),
        ],
        compiler_params=pltpu.CompilerParams(vmem_limit_bytes=58 * 2**20),
        name="spectra",
    )(*operands)


def lines_kernel(y_ref, m_ref, _, s_ref):
    rows = AEI * QC

    def line(d, lanes):
        return jnp.dot(m_ref[d], y_ref[:, lanes], preferred_element_type=F32)

    for g in range(2):
        s = line(0, pl.ds(512 * g, 256)) + line(1, pl.ds(512 * g + 256, 256))
        s_ref[g * rows : (g + 1) * rows, :] = s.astype(BF)
    s = line(0, pl.ds(1024, BTILE)) + line(1, pl.ds(1024 + BTILE, BTILE))
    s_ref[2 * rows :, :BTILE] = s.astype(BF)
    last = pl.ds(1024 + 2 * BTILE, BTILE)
    s = line(0, last) + pltpu.roll(line(1, last), 64, 1)
    s_ref[2 * rows :, BTILE:] = s.astype(BF)


def lines(y, m, after):
    vmem = pl.BlockSpec(memory_space=pltpu.VMEM)
    return pl.pallas_call(
        lines_kernel,
        in_specs=[vmem, vmem, pl.BlockSpec(memory_space=pl.ANY)],
        out_specs=vmem,
        out_shape=jax.ShapeDtypeStruct((NGRP * AEI * QC, CODES), BF),
        compiler_params=pltpu.CompilerParams(vmem_limit_bytes=40 * 2**20),
        name="lines",
    )(y, m, after)


def picked(s_ref, a_ref, h_ref, chunk):
    row = lax.broadcasted_iota(jnp.int32, (SB, CODES), 0)
    outs = []
    for g in range(GCH // CODES):
        lanes = pl.ds(g * CODES, CODES)
        r = jnp.dot(s_ref[...], h_ref[:, lanes], preferred_element_type=F32)
        code = a_ref[:, lanes] - row // QC
        acc = jnp.zeros((SB, CODES), F32)
        for a in range(0, NGRP * AEI, 2):
            acc = jnp.where(code == a, r[a * QC : (a + 2) * QC], acc)
        both = acc + pltpu.roll(acc, QC, 0)
        outs.append(jnp.where(row // QC == chunk, both, 0.0))
    return jnp.concatenate(outs, axis=1)


def first_kernel(s_ref, a_ref, b_ref, o_ref, h_ref):
    codes = lax.broadcasted_iota(jnp.int32, (CODES, GCH), 0)
    h_ref[...] = (codes == b_ref[...]).astype(F32).astype(BF)
    o_ref[...] = picked(s_ref, a_ref, h_ref, 0)


def second_kernel(s_ref, a_ref, h_ref, first_ref, oc_ref, or_ref):
    out = (first_ref[...] + picked(s_ref, a_ref, h_ref, 1)).astype(BF)
    oc_ref[0] = out
    for h in range(GCH // RB):
        or_ref[h] = out[:, h * RB : (h + 1) * RB]


def along(rows):
    return pl.BlockSpec((rows, GCH), lambda i: (0, i))


def pick_first(s, a, b):
    return pl.pallas_call(
        first_kernel,
        grid=(GP // GCH,),
        in_specs=[pl.BlockSpec((NGRP * AEI * QC, CODES), lambda i: (0, 0)), along(1), along(1)],
        out_specs=[along(SB), along(CODES)],
        out_shape=[jax.ShapeDtypeStruct((SB, GP), F32), jax.ShapeDtypeStruct((CODES, GP), BF)],
        compiler_params=pltpu.CompilerParams(vmem_limit_bytes=40 * 2**20),
        name="pick_first",
    )(s, a, b)


def pick_second(s, a, chosen, first):
    per = 4 * RB // GCH
    return pl.pallas_call(
        second_kernel,
        grid=(GP // GCH,),
        in_specs=[pl.BlockSpec((NGRP * AEI * QC, CODES), lambda i: (0, 0)), along(1), along(CODES), along(SB)],
        out_specs=[
            pl.BlockSpec((1, SB, GCH), lambda i: (i // per, 0, i % per)),
            pl.BlockSpec((GCH // RB, SB, RB), lambda i: (i, 0, 0)),
        ],
        out_shape=[
            jax.ShapeDtypeStruct((NT, SB, 4 * RB), BF),
            jax.ShapeDtypeStruct((32, SB, RB), BF),
        ],
        compiler_params=pltpu.CompilerParams(vmem_limit_bytes=40 * 2**20),
        name="pick_second",
    )(s, a, chosen, first)


KP = NT * SB
LA = 512
XORDER = (0, 1, 3, 2)
ZORDER = (0, 1, 2, 3, 7, 6, 5, 4)


def a_pieces():
    whole = [[(x, z) for x in XORDER] for z in ZORDER[:-1]]
    return whole + [[(x, 4) for x in XORDER[:2]], [(x, 4) for x in XORDER[2:]]]


def b_pieces():
    whole = [[(x, z) for z in range(NZ)] for x in XORDER[:-1]]
    return whole + [[(2, z) for z in range(NZ // 2)], [(2, z) for z in range(NZ // 2, NZ)]]


def product_kernel(xz_ref, w_ref, *refs):
    na, nb = len(a_pieces()), len(b_pieces())
    n = 1 + na + nb
    o_ref, spaces, (wr, acc_ref, sems) = refs[n], refs[n + 1 : 2 * n + 1], refs[2 * n + 1 :]
    copies = copy_in(refs[:n], spaces, sems)
    r_ref, a_refs, b_refs = spaces[0], spaces[1 : 1 + na], spaces[1 + na :]
    copies[0].wait()
    for p in range(32):
        rows = jnp.concatenate([r_ref[t, p].astype(F32) for t in range(NT)], axis=0)
        wr[p] = (rows * w_ref[KP * p : KP * (p + 1), :]).astype(BF)

    def part(pieces, ref, z_of):
        lhs = [wr[lax.rem(xz_ref[0] + (NX - dx), NX) * NZ + z_of(dz)] for dx, dz in pieces]
        return lax.dot_general(
            jnp.concatenate(lhs, axis=0), ref[...], (((0,), (0,)), ((), ())), preferred_element_type=F32
        )

    def total(pieces, operands, waits, z_of):
        acc = None
        for piece, ref, copy in zip(pieces, operands, waits):
            copy.wait()
            more = part(piece, ref, z_of)
            acc = more if acc is None else acc + more
        return acc

    acc_ref[:, :LA] = total(a_pieces(), a_refs, copies[1 : 1 + na], lambda dz: lax.rem(xz_ref[1] + (NZ - dz), NZ))
    acc_ref[:, LA:] = total(b_pieces(), b_refs, copies[1 + na :], lambda z: z)
    for q in range(4):
        o_ref[:, 375 * q : 375 * (q + 1)] = acc_ref[:375, RB * q : RB * q + 375]


def product(place, rows, weight, a_cols, b_cols):
    operands = [rows, *a_cols, *b_cols]
    vmem = pl.BlockSpec(memory_space=pltpu.VMEM)
    return pl.pallas_call(
        product_kernel,
        in_specs=[pl.BlockSpec(memory_space=pltpu.SMEM), vmem] + [pl.BlockSpec(memory_space=pl.ANY)] * len(operands),
        out_specs=vmem,
        out_shape=jax.ShapeDtypeStruct((375, 1500), F32),
        scratch_shapes=[pltpu.VMEM(x.shape, BF) for x in operands]
        + [
            pltpu.VMEM((32, KP, RB), BF),
            pltpu.VMEM((RB, 4 * RB), F32),
            pltpu.SemaphoreType.DMA((len(operands),)),
        ],
        compiler_params=pltpu.CompilerParams(vmem_limit_bytes=58 * 2**20),
        name="product",
    )(place, weight, *operands)


def ring(value, axis, size):
    return ring_on(value, shift(value, axis, size, 1), shift(value, axis, size, -1), axis, size)


def ring_on(value, up, down, axis, size):
    ups, downs = [up], [down]
    for _ in range(size // 2 - 2):
        ups.append(shift(ups[-1], axis, size, 1))
        downs.append(shift(downs[-1], axis, size, -1))
    half = value.shape[0] // 2
    far = [shift(ups[-1][:half], axis, size, 1), shift(downs[-1][half:], axis, size, -1)]
    return [value] + ups + downs, far


def pick_levels(picks, table):
    codes = jnp.arange(table.shape[0], dtype=jnp.int32)
    return jnp.sum(jnp.where(picks[:, None] == codes[None, :], table[None, :], 0.0), axis=1)


def spread(levels, places):
    codes = jnp.arange(levels.shape[0], dtype=jnp.int32)[None, :]
    return jnp.sum(jnp.where(codes == places.astype(np.int32), levels[None, :], 0.0), axis=1, keepdims=True)


def shift(value, axis, size, step):
    return lax.ppermute(value, axis, [(i, (i + step) % size) for i in range(size)])


def per_device(
    valence_waves,
    cond_waves,
    valence_energy,
    conduction_energy,
    valence_pick,
    cond_pick,
    cond_slot,
    g_index,
):
    cs, far = ring(cond_waves, "x", NX)
    cs += far
    depth, plane, kron = jnp.asarray(depth_block()), jnp.asarray(plane_block()), jnp.asarray(kron_block())
    tile = ("y", "core")
    vs = [valence_waves] + [None] * (VB - 1)
    for m in range(1, VB // 2):
        vs[m] = shift(vs[m - 1], "z", NZ, 1)
        vs[VB - m] = shift(vs[(VB - m + 1) % VB], "z", NZ, -1)
    vs[VB // 2] = shift(vs[2], "z", NZ, 2)
    specs = [spectra([vs[k] for k in slots], cs, depth, plane) for slots in SLOTS]
    slabs = [lax.all_to_all(spec, tile, split_axis=0, concat_axis=0, tiled=True) for spec in specs]

    valence_level = pick_levels(valence_pick, valence_energy)
    band_level = pick_levels(cond_pick, conduction_energy)
    slot_codes = jnp.arange(NC, dtype=jnp.int32)
    slot_level = jnp.sum(
        jnp.where(cond_slot[:, None] == slot_codes[None, :], band_level[:, None], 0.0), axis=0
    )
    factor = 4.0 / math.sqrt(NV * NC)
    xs, zs, ts, c, ms, bs = np.ix_(*(np.arange(n) for n in (NX, NZ, NT, 2, 2, 2)))
    v_of = VB * xs + (zs - np.array(SLOTS)[c, ts // 2]) % NZ
    s_of = 2 * NZ * ((xs - np.array(XORDER)[2 * (ts % 2) + ms]) % NX) + 2 * zs + bs
    v_of, s_of = (np.broadcast_to(m, (NX, NZ, NT, 2, 2, 2)).reshape(NV * NC, 1) for m in (v_of, s_of))
    weight = factor / (spread(valence_level, v_of) - spread(slot_level, s_of))

    index = jnp.pad(g_index.reshape(32, 375), ((0, 0), (0, RB - 375))).reshape(1, GP)
    a_code = index // (KEPT * HALF)
    rest = index % (KEPT * HALF)
    b_code = (rest % HALF) * KEPT + rest // HALF
    a_code = a_code + AEI * (b_code // CODES)
    b_code = b_code % CODES

    first, chosen = pick_first(lines(slabs[0].reshape(GRID * QC, YL), kron, specs[1]), a_code, b_code)
    cols, for_rows = pick_second(lines(slabs[1].reshape(GRID * QC, YL), kron, specs[1]), a_code, chosen, first)
    cols = lax.all_to_all(cols, tile, split_axis=0, concat_axis=0, tiled=True).reshape(KP, 4 * RB)
    b_bundle = lax.all_gather(cols[:, LA:], "z", axis=0, tiled=True)
    near, far = ring(cols[:, :LA], "x", NX)
    a_bundle = jnp.concatenate(near + far, axis=0)
    a_up, a_down = shift(a_bundle, "z", NZ, 1), shift(a_bundle, "z", NZ, -1)
    for_rows, a_up, a_down = lax.optimization_barrier((for_rows, a_up, a_down))
    a_cols, a_far = ring_on(a_bundle, a_up, a_down, "z", NZ)
    b_cols, b_far = ring(b_bundle, "x", NX)
    rows = lax.all_to_all(for_rows, ("x", "z"), split_axis=0, concat_axis=0, tiled=True)
    rows = lax.all_gather(rows, ("y", "core"), axis=0, tiled=False)
    place = jnp.stack([lax.axis_index("x"), lax.axis_index("z")]).astype(jnp.int32)
    return product(place, rows, weight, a_cols + a_far, b_cols + b_far)


def solution(mesh):
    fine = Mesh(mesh.devices.reshape(NX, NZ, NY, NCORE), ("x", "z", "y", "core"))
    waves = P(("x", "z"), ("y", "core"), None)
    return jax.shard_map(
        per_device,
        mesh=fine,
        in_specs=(waves, waves, P(), P(), P(), P(), P(), P()),
        out_specs=P(("x", "z"), ("y", "core")),
        check_vma=False,
    )
```

```python
import functools
import math

import jax
import jax.numpy as jnp
import ml_dtypes
import numpy as np
from jax import lax
from jax.experimental import pallas as pl
from jax.experimental.pallas import tpu as pltpu
from jax.sharding import Mesh, PartitionSpec as P

NV = 32
NC = 64
GRID = 96
KM = 18
NG = 12000
KEPT = 2 * KM + 1
HALF = KM + 1
NX, NZ, NY, NCORE = 4, 8, 4, 2
NT = NY * NCORE
SLAB = GRID // NT
VB = 8
SB = 8
VC = 4
QC = 4
SLOTS = ((0, 1, 7, 2), (6, 3, 5, 4))
ROWS = SLAB * VC * SB
ZGRP = 384
ZOUT = HALF * 8
YSTEP = 768
NSTEP = GRID * GRID // YSTEP
NCUT = 4
BTILE = 128
NBT = 5
KWIN = 5
YL = 1408
AEI = 2 * KEPT
RB = 384
GP = 32 * RB
GCH = 768
CODES = 256
NGRP = 3
BF = jnp.bfloat16
F32 = jnp.float32


def tables():
    pos = np.arange(GRID)
    scale = 1.0 / math.sqrt(GRID)

    def angles(freqs):
        turns = (np.mod(freqs, GRID)[None, :] * pos[:, None]) % GRID
        return turns.astype(np.float64) * (2.0 * math.pi / GRID)

    ad = angles(np.arange(HALF))
    depth = np.stack([np.cos(ad), -np.sin(ad)], axis=1) * scale
    ap = angles(np.arange(KEPT) - KM)
    c, s = np.cos(ap), np.sin(ap)
    plane = np.stack([np.stack([c, s]), np.stack([-s, c])], axis=2) * scale
    return depth, plane


def depth_block():
    depth, _ = tables()
    out = np.zeros((4, GRID, HALF, 2, 4), np.float64)
    for y in range(4):
        out[y, :, :, :, y] = depth.transpose(0, 2, 1)
    return out.reshape(ZGRP, ZOUT).astype(ml_dtypes.bfloat16)


def window(n):
    first = BTILE * n // KEPT
    return first, min((BTILE * n + BTILE - 1) // KEPT, HALF - 1) + 1 - first


def plane_block():
    _, plane = tables()
    perk = plane.reshape(2, GRID // 4, 4, 2, KEPT).transpose(3, 4, 1, 0, 2).reshape(2, KEPT, 2 * GRID)
    out = np.zeros((YL, KWIN, 2 * GRID), np.float64)
    for d in range(2):
        for b in range(KEPT * HALF):
            k, j = divmod(b, KEPT)
            n, r = divmod(b, BTILE)
            row = n * 2 * BTILE + d * (BTILE if n < NBT else 64) + r
            out[row, k - window(n)[0]] = perk[d, j]
    return out.reshape(YL, KWIN * 2 * GRID).astype(ml_dtypes.bfloat16)


def kron_block():
    _, plane = tables()
    out = np.zeros((2, AEI, QC, NT, QC * SLAB), np.float64)
    slabs = plane.reshape(2, NT, SLAB, AEI).transpose(0, 3, 1, 2)
    for q in range(QC):
        out[:, :, q, :, 8 * q : 8 * q + 8] = slabs[..., :8]
        out[:, :, q, :, 8 * QC + 4 * q : 8 * QC + 4 * q + 4] = slabs[..., 8:]
    return out.reshape(2, AEI * QC, GRID * QC).astype(ml_dtypes.bfloat16)


def copy_in(refs, spaces, sems):
    copies = [pltpu.make_async_copy(ref, space, sems.at[i]) for i, (ref, space) in enumerate(zip(refs, spaces))]
    for copy in copies:
        copy.start()
    return copies


def spectra_kernel(*refs):
    n = VC + NX + 3
    o_ref, dens, zs, sems = refs[n], *refs[2 * n + 1 :]
    spaces = refs[n + 1 : 2 * n + 1]
    v_refs, c_refs, (t_ref, w_ref) = spaces[:VC], spaces[VC : n - 2], spaces[n - 2 :]
    tables = copy_in([refs[n - 2]], [t_ref], sems.at[NCUT])
    cuts = []
    for cut in range(NCUT):
        lanes = pl.ds(cut * (GRID * GRID // NCUT), GRID * GRID // NCUT)
        cuts.append(copy_in([r.at[:, :, lanes] for r in refs[: n - 2]], [r.at[:, :, lanes] for r in spaces[: n - 2]], sems.at[cut]))
    tables.append(pltpu.make_async_copy(refs[n - 1], w_ref, sems.at[NCUT, 1]))
    tables[1].start()
    tables[0].wait()

    def body(step, _):
        lanes = pl.ds(pl.multiple_of(step * YSTEP, YSTEP), YSTEP)

        def parts(ref, b):
            wave = ref[b, :, lanes].astype(F32)
            return wave[:8], wave[8:]

        def tile(pieces):
            heads = [head for head, _ in pieces]
            tails = [jnp.concatenate([pieces[i][1], pieces[i + 1][1]], axis=0) for i in range(0, QC, 2)]
            return jnp.concatenate(heads + tails, axis=0).astype(BF)

        bands = [(c_refs[m], b) for m in range(3) for b in range(2)] + [(c_refs[3], 0), (c_refs[4], 0)]
        cond = [tile([parts(ref, b) for ref, b in bands[QC * h : QC * (h + 1)]]) for h in range(2)]
        for v in range(VC):
            val = tile([parts(v_refs[v], 0)] * QC)
            for h in range(2):
                r0 = (v * 2 + h) * SLAB * QC
                dens[r0 : r0 + SLAB * QC, :] = val * cond[h]
        groups = []
        for sub in range(YSTEP // ZGRP):
            z = jnp.dot(dens[:, sub * ZGRP : (sub + 1) * ZGRP], t_ref[...], preferred_element_type=F32)
            groups.append(z.T.reshape(HALF, 8, ROWS))
        zs[:, pl.ds(pl.multiple_of(step * 16, 16), 16), :] = jnp.concatenate(groups, axis=1).astype(BF)
        return 0

    for cut in range(NCUT):
        for copy in cuts[cut]:
            copy.wait()
        lax.fori_loop(cut * (NSTEP // NCUT), (cut + 1) * (NSTEP // NCUT), body, 0)
    tables[1].wait()
    for n in range(NBT + 1):
        r0 = n * 2 * BTILE
        rows = 2 * BTILE if n < NBT else BTILE
        k0, width = window(n)
        zk = zs[k0 : k0 + width].reshape(width * 2 * GRID, ROWS)
        y = jnp.dot(w_ref[r0 : r0 + rows, : width * 2 * GRID], zk, preferred_element_type=F32)
        yt = y.T.astype(BF).reshape(NT, SLAB * QC, rows)
        if n < NBT - 1:
            l0 = n // 2 * 512 + n % 2 * BTILE
            o_ref[:, :, l0 : l0 + BTILE] = yt[:, :, :BTILE]
            o_ref[:, :, l0 + 256 : l0 + 256 + BTILE] = yt[:, :, BTILE:]
        else:
            o_ref[:, :, r0 : r0 + rows] = yt


def spectra(vs, cs, t, w):
    operands = [*vs, *cs, t, w]
    return pl.pallas_call(
        spectra_kernel,
        in_specs=[pl.BlockSpec(memory_space=pl.ANY)] * len(operands),
        out_specs=pl.BlockSpec(memory_space=pltpu.VMEM),
        out_shape=jax.ShapeDtypeStruct((NT, SLAB * QC, YL), BF),
        scratch_shapes=[pltpu.VMEM(x.shape, BF) for x in operands]
        + [
            pltpu.VMEM((ROWS, YSTEP), BF),
            pltpu.VMEM((HALF, 2 * GRID, ROWS), BF),
            pltpu.SemaphoreType.DMA((NCUT + 1, len(operands) - 2)),
        ],
        compiler_params=pltpu.CompilerParams(vmem_limit_bytes=58 * 2**20),
        name="spectra",
    )(*operands)


def lines_kernel(y_ref, m_ref, s_ref):
    rows = AEI * QC

    def line(d, lanes):
        return jnp.dot(m_ref[d], y_ref[:, lanes], preferred_element_type=F32)

    for g in range(2):
        s = line(0, pl.ds(512 * g, 256)) + line(1, pl.ds(512 * g + 256, 256))
        s_ref[g * rows : (g + 1) * rows, :] = s.astype(BF)
    s = line(0, pl.ds(1024, BTILE)) + line(1, pl.ds(1024 + BTILE, BTILE))
    s_ref[2 * rows :, :BTILE] = s.astype(BF)
    last = pl.ds(1024 + 2 * BTILE, BTILE)
    s = line(0, last) + pltpu.roll(line(1, last), 64, 1)
    s_ref[2 * rows :, BTILE:] = s.astype(BF)


def lines(y, m):
    return pl.pallas_call(
        lines_kernel,
        out_shape=jax.ShapeDtypeStruct((NGRP * AEI * QC, CODES), BF),
        compiler_params=pltpu.CompilerParams(vmem_limit_bytes=40 * 2**20),
        name="lines",
    )(y, m)


def picked(s_ref, a_ref, b_ref, chunk):
    codes = lax.broadcasted_iota(jnp.int32, (CODES, CODES), 0)
    row = lax.broadcasted_iota(jnp.int32, (SB, CODES), 0)
    outs = []
    for g in range(GCH // CODES):
        lanes = pl.ds(g * CODES, CODES)
        chosen = (codes == b_ref[:, lanes]).astype(F32).astype(BF)
        r = jnp.dot(s_ref[...], chosen, preferred_element_type=F32)
        code = a_ref[:, lanes] - row // QC
        acc = jnp.zeros((SB, CODES), F32)
        for a in range(0, NGRP * AEI, 2):
            acc = jnp.where(code == a, r[a * QC : (a + 2) * QC], acc)
        both = acc + pltpu.roll(acc, QC, 0)
        outs.append(jnp.where(row // QC == chunk, both, 0.0))
    return jnp.concatenate(outs, axis=1)


def first_kernel(s_ref, a_ref, b_ref, o_ref):
    o_ref[...] = picked(s_ref, a_ref, b_ref, 0)


def second_kernel(s_ref, a_ref, b_ref, first_ref, oc_ref, or_ref):
    out = (first_ref[...] + picked(s_ref, a_ref, b_ref, 1)).astype(BF)
    oc_ref[0] = out
    for h in range(GCH // RB):
        or_ref[h] = out[:, h * RB : (h + 1) * RB]


def pick_specs():
    return [
        pl.BlockSpec((NGRP * AEI * QC, CODES), lambda i: (0, 0)),
        pl.BlockSpec((1, GCH), lambda i: (0, i)),
        pl.BlockSpec((1, GCH), lambda i: (0, i)),
    ]


def pick_first(s, a, b):
    return pl.pallas_call(
        first_kernel,
        grid=(GP // GCH,),
        in_specs=pick_specs(),
        out_specs=pl.BlockSpec((SB, GCH), lambda i: (0, i)),
        out_shape=jax.ShapeDtypeStruct((SB, GP), F32),
        compiler_params=pltpu.CompilerParams(vmem_limit_bytes=40 * 2**20),
        name="pick_first",
    )(s, a, b)


def pick_second(s, a, b, first):
    per = 4 * RB // GCH
    return pl.pallas_call(
        second_kernel,
        grid=(GP // GCH,),
        in_specs=pick_specs() + [pl.BlockSpec((SB, GCH), lambda i: (0, i))],
        out_specs=[
            pl.BlockSpec((1, SB, GCH), lambda i: (i // per, 0, i % per)),
            pl.BlockSpec((GCH // RB, SB, RB), lambda i: (i, 0, 0)),
        ],
        out_shape=[
            jax.ShapeDtypeStruct((NT, SB, 4 * RB), BF),
            jax.ShapeDtypeStruct((32, SB, RB), BF),
        ],
        compiler_params=pltpu.CompilerParams(vmem_limit_bytes=40 * 2**20),
        name="pick_second",
    )(s, a, b, first)


KP = NT * SB
LA = 640
LB = 4 * RB - LA
LG = 1024
XORDER = (0, 1, 3, 2)
ZORDER = (0, 1, 2, 3, 7, 6, 5, 4)


def a_pieces():
    whole = [[(x, z) for x in XORDER] for z in ZORDER[:-1]]
    return whole + [[(x, 4) for x in XORDER[:2]], [(x, 4) for x in XORDER[2:]]]


def b_pieces():
    whole = [[(x, z) for z in range(NZ)] for x in XORDER[:-1]]
    return whole + [[(2, z) for z in range(NZ // 2)], [(2, z) for z in range(NZ // 2, NZ)]]


def product_kernel(xz_ref, w_ref, *refs):
    na, nb = len(a_pieces()), len(b_pieces())
    n = 1 + na + nb
    o_ref, spaces, (wr, acc_ref, sems) = refs[n], refs[n + 1 : 2 * n + 1], refs[2 * n + 1 :]
    copies = copy_in(refs[:n], spaces, sems)
    r_ref, a_refs, b_refs = spaces[0], spaces[1 : 1 + na], spaces[1 + na :]
    copies[0].wait()
    for p in range(32):
        rows = jnp.concatenate([r_ref[t, p].astype(F32) for t in range(NT)], axis=0)
        wr[p] = (rows * w_ref[KP * p : KP * (p + 1), :]).astype(BF)

    def part(pieces, ref, z_of):
        lhs = [wr[lax.rem(xz_ref[0] + (NX - dx), NX) * NZ + z_of(dz)] for dx, dz in pieces]
        return lax.dot_general(
            jnp.concatenate(lhs, axis=0), ref[...], (((0,), (0,)), ((), ())), preferred_element_type=F32
        )

    def total(pieces, operands, waits, z_of):
        acc = None
        for piece, ref, copy in zip(pieces, operands, waits):
            copy.wait()
            more = part(piece, ref, z_of)
            acc = more if acc is None else acc + more
        return acc

    acc_ref[:, :LA] = total(a_pieces(), a_refs, copies[1 : 1 + na], lambda dz: lax.rem(xz_ref[1] + (NZ - dz), NZ))
    acc_ref[:, LA:] = total(b_pieces(), b_refs, copies[1 + na :], lambda z: z)
    for q in range(4):
        o_ref[:, 375 * q : 375 * (q + 1)] = acc_ref[:375, RB * q : RB * q + 375]


def product(place, rows, weight, a_cols, b_cols):
    operands = [rows, *a_cols, *b_cols]
    vmem = pl.BlockSpec(memory_space=pltpu.VMEM)
    return pl.pallas_call(
        product_kernel,
        in_specs=[pl.BlockSpec(memory_space=pltpu.SMEM), vmem] + [pl.BlockSpec(memory_space=pl.ANY)] * len(operands),
        out_specs=vmem,
        out_shape=jax.ShapeDtypeStruct((375, 1500), F32),
        scratch_shapes=[pltpu.VMEM(x.shape, BF) for x in operands]
        + [
            pltpu.VMEM((32, KP, RB), BF),
            pltpu.VMEM((RB, 4 * RB), F32),
            pltpu.SemaphoreType.DMA((len(operands),)),
        ],
        compiler_params=pltpu.CompilerParams(vmem_limit_bytes=58 * 2**20),
        name="product",
    )(place, weight, *operands)


def ring(value, axis, size):
    return ring_on(value, shift(value, axis, size, 1), shift(value, axis, size, -1), axis, size)


def ring_on(value, up, down, axis, size):
    ups, downs = [up], [down]
    for _ in range(size // 2 - 2):
        ups.append(shift(ups[-1], axis, size, 1))
        downs.append(shift(downs[-1], axis, size, -1))
    half = value.shape[0] // 2
    far = [shift(ups[-1][:half], axis, size, 1), shift(downs[-1][half:], axis, size, -1)]
    return [value] + ups + downs, far


def pick_levels(picks, table):
    codes = jnp.arange(table.shape[0], dtype=jnp.int32)
    return jnp.sum(jnp.where(picks[:, None] == codes[None, :], table[None, :], 0.0), axis=1)


def spread(levels, places):
    codes = jnp.arange(levels.shape[0], dtype=jnp.int32)[None, :]
    return jnp.sum(jnp.where(codes == places.astype(np.int32), levels[None, :], 0.0), axis=1, keepdims=True)


def shift(value, axis, size, step):
    return lax.ppermute(value, axis, [(i, (i + step) % size) for i in range(size)])


def per_device(
    valence_waves,
    cond_waves,
    valence_energy,
    conduction_energy,
    valence_pick,
    cond_pick,
    cond_slot,
    g_index,
):
    cs, far = ring(cond_waves, "x", NX)
    cs += far
    depth, plane, kron = jnp.asarray(depth_block()), jnp.asarray(plane_block()), jnp.asarray(kron_block())
    tile = ("y", "core")
    vs = [valence_waves] + [None] * (VB - 1)
    for m in range(1, VB // 2):
        vs[m] = shift(vs[m - 1], "z", NZ, 1)
        vs[VB - m] = shift(vs[(VB - m + 1) % VB], "z", NZ, -1)
    vs[VB // 2] = shift(vs[2], "z", NZ, 2)
    specs = [spectra([vs[k] for k in slots], cs, depth, plane) for slots in SLOTS]
    slabs = [lax.all_to_all(specs[0], tile, split_axis=0, concat_axis=0, tiled=True)]
    slabs[0], specs[1] = lax.optimization_barrier((slabs[0], specs[1]))
    slabs.append(lax.all_to_all(specs[1], tile, split_axis=0, concat_axis=0, tiled=True))

    valence_level = pick_levels(valence_pick, valence_energy)
    band_level = pick_levels(cond_pick, conduction_energy)
    slot_codes = jnp.arange(NC, dtype=jnp.int32)
    slot_level = jnp.sum(
        jnp.where(cond_slot[:, None] == slot_codes[None, :], band_level[:, None], 0.0), axis=0
    )
    factor = 4.0 / math.sqrt(NV * NC)
    xs, zs, ts, c, ms, bs = np.ix_(*(np.arange(n) for n in (NX, NZ, NT, 2, 2, 2)))
    v_of = VB * xs + (zs - np.array(SLOTS)[c, ts // 2]) % NZ
    s_of = 2 * NZ * ((xs - np.array(XORDER)[2 * (ts % 2) + ms]) % NX) + 2 * zs + bs
    v_of, s_of = (np.broadcast_to(m, (NX, NZ, NT, 2, 2, 2)).reshape(NV * NC, 1) for m in (v_of, s_of))
    weight = factor / (spread(valence_level, v_of) - spread(slot_level, s_of))

    index = jnp.pad(g_index.reshape(32, 375), ((0, 0), (0, RB - 375))).reshape(1, GP)
    a_code = index // (KEPT * HALF)
    rest = index % (KEPT * HALF)
    b_code = (rest % HALF) * KEPT + rest // HALF
    a_code = a_code + AEI * (b_code // CODES)
    b_code = b_code % CODES

    first = pick_first(lines(slabs[0].reshape(GRID * QC, YL), kron), a_code, b_code)
    cols, for_rows = pick_second(lines(slabs[1].reshape(GRID * QC, YL), kron), a_code, b_code, first)
    cols = lax.all_to_all(cols, tile, split_axis=0, concat_axis=0, tiled=True).reshape(KP, 4 * RB)
    b_part = jnp.concatenate([cols[:, LA:], cols[:, LA : LA + LG - LB]], axis=1)
    b_bundle = lax.all_gather(b_part, "z", axis=0, tiled=True)[:, :LB]
    a_part = cols[:, :LA]
    a_bundle = jnp.concatenate([a_part] + [shift(a_part, "x", NX, step) for step in (1, -1, 2)], axis=0)
    a_up, a_down = shift(a_bundle, "z", NZ, 1), shift(a_bundle, "z", NZ, -1)
    for_rows, a_up, a_down = lax.optimization_barrier((for_rows, a_up, a_down))
    ups, downs = [a_up], [a_down]
    for _ in range(2):
        ups.append(shift(ups[-1], "z", NZ, 1))
        downs.append(shift(downs[-1], "z", NZ, -1))
    half = a_bundle.shape[0] // 2
    a_far = [shift(ups[1][:half], "z", NZ, 2), shift(downs[1][half:], "z", NZ, -2)]
    a_cols = [a_bundle] + ups + downs
    b_cols, b_far = ring(b_bundle, "x", NX)
    rows = lax.all_to_all(for_rows, ("x", "z"), split_axis=0, concat_axis=0, tiled=True)
    rows = lax.all_gather(rows, ("y", "core"), axis=0, tiled=False)
    place = jnp.stack([lax.axis_index("x"), lax.axis_index("z")]).astype(jnp.int32)
    return product(place, rows, weight, a_cols + a_far, b_cols + b_far)


def solution(mesh):
    fine = Mesh(mesh.devices.reshape(NX, NZ, NY, NCORE), ("x", "z", "y", "core"))
    waves = P(("x", "z"), ("y", "core"), None)
    return jax.shard_map(
        per_device,
        mesh=fine,
        in_specs=(waves, waves, P(), P(), P(), P(), P(), P()),
        out_specs=P(("x", "z"), ("y", "core")),
        check_vma=False,
    )
```

```python
import functools
import math

import jax
import jax.numpy as jnp
import ml_dtypes
import numpy as np
from jax import lax
from jax.experimental import pallas as pl
from jax.experimental.pallas import tpu as pltpu
from jax.sharding import Mesh, PartitionSpec as P

NV = 32
NC = 64
GRID = 96
KM = 18
NG = 12000
KEPT = 2 * KM + 1
HALF = KM + 1
NX, NZ, NY, NCORE = 4, 8, 4, 2
NT = NY * NCORE
SLAB = GRID // NT
VB = 8
SB = 8
VC = 4
QC = 4
SLOTS = ((0, 1, 7, 2), (6, 3, 5, 4))
ROWS = SLAB * VC * SB
ZGRP = 384
ZOUT = HALF * 8
YSTEP = 768
NSTEP = GRID * GRID // YSTEP
NCUT = 4
BTILE = 128
NBT = 5
KWIN = 5
YL = 1408
AEI = 2 * KEPT
RB = 384
GP = 32 * RB
GCH = 768
CODES = 256
NGRP = 3
BF = jnp.bfloat16
F32 = jnp.float32


def tables():
    pos = np.arange(GRID)
    scale = 1.0 / math.sqrt(GRID)

    def angles(freqs):
        turns = (np.mod(freqs, GRID)[None, :] * pos[:, None]) % GRID
        return turns.astype(np.float64) * (2.0 * math.pi / GRID)

    ad = angles(np.arange(HALF))
    depth = np.stack([np.cos(ad), -np.sin(ad)], axis=1) * scale
    ap = angles(np.arange(KEPT) - KM)
    c, s = np.cos(ap), np.sin(ap)
    plane = np.stack([np.stack([c, s]), np.stack([-s, c])], axis=2) * scale
    return depth, plane


def depth_block():
    depth, _ = tables()
    out = np.zeros((4, GRID, HALF, 2, 4), np.float64)
    for y in range(4):
        out[y, :, :, :, y] = depth.transpose(0, 2, 1)
    return out.reshape(ZGRP, ZOUT).astype(ml_dtypes.bfloat16)


def window(n):
    first = BTILE * n // KEPT
    return first, min((BTILE * n + BTILE - 1) // KEPT, HALF - 1) + 1 - first


def plane_block():
    _, plane = tables()
    perk = plane.reshape(2, GRID // 4, 4, 2, KEPT).transpose(3, 4, 1, 0, 2).reshape(2, KEPT, 2 * GRID)
    out = np.zeros((YL, KWIN, 2 * GRID), np.float64)
    for d in range(2):
        for b in range(KEPT * HALF):
            k, j = divmod(b, KEPT)
            n, r = divmod(b, BTILE)
            row = n * 2 * BTILE + d * (BTILE if n < NBT else 64) + r
            out[row, k - window(n)[0]] = perk[d, j]
    return out.reshape(YL, KWIN * 2 * GRID).astype(ml_dtypes.bfloat16)


def kron_block():
    _, plane = tables()
    out = np.zeros((2, AEI, QC, NT, QC * SLAB), np.float64)
    slabs = plane.reshape(2, NT, SLAB, AEI).transpose(0, 3, 1, 2)
    for q in range(QC):
        out[:, :, q, :, 8 * q : 8 * q + 8] = slabs[..., :8]
        out[:, :, q, :, 8 * QC + 4 * q : 8 * QC + 4 * q + 4] = slabs[..., 8:]
    return out.reshape(2, AEI * QC, GRID * QC).astype(ml_dtypes.bfloat16)


def copy_in(refs, spaces, sems):
    copies = [pltpu.make_async_copy(ref, space, sems.at[i]) for i, (ref, space) in enumerate(zip(refs, spaces))]
    for copy in copies:
        copy.start()
    return copies


def spectra_kernel(*refs):
    n = VC + NX + 3
    o_ref, dens, zs, sems = refs[n], *refs[2 * n + 1 :]
    spaces = refs[n + 1 : 2 * n + 1]
    v_refs, c_refs, (t_ref, w_ref) = spaces[:VC], spaces[VC : n - 2], spaces[n - 2 :]
    tables = copy_in([refs[n - 2]], [t_ref], sems.at[NCUT])
    cuts = []
    for cut in range(NCUT):
        lanes = pl.ds(cut * (GRID * GRID // NCUT), GRID * GRID // NCUT)
        cuts.append(copy_in([r.at[:, :, lanes] for r in refs[: n - 2]], [r.at[:, :, lanes] for r in spaces[: n - 2]], sems.at[cut]))
    tables.append(pltpu.make_async_copy(refs[n - 1], w_ref, sems.at[NCUT, 1]))
    tables[1].start()
    tables[0].wait()

    def body(step, _):
        lanes = pl.ds(pl.multiple_of(step * YSTEP, YSTEP), YSTEP)

        def parts(ref, b):
            wave = ref[b, :, lanes].astype(F32)
            return wave[:8], wave[8:]

        def tile(pieces):
            heads = [head for head, _ in pieces]
            tails = [jnp.concatenate([pieces[i][1], pieces[i + 1][1]], axis=0) for i in range(0, QC, 2)]
            return jnp.concatenate(heads + tails, axis=0).astype(BF)

        bands = [(c_refs[m], b) for m in range(3) for b in range(2)] + [(c_refs[3], 0), (c_refs[4], 0)]
        cond = [tile([parts(ref, b) for ref, b in bands[QC * h : QC * (h + 1)]]) for h in range(2)]
        for v in range(VC):
            val = tile([parts(v_refs[v], 0)] * QC)
            for h in range(2):
                r0 = (v * 2 + h) * SLAB * QC
                dens[r0 : r0 + SLAB * QC, :] = val * cond[h]
        groups = []
        for sub in range(YSTEP // ZGRP):
            z = jnp.dot(dens[:, sub * ZGRP : (sub + 1) * ZGRP], t_ref[...], preferred_element_type=F32)
            groups.append(z.T.reshape(HALF, 8, ROWS))
        zs[:, pl.ds(pl.multiple_of(step * 16, 16), 16), :] = jnp.concatenate(groups, axis=1).astype(BF)
        return 0

    for cut in range(NCUT):
        for copy in cuts[cut]:
            copy.wait()
        lax.fori_loop(cut * (NSTEP // NCUT), (cut + 1) * (NSTEP // NCUT), body, 0)
    tables[1].wait()
    for n in range(NBT + 1):
        r0 = n * 2 * BTILE
        rows = 2 * BTILE if n < NBT else BTILE
        k0, width = window(n)
        zk = zs[k0 : k0 + width].reshape(width * 2 * GRID, ROWS)
        y = jnp.dot(w_ref[r0 : r0 + rows, : width * 2 * GRID], zk, preferred_element_type=F32)
        yt = y.T.astype(BF).reshape(NT, SLAB * QC, rows)
        if n < NBT - 1:
            l0 = n // 2 * 512 + n % 2 * BTILE
            o_ref[:, :, l0 : l0 + BTILE] = yt[:, :, :BTILE]
            o_ref[:, :, l0 + 256 : l0 + 256 + BTILE] = yt[:, :, BTILE:]
        else:
            o_ref[:, :, r0 : r0 + rows] = yt


def spectra(vs, cs, t, w):
    operands = [*vs, *cs, t, w]
    return pl.pallas_call(
        spectra_kernel,
        in_specs=[pl.BlockSpec(memory_space=pl.ANY)] * len(operands),
        out_specs=pl.BlockSpec(memory_space=pltpu.VMEM),
        out_shape=jax.ShapeDtypeStruct((NT, SLAB * QC, YL), BF),
        scratch_shapes=[pltpu.VMEM(x.shape, BF) for x in operands]
        + [
            pltpu.VMEM((ROWS, YSTEP), BF),
            pltpu.VMEM((HALF, 2 * GRID, ROWS), BF),
            pltpu.SemaphoreType.DMA((NCUT + 1, len(operands) - 2)),
        ],
        compiler_params=pltpu.CompilerParams(vmem_limit_bytes=58 * 2**20),
        name="spectra",
    )(*operands)


def lines_kernel(y_ref, m_ref, s_ref):
    rows = AEI * QC

    def line(d, lanes):
        return jnp.dot(m_ref[d], y_ref[:, lanes], preferred_element_type=F32)

    for g in range(2):
        s = line(0, pl.ds(512 * g, 256)) + line(1, pl.ds(512 * g + 256, 256))
        s_ref[g * rows : (g + 1) * rows, :] = s.astype(BF)
    s = line(0, pl.ds(1024, BTILE)) + line(1, pl.ds(1024 + BTILE, BTILE))
    s_ref[2 * rows :, :BTILE] = s.astype(BF)
    last = pl.ds(1024 + 2 * BTILE, BTILE)
    s = line(0, last) + pltpu.roll(line(1, last), 64, 1)
    s_ref[2 * rows :, BTILE:] = s.astype(BF)


def lines(y, m):
    return pl.pallas_call(
        lines_kernel,
        out_shape=jax.ShapeDtypeStruct((NGRP * AEI * QC, CODES), BF),
        compiler_params=pltpu.CompilerParams(vmem_limit_bytes=40 * 2**20),
        name="lines",
    )(y, m)


def picked(s_ref, a_ref, b_ref, chunk):
    codes = lax.broadcasted_iota(jnp.int32, (CODES, CODES), 0)
    row = lax.broadcasted_iota(jnp.int32, (SB, CODES), 0)
    outs = []
    for g in range(GCH // CODES):
        lanes = pl.ds(g * CODES, CODES)
        chosen = (codes == b_ref[:, lanes]).astype(F32).astype(BF)
        r = jnp.dot(s_ref[...], chosen, preferred_element_type=F32)
        code = a_ref[:, lanes] - row // QC
        acc = jnp.zeros((SB, CODES), F32)
        for a in range(0, NGRP * AEI, 2):
            acc = jnp.where(code == a, r[a * QC : (a + 2) * QC], acc)
        both = acc + pltpu.roll(acc, QC, 0)
        outs.append(jnp.where(row // QC == chunk, both, 0.0))
    return jnp.concatenate(outs, axis=1)


def first_kernel(s_ref, a_ref, b_ref, o_ref):
    o_ref[...] = picked(s_ref, a_ref, b_ref, 0)


def second_kernel(s_ref, a_ref, b_ref, first_ref, oc_ref, or_ref):
    out = (first_ref[...] + picked(s_ref, a_ref, b_ref, 1)).astype(BF)
    oc_ref[0] = out
    for h in range(GCH // RB):
        or_ref[h] = out[:, h * RB : (h + 1) * RB]


def pick_specs():
    return [
        pl.BlockSpec((NGRP * AEI * QC, CODES), lambda i: (0, 0)),
        pl.BlockSpec((1, GCH), lambda i: (0, i)),
        pl.BlockSpec((1, GCH), lambda i: (0, i)),
    ]


def pick_first(s, a, b):
    return pl.pallas_call(
        first_kernel,
        grid=(GP // GCH,),
        in_specs=pick_specs(),
        out_specs=pl.BlockSpec((SB, GCH), lambda i: (0, i)),
        out_shape=jax.ShapeDtypeStruct((SB, GP), F32),
        compiler_params=pltpu.CompilerParams(vmem_limit_bytes=40 * 2**20),
        name="pick_first",
    )(s, a, b)


def pick_second(s, a, b, first):
    per = 4 * RB // GCH
    return pl.pallas_call(
        second_kernel,
        grid=(GP // GCH,),
        in_specs=pick_specs() + [pl.BlockSpec((SB, GCH), lambda i: (0, i))],
        out_specs=[
            pl.BlockSpec((1, SB, GCH), lambda i: (i // per, 0, i % per)),
            pl.BlockSpec((GCH // RB, SB, RB), lambda i: (i, 0, 0)),
        ],
        out_shape=[
            jax.ShapeDtypeStruct((NT, SB, 4 * RB), BF),
            jax.ShapeDtypeStruct((32, SB, RB), BF),
        ],
        compiler_params=pltpu.CompilerParams(vmem_limit_bytes=40 * 2**20),
        name="pick_second",
    )(s, a, b, first)


KP = NT * SB
LA = 512
XORDER = (0, 1, 3, 2)
ZORDER = (0, 1, 2, 3, 7, 6, 5, 4)


def a_pieces():
    whole = [[(x, z) for x in XORDER] for z in ZORDER[:-1]]
    return whole + [[(x, 4) for x in XORDER[:2]], [(x, 4) for x in XORDER[2:]]]


def b_pieces():
    whole = [[(x, z) for z in range(NZ)] for x in XORDER[:-1]]
    return whole + [[(2, z) for z in range(NZ // 2)], [(2, z) for z in range(NZ // 2, NZ)]]


def product_kernel(xz_ref, w_ref, *refs):
    na, nb = len(a_pieces()), len(b_pieces())
    n = 1 + na + nb
    o_ref, spaces, (wr, acc_ref, sems) = refs[n], refs[n + 1 : 2 * n + 1], refs[2 * n + 1 :]
    copies = copy_in(refs[:n], spaces, sems)
    r_ref, a_refs, b_refs = spaces[0], spaces[1 : 1 + na], spaces[1 + na :]
    copies[0].wait()
    for p in range(32):
        rows = jnp.concatenate([r_ref[t, p].astype(F32) for t in range(NT)], axis=0)
        wr[p] = (rows * w_ref[KP * p : KP * (p + 1), :]).astype(BF)

    def part(pieces, ref, z_of):
        lhs = [wr[lax.rem(xz_ref[0] + (NX - dx), NX) * NZ + z_of(dz)] for dx, dz in pieces]
        return lax.dot_general(
            jnp.concatenate(lhs, axis=0), ref[...], (((0,), (0,)), ((), ())), preferred_element_type=F32
        )

    def total(pieces, operands, waits, z_of):
        acc = None
        for piece, ref, copy in zip(pieces, operands, waits):
            copy.wait()
            more = part(piece, ref, z_of)
            acc = more if acc is None else acc + more
        return acc

    acc_ref[:, :LA] = total(a_pieces(), a_refs, copies[1 : 1 + na], lambda dz: lax.rem(xz_ref[1] + (NZ - dz), NZ))
    acc_ref[:, LA:] = total(b_pieces(), b_refs, copies[1 + na :], lambda z: z)
    for q in range(4):
        o_ref[:, 375 * q : 375 * (q + 1)] = acc_ref[:375, RB * q : RB * q + 375]


def product(place, rows, weight, a_cols, b_cols):
    operands = [rows, *a_cols, *b_cols]
    vmem = pl.BlockSpec(memory_space=pltpu.VMEM)
    return pl.pallas_call(
        product_kernel,
        in_specs=[pl.BlockSpec(memory_space=pltpu.SMEM), vmem] + [pl.BlockSpec(memory_space=pl.ANY)] * len(operands),
        out_specs=vmem,
        out_shape=jax.ShapeDtypeStruct((375, 1500), F32),
        scratch_shapes=[pltpu.VMEM(x.shape, BF) for x in operands]
        + [
            pltpu.VMEM((32, KP, RB), BF),
            pltpu.VMEM((RB, 4 * RB), F32),
            pltpu.SemaphoreType.DMA((len(operands),)),
        ],
        compiler_params=pltpu.CompilerParams(vmem_limit_bytes=58 * 2**20),
        name="product",
    )(place, weight, *operands)


def ring(value, axis, size):
    return ring_on(value, shift(value, axis, size, 1), shift(value, axis, size, -1), axis, size)


def ring_on(value, up, down, axis, size):
    ups, downs = [up], [down]
    for _ in range(size // 2 - 2):
        ups.append(shift(ups[-1], axis, size, 1))
        downs.append(shift(downs[-1], axis, size, -1))
    half = value.shape[0] // 2
    far = [shift(ups[-1][:half], axis, size, 1), shift(downs[-1][half:], axis, size, -1)]
    return [value] + ups + downs, far


def pick_levels(picks, table):
    codes = jnp.arange(table.shape[0], dtype=jnp.int32)
    return jnp.sum(jnp.where(picks[:, None] == codes[None, :], table[None, :], 0.0), axis=1)


def spread(levels, places):
    codes = jnp.arange(levels.shape[0], dtype=jnp.int32)[None, :]
    return jnp.sum(jnp.where(codes == places.astype(np.int32), levels[None, :], 0.0), axis=1, keepdims=True)


def shift(value, axis, size, step):
    return lax.ppermute(value, axis, [(i, (i + step) % size) for i in range(size)])


def per_device(
    valence_waves,
    cond_waves,
    valence_energy,
    conduction_energy,
    valence_pick,
    cond_pick,
    cond_slot,
    g_index,
):
    cs, far = ring(cond_waves, "x", NX)
    cs += far
    depth, plane, kron = jnp.asarray(depth_block()), jnp.asarray(plane_block()), jnp.asarray(kron_block())
    tile = ("y", "core")
    vs = [valence_waves] + [None] * (VB - 1)
    for m in range(1, VB // 2):
        vs[m] = shift(vs[m - 1], "z", NZ, 1)
        vs[VB - m] = shift(vs[(VB - m + 1) % VB], "z", NZ, -1)
    vs[VB // 2] = shift(vs[2], "z", NZ, 2)
    specs = [spectra([vs[k] for k in slots], cs, depth, plane) for slots in SLOTS]
    slabs = [lax.all_to_all(specs[0], tile, split_axis=0, concat_axis=0, tiled=True)]
    slabs[0], specs[1] = lax.optimization_barrier((slabs[0], specs[1]))
    slabs.append(lax.all_to_all(specs[1], tile, split_axis=0, concat_axis=0, tiled=True))

    valence_level = pick_levels(valence_pick, valence_energy)
    band_level = pick_levels(cond_pick, conduction_energy)
    slot_codes = jnp.arange(NC, dtype=jnp.int32)
    slot_level = jnp.sum(
        jnp.where(cond_slot[:, None] == slot_codes[None, :], band_level[:, None], 0.0), axis=0
    )
    factor = 4.0 / math.sqrt(NV * NC)
    xs, zs, ts, c, ms, bs = np.ix_(*(np.arange(n) for n in (NX, NZ, NT, 2, 2, 2)))
    v_of = VB * xs + (zs - np.array(SLOTS)[c, ts // 2]) % NZ
    s_of = 2 * NZ * ((xs - np.array(XORDER)[2 * (ts % 2) + ms]) % NX) + 2 * zs + bs
    v_of, s_of = (np.broadcast_to(m, (NX, NZ, NT, 2, 2, 2)).reshape(NV * NC, 1) for m in (v_of, s_of))
    weight = factor / (spread(valence_level, v_of) - spread(slot_level, s_of))

    index = jnp.pad(g_index.reshape(32, 375), ((0, 0), (0, RB - 375))).reshape(1, GP)
    a_code = index // (KEPT * HALF)
    rest = index % (KEPT * HALF)
    b_code = (rest % HALF) * KEPT + rest // HALF
    a_code = a_code + AEI * (b_code // CODES)
    b_code = b_code % CODES

    first = pick_first(lines(slabs[0].reshape(GRID * QC, YL), kron), a_code, b_code)
    cols, for_rows = pick_second(lines(slabs[1].reshape(GRID * QC, YL), kron), a_code, b_code, first)
    cols = lax.all_to_all(cols, tile, split_axis=0, concat_axis=0, tiled=True).reshape(KP, 4 * RB)
    b_bundle = lax.all_gather(cols[:, LA:], "z", axis=0, tiled=True)
    a_part = cols[:, :LA]
    a_bundle = jnp.concatenate([a_part] + [shift(a_part, "x", NX, step) for step in (1, -1, 2)], axis=0)
    for_rows, a_bundle = lax.optimization_barrier((for_rows, a_bundle))
    a_up, a_down = shift(a_bundle, "z", NZ, 1), shift(a_bundle, "z", NZ, -1)
    b_bundle, a_up, a_down = lax.optimization_barrier((b_bundle, a_up, a_down))
    a_cols, a_far = ring_on(a_bundle, a_up, a_down, "z", NZ)
    b_cols, b_far = ring(b_bundle, "x", NX)
    rows = lax.all_to_all(for_rows, ("x", "z"), split_axis=0, concat_axis=0, tiled=True)
    rows = lax.all_gather(rows, ("y", "core"), axis=0, tiled=False)
    place = jnp.stack([lax.axis_index("x"), lax.axis_index("z")]).astype(jnp.int32)
    return product(place, rows, weight, a_cols + a_far, b_cols + b_far)


def solution(mesh):
    fine = Mesh(mesh.devices.reshape(NX, NZ, NY, NCORE), ("x", "z", "y", "core"))
    waves = P(("x", "z"), ("y", "core"), None)
    return jax.shard_map(
        per_device,
        mesh=fine,
        in_specs=(waves, waves, P(), P(), P(), P(), P(), P()),
        out_specs=P(("x", "z"), ("y", "core")),
        check_vma=False,
    )
```

```python
import functools
import math

import jax
import jax.numpy as jnp
import ml_dtypes
import numpy as np
from jax import lax
from jax.experimental import pallas as pl
from jax.experimental.pallas import tpu as pltpu
from jax.sharding import Mesh, PartitionSpec as P

NV = 32
NC = 64
GRID = 96
KM = 18
NG = 12000
KEPT = 2 * KM + 1
HALF = KM + 1
NX, NZ, NY, NCORE = 4, 8, 4, 2
NT = NY * NCORE
SLAB = GRID // NT
VB = 8
SB = 8
VC = 4
QC = 4
SLOTS = ((0, 1, 7, 2), (6, 3, 5, 4))
ROWS = SLAB * VC * SB
ZGRP = 384
ZOUT = HALF * 8
YSTEP = 768
NSTEP = GRID * GRID // YSTEP
NCUT = 4
BTILE = 128
NBT = 5
KWIN = 5
YL = 1408
AEI = 2 * KEPT
RB = 384
GP = 32 * RB
GCH = 768
CODES = 256
NGRP = 3
BF = jnp.bfloat16
F32 = jnp.float32


def tables():
    pos = np.arange(GRID)
    scale = 1.0 / math.sqrt(GRID)

    def angles(freqs):
        turns = (np.mod(freqs, GRID)[None, :] * pos[:, None]) % GRID
        return turns.astype(np.float64) * (2.0 * math.pi / GRID)

    ad = angles(np.arange(HALF))
    depth = np.stack([np.cos(ad), -np.sin(ad)], axis=1) * scale
    ap = angles(np.arange(KEPT) - KM)
    c, s = np.cos(ap), np.sin(ap)
    plane = np.stack([np.stack([c, s]), np.stack([-s, c])], axis=2) * scale
    return depth, plane


def depth_block():
    depth, _ = tables()
    out = np.zeros((4, GRID, HALF, 2, 4), np.float64)
    for y in range(4):
        out[y, :, :, :, y] = depth.transpose(0, 2, 1)
    return out.reshape(ZGRP, ZOUT).astype(ml_dtypes.bfloat16)


def window(n):
    first = BTILE * n // KEPT
    return first, min((BTILE * n + BTILE - 1) // KEPT, HALF - 1) + 1 - first


def plane_block():
    _, plane = tables()
    perk = plane.reshape(2, GRID // 4, 4, 2, KEPT).transpose(3, 4, 1, 0, 2).reshape(2, KEPT, 2 * GRID)
    out = np.zeros((YL, KWIN, 2 * GRID), np.float64)
    for d in range(2):
        for b in range(KEPT * HALF):
            k, j = divmod(b, KEPT)
            n, r = divmod(b, BTILE)
            row = n * 2 * BTILE + d * (BTILE if n < NBT else 64) + r
            out[row, k - window(n)[0]] = perk[d, j]
    return out.reshape(YL, KWIN * 2 * GRID).astype(ml_dtypes.bfloat16)


def kron_block():
    _, plane = tables()
    out = np.zeros((2, AEI, QC, NT, QC * SLAB), np.float64)
    slabs = plane.reshape(2, NT, SLAB, AEI).transpose(0, 3, 1, 2)
    for q in range(QC):
        out[:, :, q, :, 8 * q : 8 * q + 8] = slabs[..., :8]
        out[:, :, q, :, 8 * QC + 4 * q : 8 * QC + 4 * q + 4] = slabs[..., 8:]
    return out.reshape(2, AEI * QC, GRID * QC).astype(ml_dtypes.bfloat16)


def copy_in(refs, spaces, sems):
    copies = [pltpu.make_async_copy(ref, space, sems.at[i]) for i, (ref, space) in enumerate(zip(refs, spaces))]
    for copy in copies:
        copy.start()
    return copies


def spectra_kernel(*refs):
    n = VC + NX + 3
    o_ref, dens, zs, sems = refs[n], *refs[2 * n + 1 :]
    spaces = refs[n + 1 : 2 * n + 1]
    v_refs, c_refs, (t_ref, w_ref) = spaces[:VC], spaces[VC : n - 2], spaces[n - 2 :]
    tables = copy_in([refs[n - 2]], [t_ref], sems.at[NCUT])
    cuts = []
    for cut in range(NCUT):
        lanes = pl.ds(cut * (GRID * GRID // NCUT), GRID * GRID // NCUT)
        cuts.append(copy_in([r.at[:, :, lanes] for r in refs[: n - 2]], [r.at[:, :, lanes] for r in spaces[: n - 2]], sems.at[cut]))
    tables.append(pltpu.make_async_copy(refs[n - 1], w_ref, sems.at[NCUT, 1]))
    tables[1].start()
    tables[0].wait()

    def body(step, _):
        lanes = pl.ds(pl.multiple_of(step * YSTEP, YSTEP), YSTEP)

        def parts(ref, b):
            wave = ref[b, :, lanes].astype(F32)
            return wave[:8], wave[8:]

        def tile(pieces):
            heads = [head for head, _ in pieces]
            tails = [jnp.concatenate([pieces[i][1], pieces[i + 1][1]], axis=0) for i in range(0, QC, 2)]
            return jnp.concatenate(heads + tails, axis=0).astype(BF)

        bands = [(c_refs[m], b) for m in range(3) for b in range(2)] + [(c_refs[3], 0), (c_refs[4], 0)]
        cond = [tile([parts(ref, b) for ref, b in bands[QC * h : QC * (h + 1)]]) for h in range(2)]
        for v in range(VC):
            val = tile([parts(v_refs[v], 0)] * QC)
            for h in range(2):
                r0 = (v * 2 + h) * SLAB * QC
                dens[r0 : r0 + SLAB * QC, :] = val * cond[h]
        groups = []
        for sub in range(YSTEP // ZGRP):
            z = jnp.dot(dens[:, sub * ZGRP : (sub + 1) * ZGRP], t_ref[...], preferred_element_type=F32)
            groups.append(z.T.reshape(HALF, 8, ROWS))
        zs[:, pl.ds(pl.multiple_of(step * 16, 16), 16), :] = jnp.concatenate(groups, axis=1).astype(BF)
        return 0

    for cut in range(NCUT):
        for copy in cuts[cut]:
            copy.wait()
        lax.fori_loop(cut * (NSTEP // NCUT), (cut + 1) * (NSTEP // NCUT), body, 0)
    tables[1].wait()
    for n in range(NBT + 1):
        r0 = n * 2 * BTILE
        rows = 2 * BTILE if n < NBT else BTILE
        k0, width = window(n)
        zk = zs[k0 : k0 + width].reshape(width * 2 * GRID, ROWS)
        y = jnp.dot(w_ref[r0 : r0 + rows, : width * 2 * GRID], zk, preferred_element_type=F32)
        yt = y.T.astype(BF).reshape(NT, SLAB * QC, rows)
        if n < NBT - 1:
            l0 = n // 2 * 512 + n % 2 * BTILE
            o_ref[:, :, l0 : l0 + BTILE] = yt[:, :, :BTILE]
            o_ref[:, :, l0 + 256 : l0 + 256 + BTILE] = yt[:, :, BTILE:]
        else:
            o_ref[:, :, r0 : r0 + rows] = yt


def spectra(vs, cs, t, w):
    operands = [*vs, *cs, t, w]
    return pl.pallas_call(
        spectra_kernel,
        in_specs=[pl.BlockSpec(memory_space=pl.ANY)] * len(operands),
        out_specs=pl.BlockSpec(memory_space=pltpu.VMEM),
        out_shape=jax.ShapeDtypeStruct((NT, SLAB * QC, YL), BF),
        scratch_shapes=[pltpu.VMEM(x.shape, BF) for x in operands]
        + [
            pltpu.VMEM((ROWS, YSTEP), BF),
            pltpu.VMEM((HALF, 2 * GRID, ROWS), BF),
            pltpu.SemaphoreType.DMA((NCUT + 1, len(operands) - 2)),
        ],
        compiler_params=pltpu.CompilerParams(vmem_limit_bytes=58 * 2**20),
        name="spectra",
    )(*operands)


def lines_kernel(y_ref, m_ref, s_ref):
    rows = AEI * QC

    def line(d, lanes):
        return jnp.dot(m_ref[d], y_ref[:, lanes], preferred_element_type=F32)

    for g in range(2):
        s = line(0, pl.ds(512 * g, 256)) + line(1, pl.ds(512 * g + 256, 256))
        s_ref[g * rows : (g + 1) * rows, :] = s.astype(BF)
    s = line(0, pl.ds(1024, BTILE)) + line(1, pl.ds(1024 + BTILE, BTILE))
    s_ref[2 * rows :, :BTILE] = s.astype(BF)
    last = pl.ds(1024 + 2 * BTILE, BTILE)
    s = line(0, last) + pltpu.roll(line(1, last), 64, 1)
    s_ref[2 * rows :, BTILE:] = s.astype(BF)


def lines(y, m):
    return pl.pallas_call(
        lines_kernel,
        out_shape=jax.ShapeDtypeStruct((NGRP * AEI * QC, CODES), BF),
        compiler_params=pltpu.CompilerParams(vmem_limit_bytes=40 * 2**20),
        name="lines",
    )(y, m)


def picked(s_ref, a_ref, b_ref, chunk):
    codes = lax.broadcasted_iota(jnp.int32, (CODES, CODES), 0)
    row = lax.broadcasted_iota(jnp.int32, (SB, CODES), 0)
    outs = []
    for g in range(GCH // CODES):
        lanes = pl.ds(g * CODES, CODES)
        chosen = (codes == b_ref[:, lanes]).astype(F32).astype(BF)
        r = jnp.dot(s_ref[...], chosen, preferred_element_type=F32)
        code = a_ref[:, lanes] - row // QC
        acc = jnp.zeros((SB, CODES), F32)
        for a in range(0, NGRP * AEI, 2):
            acc = jnp.where(code == a, r[a * QC : (a + 2) * QC], acc)
        both = acc + pltpu.roll(acc, QC, 0)
        outs.append(jnp.where(row // QC == chunk, both, 0.0))
    return jnp.concatenate(outs, axis=1)


def first_kernel(s_ref, a_ref, b_ref, o_ref):
    o_ref[...] = picked(s_ref, a_ref, b_ref, 0)


def second_kernel(s_ref, a_ref, b_ref, first_ref, oc_ref, or_ref):
    out = (first_ref[...] + picked(s_ref, a_ref, b_ref, 1)).astype(BF)
    oc_ref[0] = out
    for h in range(GCH // RB):
        or_ref[h] = out[:, h * RB : (h + 1) * RB]


def pick_specs():
    return [
        pl.BlockSpec((NGRP * AEI * QC, CODES), lambda i: (0, 0)),
        pl.BlockSpec((1, GCH), lambda i: (0, i)),
        pl.BlockSpec((1, GCH), lambda i: (0, i)),
    ]


def pick_first(s, a, b):
    return pl.pallas_call(
        first_kernel,
        grid=(GP // GCH,),
        in_specs=pick_specs(),
        out_specs=pl.BlockSpec((SB, GCH), lambda i: (0, i)),
        out_shape=jax.ShapeDtypeStruct((SB, GP), F32),
        compiler_params=pltpu.CompilerParams(vmem_limit_bytes=40 * 2**20),
        name="pick_first",
    )(s, a, b)


def pick_second(s, a, b, first):
    per = 4 * RB // GCH
    return pl.pallas_call(
        second_kernel,
        grid=(GP // GCH,),
        in_specs=pick_specs() + [pl.BlockSpec((SB, GCH), lambda i: (0, i))],
        out_specs=[
            pl.BlockSpec((1, SB, GCH), lambda i: (i // per, 0, i % per)),
            pl.BlockSpec((GCH // RB, SB, RB), lambda i: (i, 0, 0)),
        ],
        out_shape=[
            jax.ShapeDtypeStruct((NT, SB, 4 * RB), BF),
            jax.ShapeDtypeStruct((32, SB, RB), BF),
        ],
        compiler_params=pltpu.CompilerParams(vmem_limit_bytes=40 * 2**20),
        name="pick_second",
    )(s, a, b, first)


KP = NT * SB
LA = 512
XORDER = (0, 1, 3, 2)
ZORDER = (0, 1, 2, 3, 7, 6, 5, 4)


def a_pieces():
    whole = [[(x, z) for x in XORDER] for z in ZORDER[:-1]]
    return whole + [[(x, 4) for x in XORDER[:2]], [(x, 4) for x in XORDER[2:]]]


def b_pieces():
    whole = [[(x, z) for z in range(NZ)] for x in XORDER[:-1]]
    return whole + [[(2, z) for z in range(NZ // 2)], [(2, z) for z in range(NZ // 2, NZ)]]


A_NEAR = 7
B_NEAR = 3


def owner_of(xz_ref, dx, z):
    return lax.rem(xz_ref[0] + (NX - dx), NX) * NZ + z


def z_back(xz_ref, dz):
    return lax.rem(xz_ref[1] + (NZ - dz), NZ)


def matched(lhs, ref):
    return lax.dot_general(jnp.concatenate(lhs, axis=0), ref[...], (((0,), (0,)), ((), ())), preferred_element_type=F32)


def near_kernel(xz_ref, w_ref, *refs):
    n = 1 + A_NEAR + B_NEAR
    acc_ref, wr, spaces, sems = refs[n], refs[n + 1], refs[n + 2 : 2 * n + 2], refs[2 * n + 2]
    copies = copy_in(refs[:n], spaces, sems)
    r_ref = spaces[0]
    copies[0].wait()
    for p in range(32):
        rows = jnp.concatenate([r_ref[t, p].astype(F32) for t in range(NT)], axis=0)
        wr[p] = (rows * w_ref[KP * p : KP * (p + 1), :]).astype(BF)

    def total(pieces, operands, waits, z_of):
        acc = None
        for piece, ref, copy in zip(pieces, operands, waits):
            copy.wait()
            more = matched([wr[owner_of(xz_ref, dx, z_of(z))] for dx, z in piece], ref)
            acc = more if acc is None else acc + more
        return acc

    a_end = 1 + A_NEAR
    acc_ref[:, :LA] = total(a_pieces()[:A_NEAR], spaces[1:a_end], copies[1:a_end], lambda dz: z_back(xz_ref, dz))
    acc_ref[:, LA:] = total(b_pieces()[:B_NEAR], spaces[a_end:], copies[a_end:], lambda z: z)


def product_near(place, rows, weight, a_cols, b_cols):
    operands = [rows, *a_cols, *b_cols]
    vmem = pl.BlockSpec(memory_space=pltpu.VMEM)
    return pl.pallas_call(
        near_kernel,
        in_specs=[pl.BlockSpec(memory_space=pltpu.SMEM), vmem] + [pl.BlockSpec(memory_space=pl.ANY)] * len(operands),
        out_specs=[vmem, vmem],
        out_shape=[jax.ShapeDtypeStruct((RB, 4 * RB), F32), jax.ShapeDtypeStruct((32, KP, RB), BF)],
        scratch_shapes=[pltpu.VMEM(x.shape, BF) for x in operands] + [pltpu.SemaphoreType.DMA((len(operands),))],
        compiler_params=pltpu.CompilerParams(vmem_limit_bytes=58 * 2**20),
        name="product_near",
    )(place, weight, *operands)


def far_blocks():
    return a_pieces()[A_NEAR:], b_pieces()[B_NEAR:]


def far_kernel(xz_ref, acc_any, wr_any, *refs):
    a_far, b_far = far_blocks()
    n = len(a_far) + len(b_far)
    o_ref, acc, lhs, spaces, sems, row_sems = refs[n], refs[n + 1], refs[n + 2], refs[n + 3 : 2 * n + 3], *refs[2 * n + 3 :]
    owners = [owner_of(xz_ref, dx, z_back(xz_ref, dz)) for piece in a_far for dx, dz in piece]
    owners += [owner_of(xz_ref, dx, z) for piece in b_far for dx, z in piece]
    row_copies = [pltpu.make_async_copy(wr_any.at[p], lhs.at[i], row_sems.at[i]) for i, p in enumerate(owners)]
    for copy in row_copies:
        copy.start()
    copies = copy_in([*refs[:n], acc_any], [*spaces, acc], sems)
    for copy in row_copies + copies:
        copy.wait()

    first = 0
    for half, pieces, operands in ((slice(0, LA), a_far, spaces[: len(a_far)]), (slice(LA, None), b_far, spaces[len(a_far) :])):
        for piece, ref in zip(pieces, operands):
            acc[:, half] += matched([lhs[first + i] for i in range(len(piece))], ref)
            first += len(piece)
    for q in range(4):
        o_ref[:, 375 * q : 375 * (q + 1)] = acc[:375, RB * q : RB * q + 375]


def product_far(place, acc, wr, a_cols, b_cols):
    operands = [*a_cols, *b_cols]
    count = sum(len(piece) for pieces in far_blocks() for piece in pieces)
    return pl.pallas_call(
        far_kernel,
        in_specs=[pl.BlockSpec(memory_space=pltpu.SMEM)] + [pl.BlockSpec(memory_space=pl.ANY)] * (2 + len(operands)),
        out_specs=pl.BlockSpec(memory_space=pltpu.VMEM),
        out_shape=jax.ShapeDtypeStruct((375, 1500), F32),
        scratch_shapes=[pltpu.VMEM((RB, 4 * RB), F32), pltpu.VMEM((count, KP, RB), BF)]
        + [pltpu.VMEM(x.shape, BF) for x in operands]
        + [pltpu.SemaphoreType.DMA((len(operands) + 1,)), pltpu.SemaphoreType.DMA((count,))],
        compiler_params=pltpu.CompilerParams(vmem_limit_bytes=58 * 2**20),
        name="product_far",
    )(place, acc, wr, *operands)


def ring(value, axis, size):
    return ring_on(value, shift(value, axis, size, 1), shift(value, axis, size, -1), axis, size)


def ring_on(value, up, down, axis, size):
    ups, downs = [up], [down]
    for _ in range(size // 2 - 2):
        ups.append(shift(ups[-1], axis, size, 1))
        downs.append(shift(downs[-1], axis, size, -1))
    half = value.shape[0] // 2
    far = [shift(ups[-1][:half], axis, size, 1), shift(downs[-1][half:], axis, size, -1)]
    return [value] + ups + downs, far


def pick_levels(picks, table):
    codes = jnp.arange(table.shape[0], dtype=jnp.int32)
    return jnp.sum(jnp.where(picks[:, None] == codes[None, :], table[None, :], 0.0), axis=1)


def spread(levels, places):
    codes = jnp.arange(levels.shape[0], dtype=jnp.int32)[None, :]
    return jnp.sum(jnp.where(codes == places.astype(np.int32), levels[None, :], 0.0), axis=1, keepdims=True)


def shift(value, axis, size, step):
    return lax.ppermute(value, axis, [(i, (i + step) % size) for i in range(size)])


def per_device(
    valence_waves,
    cond_waves,
    valence_energy,
    conduction_energy,
    valence_pick,
    cond_pick,
    cond_slot,
    g_index,
):
    cs, far = ring(cond_waves, "x", NX)
    cs += far
    depth, plane, kron = jnp.asarray(depth_block()), jnp.asarray(plane_block()), jnp.asarray(kron_block())
    tile = ("y", "core")
    vs = [valence_waves] + [None] * (VB - 1)
    for m in range(1, VB // 2):
        vs[m] = shift(vs[m - 1], "z", NZ, 1)
        vs[VB - m] = shift(vs[(VB - m + 1) % VB], "z", NZ, -1)
    vs[VB // 2] = shift(vs[2], "z", NZ, 2)
    specs = [spectra([vs[k] for k in slots], cs, depth, plane) for slots in SLOTS]
    slabs = [lax.all_to_all(specs[0], tile, split_axis=0, concat_axis=0, tiled=True)]
    slabs[0], specs[1] = lax.optimization_barrier((slabs[0], specs[1]))
    slabs.append(lax.all_to_all(specs[1], tile, split_axis=0, concat_axis=0, tiled=True))

    valence_level = pick_levels(valence_pick, valence_energy)
    band_level = pick_levels(cond_pick, conduction_energy)
    slot_codes = jnp.arange(NC, dtype=jnp.int32)
    slot_level = jnp.sum(
        jnp.where(cond_slot[:, None] == slot_codes[None, :], band_level[:, None], 0.0), axis=0
    )
    factor = 4.0 / math.sqrt(NV * NC)
    xs, zs, ts, c, ms, bs = np.ix_(*(np.arange(n) for n in (NX, NZ, NT, 2, 2, 2)))
    v_of = VB * xs + (zs - np.array(SLOTS)[c, ts // 2]) % NZ
    s_of = 2 * NZ * ((xs - np.array(XORDER)[2 * (ts % 2) + ms]) % NX) + 2 * zs + bs
    v_of, s_of = (np.broadcast_to(m, (NX, NZ, NT, 2, 2, 2)).reshape(NV * NC, 1) for m in (v_of, s_of))
    weight = factor / (spread(valence_level, v_of) - spread(slot_level, s_of))

    index = jnp.pad(g_index.reshape(32, 375), ((0, 0), (0, RB - 375))).reshape(1, GP)
    a_code = index // (KEPT * HALF)
    rest = index % (KEPT * HALF)
    b_code = (rest % HALF) * KEPT + rest // HALF
    a_code = a_code + AEI * (b_code // CODES)
    b_code = b_code % CODES

    first = pick_first(lines(slabs[0].reshape(GRID * QC, YL), kron), a_code, b_code)
    cols, for_rows = pick_second(lines(slabs[1].reshape(GRID * QC, YL), kron), a_code, b_code, first)
    cols = lax.all_to_all(cols, tile, split_axis=0, concat_axis=0, tiled=True).reshape(KP, 4 * RB)
    b_bundle = lax.all_gather(cols[:, LA:], "z", axis=0, tiled=True)
    a_part = cols[:, :LA]
    a_bundle = jnp.concatenate([a_part] + [shift(a_part, "x", NX, step) for step in (1, -1, 2)], axis=0)
    for_rows, a_bundle = lax.optimization_barrier((for_rows, a_bundle))
    a_up, a_down = shift(a_bundle, "z", NZ, 1), shift(a_bundle, "z", NZ, -1)
    b_bundle, a_up, a_down = lax.optimization_barrier((b_bundle, a_up, a_down))
    a_cols, a_far = ring_on(a_bundle, a_up, a_down, "z", NZ)
    b_cols, b_far = ring(b_bundle, "x", NX)
    rows = lax.all_to_all(for_rows, ("x", "z"), split_axis=0, concat_axis=0, tiled=True)
    rows = lax.all_gather(rows, ("y", "core"), axis=0, tiled=False)
    place = jnp.stack([lax.axis_index("x"), lax.axis_index("z")]).astype(jnp.int32)
    acc, wr = product_near(place, rows, weight, a_cols, b_cols)
    return product_far(place, acc, wr, a_far, b_far)


def solution(mesh):
    fine = Mesh(mesh.devices.reshape(NX, NZ, NY, NCORE), ("x", "z", "y", "core"))
    waves = P(("x", "z"), ("y", "core"), None)
    return jax.shard_map(
        per_device,
        mesh=fine,
        in_specs=(waves, waves, P(), P(), P(), P(), P(), P()),
        out_specs=P(("x", "z"), ("y", "core")),
        check_vma=False,
    )
```

```python
import functools
import math

import jax
import jax.numpy as jnp
import ml_dtypes
import numpy as np
from jax import lax
from jax.experimental import pallas as pl
from jax.experimental.pallas import tpu as pltpu
from jax.sharding import Mesh, PartitionSpec as P

NV = 32
NC = 64
GRID = 96
KM = 18
NG = 12000
KEPT = 2 * KM + 1
HALF = KM + 1
NX, NZ, NY, NCORE = 4, 8, 4, 2
NT = NY * NCORE
SLAB = GRID // NT
VB = 8
SB = 8
VC = 4
QC = 4
SLOTS = ((0, 1, 7, 2), (6, 3, 5, 4))
ROWS = SLAB * VC * SB
ZGRP = 384
ZOUT = HALF * 8
YSTEP = 768
NSTEP = GRID * GRID // YSTEP
NCUT = 4
BTILE = 128
NBT = 5
KWIN = 5
YL = 1408
AEI = 2 * KEPT
RB = 384
GP = 32 * RB
GCH = 768
CODES = 256
NGRP = 3
BF = jnp.bfloat16
F32 = jnp.float32


def tables():
    pos = np.arange(GRID)
    scale = 1.0 / math.sqrt(GRID)

    def angles(freqs):
        turns = (np.mod(freqs, GRID)[None, :] * pos[:, None]) % GRID
        return turns.astype(np.float64) * (2.0 * math.pi / GRID)

    ad = angles(np.arange(HALF))
    depth = np.stack([np.cos(ad), -np.sin(ad)], axis=1) * scale
    ap = angles(np.arange(KEPT) - KM)
    c, s = np.cos(ap), np.sin(ap)
    plane = np.stack([np.stack([c, s]), np.stack([-s, c])], axis=2) * scale
    return depth, plane


def depth_block():
    depth, _ = tables()
    out = np.zeros((4, GRID, HALF, 2, 4), np.float64)
    for y in range(4):
        out[y, :, :, :, y] = depth.transpose(0, 2, 1)
    return out.reshape(ZGRP, ZOUT).astype(ml_dtypes.bfloat16)


def window(n):
    first = BTILE * n // KEPT
    return first, min((BTILE * n + BTILE - 1) // KEPT, HALF - 1) + 1 - first


def plane_block():
    _, plane = tables()
    perk = plane.reshape(2, GRID // 4, 4, 2, KEPT).transpose(3, 4, 1, 0, 2).reshape(2, KEPT, 2 * GRID)
    out = np.zeros((YL, KWIN, 2 * GRID), np.float64)
    for d in range(2):
        for b in range(KEPT * HALF):
            k, j = divmod(b, KEPT)
            n, r = divmod(b, BTILE)
            row = n * 2 * BTILE + d * (BTILE if n < NBT else 64) + r
            out[row, k - window(n)[0]] = perk[d, j]
    return out.reshape(YL, KWIN * 2 * GRID).astype(ml_dtypes.bfloat16)


def kron_block():
    _, plane = tables()
    out = np.zeros((2, AEI, QC, NT, QC * SLAB), np.float64)
    slabs = plane.reshape(2, NT, SLAB, AEI).transpose(0, 3, 1, 2)
    for q in range(QC):
        out[:, :, q, :, 8 * q : 8 * q + 8] = slabs[..., :8]
        out[:, :, q, :, 8 * QC + 4 * q : 8 * QC + 4 * q + 4] = slabs[..., 8:]
    return out.reshape(2, AEI * QC, GRID * QC).astype(ml_dtypes.bfloat16)


def copy_in(refs, spaces, sems):
    copies = [pltpu.make_async_copy(ref, space, sems.at[i]) for i, (ref, space) in enumerate(zip(refs, spaces))]
    for copy in copies:
        copy.start()
    return copies


def spectra_kernel(*refs):
    n = VC + NX + 3
    o_ref, dens, zs, sems = refs[n], *refs[2 * n + 1 :]
    spaces = refs[n + 1 : 2 * n + 1]
    v_refs, c_refs, (t_ref, w_ref) = spaces[:VC], spaces[VC : n - 2], spaces[n - 2 :]
    tables = copy_in([refs[n - 2]], [t_ref], sems.at[NCUT])
    cuts = []
    for cut in range(NCUT):
        lanes = pl.ds(cut * (GRID * GRID // NCUT), GRID * GRID // NCUT)
        cuts.append(copy_in([r.at[:, :, lanes] for r in refs[: n - 2]], [r.at[:, :, lanes] for r in spaces[: n - 2]], sems.at[cut]))
    tables.append(pltpu.make_async_copy(refs[n - 1], w_ref, sems.at[NCUT, 1]))
    tables[1].start()
    tables[0].wait()

    def body(step, _):
        lanes = pl.ds(pl.multiple_of(step * YSTEP, YSTEP), YSTEP)

        def parts(ref, b):
            wave = ref[b, :, lanes].astype(F32)
            return wave[:8], wave[8:]

        def tile(pieces):
            heads = [head for head, _ in pieces]
            tails = [jnp.concatenate([pieces[i][1], pieces[i + 1][1]], axis=0) for i in range(0, QC, 2)]
            return jnp.concatenate(heads + tails, axis=0).astype(BF)

        bands = [(c_refs[m], b) for m in range(3) for b in range(2)] + [(c_refs[3], 0), (c_refs[4], 0)]
        cond = [tile([parts(ref, b) for ref, b in bands[QC * h : QC * (h + 1)]]) for h in range(2)]
        for v in range(VC):
            val = tile([parts(v_refs[v], 0)] * QC)
            for h in range(2):
                r0 = (v * 2 + h) * SLAB * QC
                dens[r0 : r0 + SLAB * QC, :] = val * cond[h]
        groups = []
        for sub in range(YSTEP // ZGRP):
            z = jnp.dot(dens[:, sub * ZGRP : (sub + 1) * ZGRP], t_ref[...], preferred_element_type=F32)
            groups.append(z.T.reshape(HALF, 8, ROWS))
        zs[:, pl.ds(pl.multiple_of(step * 16, 16), 16), :] = jnp.concatenate(groups, axis=1).astype(BF)
        return 0

    for cut in range(NCUT):
        for copy in cuts[cut]:
            copy.wait()
        lax.fori_loop(cut * (NSTEP // NCUT), (cut + 1) * (NSTEP // NCUT), body, 0)
    tables[1].wait()
    for n in range(NBT + 1):
        r0 = n * 2 * BTILE
        rows = 2 * BTILE if n < NBT else BTILE
        k0, width = window(n)
        zk = zs[k0 : k0 + width].reshape(width * 2 * GRID, ROWS)
        y = jnp.dot(w_ref[r0 : r0 + rows, : width * 2 * GRID], zk, preferred_element_type=F32)
        yt = y.T.astype(BF).reshape(NT, SLAB * QC, rows)
        if n < NBT - 1:
            l0 = n // 2 * 512 + n % 2 * BTILE
            o_ref[:, :, l0 : l0 + BTILE] = yt[:, :, :BTILE]
            o_ref[:, :, l0 + 256 : l0 + 256 + BTILE] = yt[:, :, BTILE:]
        else:
            o_ref[:, :, r0 : r0 + rows] = yt


def spectra(vs, cs, t, w):
    operands = [*vs, *cs, t, w]
    return pl.pallas_call(
        spectra_kernel,
        in_specs=[pl.BlockSpec(memory_space=pl.ANY)] * len(operands),
        out_specs=pl.BlockSpec(memory_space=pltpu.VMEM),
        out_shape=jax.ShapeDtypeStruct((NT, SLAB * QC, YL), BF),
        scratch_shapes=[pltpu.VMEM(x.shape, BF) for x in operands]
        + [
            pltpu.VMEM((ROWS, YSTEP), BF),
            pltpu.VMEM((HALF, 2 * GRID, ROWS), BF),
            pltpu.SemaphoreType.DMA((NCUT + 1, len(operands) - 2)),
        ],
        compiler_params=pltpu.CompilerParams(vmem_limit_bytes=58 * 2**20),
        name="spectra",
    )(*operands)


def lines_kernel(y_ref, m_ref, s_ref):
    rows = AEI * QC

    def line(d, lanes):
        return jnp.dot(m_ref[d], y_ref[:, lanes], preferred_element_type=F32)

    for g in range(2):
        s = line(0, pl.ds(512 * g, 256)) + line(1, pl.ds(512 * g + 256, 256))
        s_ref[g * rows : (g + 1) * rows, :] = s.astype(BF)
    s = line(0, pl.ds(1024, BTILE)) + line(1, pl.ds(1024 + BTILE, BTILE))
    s_ref[2 * rows :, :BTILE] = s.astype(BF)
    last = pl.ds(1024 + 2 * BTILE, BTILE)
    s = line(0, last) + pltpu.roll(line(1, last), 64, 1)
    s_ref[2 * rows :, BTILE:] = s.astype(BF)


def lines(y, m):
    return pl.pallas_call(
        lines_kernel,
        out_shape=jax.ShapeDtypeStruct((NGRP * AEI * QC, CODES), BF),
        compiler_params=pltpu.CompilerParams(vmem_limit_bytes=40 * 2**20),
        name="lines",
    )(y, m)


def picked(s_ref, a_ref, b_ref, chunk):
    codes = lax.broadcasted_iota(jnp.int32, (CODES, CODES), 0)
    row = lax.broadcasted_iota(jnp.int32, (SB, CODES), 0)
    outs = []
    for g in range(GCH // CODES):
        lanes = pl.ds(g * CODES, CODES)
        chosen = (codes == b_ref[:, lanes]).astype(F32).astype(BF)
        r = jnp.dot(s_ref[...], chosen, preferred_element_type=F32)
        code = a_ref[:, lanes] - row // QC
        acc = jnp.zeros((SB, CODES), F32)
        for a in range(0, NGRP * AEI, 2):
            acc = jnp.where(code == a, r[a * QC : (a + 2) * QC], acc)
        both = acc + pltpu.roll(acc, QC, 0)
        outs.append(jnp.where(row // QC == chunk, both, 0.0))
    return jnp.concatenate(outs, axis=1)


def first_kernel(s_ref, a_ref, b_ref, o_ref):
    o_ref[...] = picked(s_ref, a_ref, b_ref, 0)


def second_kernel(s_ref, a_ref, b_ref, first_ref, oc_ref, or_ref):
    out = (first_ref[...] + picked(s_ref, a_ref, b_ref, 1)).astype(BF)
    oc_ref[0] = out
    for h in range(GCH // RB):
        or_ref[h] = out[:, h * RB : (h + 1) * RB]


def pick_specs():
    return [
        pl.BlockSpec((NGRP * AEI * QC, CODES), lambda i: (0, 0)),
        pl.BlockSpec((1, GCH), lambda i: (0, i)),
        pl.BlockSpec((1, GCH), lambda i: (0, i)),
    ]


def pick_first(s, a, b):
    return pl.pallas_call(
        first_kernel,
        grid=(GP // GCH,),
        in_specs=pick_specs(),
        out_specs=pl.BlockSpec((SB, GCH), lambda i: (0, i)),
        out_shape=jax.ShapeDtypeStruct((SB, GP), F32),
        compiler_params=pltpu.CompilerParams(vmem_limit_bytes=40 * 2**20),
        name="pick_first",
    )(s, a, b)


def pick_second(s, a, b, first):
    per = 4 * RB // GCH
    return pl.pallas_call(
        second_kernel,
        grid=(GP // GCH,),
        in_specs=pick_specs() + [pl.BlockSpec((SB, GCH), lambda i: (0, i))],
        out_specs=[
            pl.BlockSpec((1, SB, GCH), lambda i: (i // per, 0, i % per)),
            pl.BlockSpec((GCH // RB, SB, RB), lambda i: (i, 0, 0)),
        ],
        out_shape=[
            jax.ShapeDtypeStruct((NT, SB, 4 * RB), BF),
            jax.ShapeDtypeStruct((32, SB, RB), BF),
        ],
        compiler_params=pltpu.CompilerParams(vmem_limit_bytes=40 * 2**20),
        name="pick_second",
    )(s, a, b, first)


KP = NT * SB
LA = 512
XORDER = (0, 1, 3, 2)
ZORDER = (0, 1, 2, 3, 7, 6, 5, 4)


def a_pieces():
    whole = [[(x, z) for x in XORDER] for z in ZORDER[:-1]]
    return whole + [[(x, 4) for x in XORDER[:2]], [(x, 4) for x in XORDER[2:]]]


def b_pieces():
    whole = [[(x, z) for z in range(NZ)] for x in XORDER[:-1]]
    return whole + [[(2, z) for z in range(NZ // 2)], [(2, z) for z in range(NZ // 2, NZ)]]


A_NEAR = 7
B_NEAR = 3


def owner_of(xz_ref, dx, z):
    return lax.rem(xz_ref[0] + (NX - dx), NX) * NZ + z


def z_back(xz_ref, dz):
    return lax.rem(xz_ref[1] + (NZ - dz), NZ)


def matched(lhs, ref):
    return lax.dot_general(jnp.concatenate(lhs, axis=0), ref[...], (((0,), (0,)), ((), ())), preferred_element_type=F32)


def near_kernel(xz_ref, w_ref, *refs):
    n = 1 + A_NEAR + B_NEAR
    acc_ref, wr, spaces, sems = refs[n], refs[n + 1], refs[n + 2 : 2 * n + 2], refs[2 * n + 2]
    copies = copy_in(refs[:n], spaces, sems)
    r_ref = spaces[0]
    copies[0].wait()
    for p in range(32):
        rows = jnp.concatenate([r_ref[t, p].astype(F32) for t in range(NT)], axis=0)
        wr[p] = (rows * w_ref[KP * p : KP * (p + 1), :]).astype(BF)

    def total(pieces, operands, waits, z_of):
        acc = None
        for piece, ref, copy in zip(pieces, operands, waits):
            copy.wait()
            more = matched([wr[owner_of(xz_ref, dx, z_of(z))] for dx, z in piece], ref)
            acc = more if acc is None else acc + more
        return acc

    a_end = 1 + A_NEAR
    acc_ref[:, :LA] = total(a_pieces()[:A_NEAR], spaces[1:a_end], copies[1:a_end], lambda dz: z_back(xz_ref, dz))
    acc_ref[:, LA:] = total(b_pieces()[:B_NEAR], spaces[a_end:], copies[a_end:], lambda z: z)


def product_near(place, rows, weight, a_cols, b_cols):
    operands = [rows, *a_cols, *b_cols]
    vmem = pl.BlockSpec(memory_space=pltpu.VMEM)
    return pl.pallas_call(
        near_kernel,
        in_specs=[pl.BlockSpec(memory_space=pltpu.SMEM), vmem] + [pl.BlockSpec(memory_space=pl.ANY)] * len(operands),
        out_specs=[vmem, vmem],
        out_shape=[jax.ShapeDtypeStruct((RB, 4 * RB), F32), jax.ShapeDtypeStruct((32, KP, RB), BF)],
        scratch_shapes=[pltpu.VMEM(x.shape, BF) for x in operands] + [pltpu.SemaphoreType.DMA((len(operands),))],
        compiler_params=pltpu.CompilerParams(vmem_limit_bytes=58 * 2**20),
        name="product_near",
    )(place, weight, *operands)


def far_blocks():
    return a_pieces()[A_NEAR:], b_pieces()[B_NEAR:]


def far_kernel(xz_ref, acc_any, wr_any, *refs):
    a_far, b_far = far_blocks()
    n = len(a_far) + len(b_far)
    o_ref, acc, lhs, spaces, sems, row_sems = refs[n], refs[n + 1], refs[n + 2], refs[n + 3 : 2 * n + 3], *refs[2 * n + 3 :]
    owners = [owner_of(xz_ref, dx, z_back(xz_ref, dz)) for piece in a_far for dx, dz in piece]
    owners += [owner_of(xz_ref, dx, z) for piece in b_far for dx, z in piece]
    row_copies = [pltpu.make_async_copy(wr_any.at[p], lhs.at[i], row_sems.at[i]) for i, p in enumerate(owners)]
    for copy in row_copies:
        copy.start()
    copies = copy_in([*refs[:n], acc_any], [*spaces, acc], sems)
    for copy in row_copies + copies:
        copy.wait()

    first = 0
    for half, pieces, operands in ((slice(0, LA), a_far, spaces[: len(a_far)]), (slice(LA, None), b_far, spaces[len(a_far) :])):
        for piece, ref in zip(pieces, operands):
            acc[:, half] += matched([lhs[first + i] for i in range(len(piece))], ref)
            first += len(piece)
    for q in range(4):
        o_ref[:, 375 * q : 375 * (q + 1)] = acc[:375, RB * q : RB * q + 375]


def product_far(place, acc, wr, a_cols, b_cols):
    operands = [*a_cols, *b_cols]
    count = sum(len(piece) for pieces in far_blocks() for piece in pieces)
    return pl.pallas_call(
        far_kernel,
        in_specs=[pl.BlockSpec(memory_space=pltpu.SMEM)] + [pl.BlockSpec(memory_space=pl.ANY)] * (2 + len(operands)),
        out_specs=pl.BlockSpec(memory_space=pltpu.VMEM),
        out_shape=jax.ShapeDtypeStruct((375, 1500), F32),
        scratch_shapes=[pltpu.VMEM((RB, 4 * RB), F32), pltpu.VMEM((count, KP, RB), BF)]
        + [pltpu.VMEM(x.shape, BF) for x in operands]
        + [pltpu.SemaphoreType.DMA((len(operands) + 1,)), pltpu.SemaphoreType.DMA((count,))],
        compiler_params=pltpu.CompilerParams(vmem_limit_bytes=58 * 2**20),
        name="product_far",
    )(place, acc, wr, *operands)


def ring(value, axis, size):
    return ring_on(value, shift(value, axis, size, 1), shift(value, axis, size, -1), axis, size)


def ring_on(value, up, down, axis, size):
    ups, downs = [up], [down]
    for _ in range(size // 2 - 2):
        ups.append(shift(ups[-1], axis, size, 1))
        downs.append(shift(downs[-1], axis, size, -1))
    half = value.shape[0] // 2
    far = [shift(ups[-1][:half], axis, size, 1), shift(downs[-1][half:], axis, size, -1)]
    return [value] + ups + downs, far


def pick_levels(picks, table):
    codes = jnp.arange(table.shape[0], dtype=jnp.int32)
    return jnp.sum(jnp.where(picks[:, None] == codes[None, :], table[None, :], 0.0), axis=1)


def spread(levels, places):
    codes = jnp.arange(levels.shape[0], dtype=jnp.int32)[None, :]
    return jnp.sum(jnp.where(codes == places.astype(np.int32), levels[None, :], 0.0), axis=1, keepdims=True)


def shift(value, axis, size, step):
    return lax.ppermute(value, axis, [(i, (i + step) % size) for i in range(size)])


def per_device(
    valence_waves,
    cond_waves,
    valence_energy,
    conduction_energy,
    valence_pick,
    cond_pick,
    cond_slot,
    g_index,
):
    cs, far = ring(cond_waves, "x", NX)
    cs += far
    depth, plane, kron = jnp.asarray(depth_block()), jnp.asarray(plane_block()), jnp.asarray(kron_block())
    tile = ("y", "core")
    vs = [valence_waves] + [None] * (VB - 1)
    for m in range(1, VB // 2):
        vs[m] = shift(vs[m - 1], "z", NZ, 1)
        vs[VB - m] = shift(vs[(VB - m + 1) % VB], "z", NZ, -1)
    vs[VB // 2] = shift(vs[2], "z", NZ, 2)
    specs = [spectra([vs[k] for k in slots], cs, depth, plane) for slots in SLOTS]
    valence_level = pick_levels(valence_pick, valence_energy)
    band_level = pick_levels(cond_pick, conduction_energy)
    slot_codes = jnp.arange(NC, dtype=jnp.int32)
    slot_level = jnp.sum(
        jnp.where(cond_slot[:, None] == slot_codes[None, :], band_level[:, None], 0.0), axis=0
    )
    factor = 4.0 / math.sqrt(NV * NC)
    xs, zs, ts, c, ms, bs = np.ix_(*(np.arange(n) for n in (NX, NZ, NT, 2, 2, 2)))
    v_of = VB * xs + (zs - np.array(SLOTS)[c, ts // 2]) % NZ
    s_of = 2 * NZ * ((xs - np.array(XORDER)[2 * (ts % 2) + ms]) % NX) + 2 * zs + bs
    v_of, s_of = (np.broadcast_to(m, (NX, NZ, NT, 2, 2, 2)).reshape(NV * NC, 1) for m in (v_of, s_of))
    weight = factor / (spread(valence_level, v_of) - spread(slot_level, s_of))

    index = jnp.pad(g_index.reshape(32, 375), ((0, 0), (0, RB - 375))).reshape(1, GP)
    a_code = index // (KEPT * HALF)
    rest = index % (KEPT * HALF)
    b_code = (rest % HALF) * KEPT + rest // HALF
    a_code = a_code + AEI * (b_code // CODES)
    b_code = b_code % CODES

    slabs = [lax.all_to_all(specs[0], tile, split_axis=0, concat_axis=0, tiled=True)]
    slabs[0], specs[1], weight = lax.optimization_barrier((slabs[0], specs[1], weight))
    slabs.append(lax.all_to_all(specs[1], tile, split_axis=0, concat_axis=0, tiled=True))

    first = pick_first(lines(slabs[0].reshape(GRID * QC, YL), kron), a_code, b_code)
    cols, for_rows = pick_second(lines(slabs[1].reshape(GRID * QC, YL), kron), a_code, b_code, first)
    cols = lax.all_to_all(cols, tile, split_axis=0, concat_axis=0, tiled=True).reshape(KP, 4 * RB)
    b_bundle = lax.all_gather(cols[:, LA:], "z", axis=0, tiled=True)
    a_part = cols[:, :LA]
    a_bundle = jnp.concatenate([a_part] + [shift(a_part, "x", NX, step) for step in (1, -1, 2)], axis=0)
    for_rows, a_bundle = lax.optimization_barrier((for_rows, a_bundle))
    a_up, a_down = shift(a_bundle, "z", NZ, 1), shift(a_bundle, "z", NZ, -1)
    b_bundle, a_up, a_down = lax.optimization_barrier((b_bundle, a_up, a_down))
    a_cols, a_far = ring_on(a_bundle, a_up, a_down, "z", NZ)
    b_cols, b_far = ring(b_bundle, "x", NX)
    rows = lax.all_to_all(for_rows, ("x", "z"), split_axis=0, concat_axis=0, tiled=True)
    rows = lax.all_gather(rows, ("y", "core"), axis=0, tiled=False)
    place = jnp.stack([lax.axis_index("x"), lax.axis_index("z")]).astype(jnp.int32)
    acc, wr = product_near(place, rows, weight, a_cols, b_cols)
    return product_far(place, acc, wr, a_far, b_far)


def solution(mesh):
    fine = Mesh(mesh.devices.reshape(NX, NZ, NY, NCORE), ("x", "z", "y", "core"))
    waves = P(("x", "z"), ("y", "core"), None)
    return jax.shard_map(
        per_device,
        mesh=fine,
        in_specs=(waves, waves, P(), P(), P(), P(), P(), P()),
        out_specs=P(("x", "z"), ("y", "core")),
        check_vma=False,
    )
```
